128 devices in a mesh: seq: 32 (over x, z, core), head: 4 (over y).
Axes of the slice: x: 4, y: 4, z: 4, core: 2. Of those that a mesh axis runs over, the one named last changes fastest.
Arguments:
- queries: bfloat16 [24576, 8192], P('seq', 'head'), may hold values from -3 to 3
- keys: bfloat16 [24576, 8192], P('seq', 'head'), may hold values from -3 to 3
- values: bfloat16 [24576, 8192], P('seq', 'head'), may hold values from -13 to 13
- log_decay: float32 [64, 24576], P('head', 'seq'), may hold values from -1 to 0, as said below
- gain: float32 [8192], P('head'), may hold values from 0.25 to 1.75
- grad_out: bfloat16 [24576, 8192], P('seq', 'head'), may hold values from -5 to 5
Outputs:
- output: bfloat16 [24576, 8192], P('seq', 'head')
- grad_queries: bfloat16 [24576, 8192], P('seq', 'head')
- grad_keys: bfloat16 [24576, 8192], P('seq', 'head')
- grad_values: bfloat16 [24576, 8192], P('seq', 'head')
- grad_gain: float32 [8192], P('head')
The draws below stay inside these ranges and needn't reach their ends.
Inputs may be any that keep to these rules, and one draw needn't show every extreme that they name: `log_decay`: every entry is negative.
All inputs are finite; a program needn't handle non-finite values.
Results may differ from the reference program's by a relative error of at most 0.012.
Values sent between devices are 32-bit elements; how exact they have to be, the bound alone decides.
No kernel may reach another device: no remote copies, remote signals or barrier semaphores. Data moves between devices by JAX's collectives and lax.ppermute only.
A program may use at most 192 MiB of HBM per device.

```python
import math
import jax
import jax.numpy as jnp
from jax import lax

HEAD_TOTAL = 64
DH = 128
SPAN = 128
TOK_DEV = 768
TOKEN_TOTAL = 24576


def head_scale():
    head_ids = jnp.arange(HEAD_TOTAL * DH) // DH
    return 0.6 + 1.2 * head_ids.astype(jnp.float32) / max(HEAD_TOTAL - 1, 1)


def key_field(key):
    field_key = jax.random.fold_in(key, 13)
    return jnp.clip(jax.random.normal(field_key, (TOKEN_TOTAL, HEAD_TOTAL * DH), jnp.float32), -6.0, 6.0)


def value_field(key):
    field_key = jax.random.fold_in(key, 17)
    return jnp.clip(jax.random.normal(field_key, (TOKEN_TOTAL, HEAD_TOTAL * DH), jnp.float32), -6.0, 6.0)


def draw_keys(key, part):
    shared = key_field(key)
    return (0.5 * shared).astype(jnp.bfloat16)


def draw_queries(key, part):
    shared = key_field(key)
    key = jax.random.fold_in(key, 2)
    own = jnp.clip(jax.random.normal(key, (TOKEN_TOTAL, HEAD_TOTAL * DH), jnp.float32), -6.0, 6.0)
    return jnp.clip(0.5 * (0.8 * shared + 0.6 * own), -3.0, 3.0).astype(jnp.bfloat16)


def draw_values(key, part):
    shared = value_field(key)
    return (shared * head_scale()[None, :]).astype(jnp.bfloat16)


def draw_grad_out(key, part):
    shared = value_field(key)
    key = jax.random.fold_in(key, 7)
    key_one = jax.random.fold_in(key, 0)
    key_three = jax.random.fold_in(key, 2)
    places = 0.5 + jnp.arange(TOKEN_TOTAL).astype(jnp.float32) / TOKEN_TOTAL
    token_sign = jnp.where(jax.random.uniform(key_three, (TOKEN_TOTAL, 1)) < 0.5, -1.0, 1.0)
    basic = jnp.clip(jax.random.normal(key_one, (TOKEN_TOTAL, HEAD_TOTAL * DH), jnp.float32), -6.0, 6.0)
    basic = basic + 0.8 * token_sign * shared
    scaled = 0.25 * basic * places[:, None] * head_scale()[None, :]
    return jnp.clip(scaled, -5.0, 5.0).astype(jnp.bfloat16)


def draw_log_decay(key, part):
    key = jax.random.fold_in(key, 11)
    every_key_rows = jax.random.split(key, 8)
    fast_share = 0.25
    medium_share = 0.25
    pick = jax.random.uniform(every_key_rows[0], (HEAD_TOTAL, 1))
    fast_heads = pick < fast_share
    medium_heads = jnp.logical_and(pick >= fast_share, pick < fast_share + medium_share)
    fast_rate = jax.random.uniform(every_key_rows[1], (HEAD_TOTAL, 1), jnp.float32, 1.0 / 50.0, 1.0 / 30.0)
    medium_rate = jax.random.uniform(every_key_rows[7], (HEAD_TOTAL, 1), jnp.float32, 1.0 / 220.0, 1.0 / 100.0)
    slow_rate = jnp.exp(jax.random.uniform(every_key_rows[2], (HEAD_TOTAL, 1), jnp.float32, math.log(0.05), math.log(0.4))) / TOKEN_TOTAL
    rate = jnp.where(fast_heads, fast_rate, jnp.where(medium_heads, medium_rate, slow_rate))
    runs = TOKEN_TOTAL // TOK_DEV
    run_factor = jnp.repeat(jax.random.uniform(every_key_rows[3], (HEAD_TOTAL, runs), jnp.float32, 0.7, 1.4), TOK_DEV, axis=1)
    token_factor = jax.random.uniform(every_key_rows[4], (HEAD_TOTAL, TOKEN_TOTAL), jnp.float32, 0.5, 1.5)
    constant_decay = -rate * run_factor * token_factor
    spike_location = jax.random.randint(every_key_rows[5], (HEAD_TOTAL, 2), 0, TOKEN_TOTAL)
    spike_retain = jax.random.uniform(every_key_rows[6], (HEAD_TOTAL, 2), jnp.float32, 0.5, 0.8)
    match_tally = jnp.arange(TOKEN_TOTAL)[None, None, :] == spike_location[:, :, None]
    spike_events = jnp.sum(jnp.where(match_tally, jnp.log(spike_retain)[:, :, None], 0.0), axis=1)
    return constant_decay + spike_events


def setup_inputs(seed: int = 0) -> dict:
    splits = jax.random.split(jax.random.key(seed), 7)
    queries = draw_queries(jax.random.fold_in(splits[6], 71), 0)
    keys = draw_keys(jax.random.fold_in(splits[6], 71), 0)
    values = draw_values(jax.random.fold_in(splits[6], 71), 0)
    log_decay = draw_log_decay(jax.random.fold_in(splits[6], 71), 0)
    gain = jnp.clip(1.0 + 0.15 * jax.random.normal(splits[4], (HEAD_TOTAL * DH,), jnp.float32), 0.25, 1.75)
    grad_out = draw_grad_out(jax.random.fold_in(splits[6], 71), 0)
    return {"queries": queries, "keys": keys, "values": values, "log_decay": log_decay, "gain": gain, "grad_out": grad_out}


def split_heads(array, groups):
    size_group = HEAD_TOTAL // groups
    shaped = array.reshape(TOKEN_TOTAL // SPAN, SPAN, groups, size_group, DH)
    return shaped.transpose(2, 0, 1, 3, 4)

def merge_heads(array):
    return array.transpose(1, 2, 0, 3, 4).reshape(TOKEN_TOTAL, HEAD_TOTAL * DH)

def span_terms(query_blocks, key_blocks, value_blocks, log_blocks):
    cumulative = jnp.cumsum(log_blocks, axis=2)
    block_logs = cumulative[:, :, -1]
    places = jnp.arange(cumulative.shape[2])
    triangle = places[:, None] >= places[None, :]
    diffs = cumulative[:, :, :, None] - cumulative[:, :, None, :]
    decays = jnp.where(triangle, jnp.exp(jnp.minimum(diffs, 0.0)), 0.0)
    query_scale = jnp.exp(cumulative).transpose(1, 2, 0)[..., None]
    key_scale = jnp.exp(block_logs[:, :, None] - cumulative).transpose(1, 2, 0)[..., None]
    query_float = query_blocks.astype(jnp.float32)
    key_float = key_blocks.astype(jnp.float32)
    value_float = value_blocks.astype(jnp.float32)
    scores = jnp.einsum('nihd,njhd->hnij', query_float, key_float)
    weights = (scores * decays).astype(jnp.bfloat16)
    query_decayed = (query_float * query_scale).astype(jnp.bfloat16)
    key_decayed = (key_float * key_scale).astype(jnp.bfloat16)
    updates = jnp.einsum('nihd,nihe->nhde', key_decayed.astype(jnp.float32), value_float)

    def advance(state_now, paired):
        factor, update = paired
        return (factor[:, None, None] * state_now + update, state_now)
    start_state = jnp.zeros((updates.shape[1], updates.shape[2], updates.shape[3]), jnp.float32)
    _, state_in = lax.scan(advance, start_state, (jnp.exp(block_logs).T, updates))
    state_low = state_in.astype(jnp.bfloat16)
    return (decays, query_scale, key_scale, block_logs, weights, query_decayed, key_decayed, state_low)

def forward_group(operands):
    query_blocks, key_blocks, value_blocks, log_blocks = operands
    terms = span_terms(query_blocks, key_blocks, value_blocks, log_blocks)
    weights, query_decayed, state_low = (terms[4], terms[5], terms[7])
    local_part = jnp.einsum('hnij,njhe->nihe', weights.astype(jnp.float32), value_blocks.astype(jnp.float32))
    carried = jnp.einsum('nihd,nhde->nihe', query_decayed.astype(jnp.float32), state_low.astype(jnp.float32))
    return (local_part + carried).astype(jnp.bfloat16)

def backward_group(operands):
    query_blocks, key_blocks, value_blocks, log_blocks, grad_blocks = operands
    decays, query_scale, key_scale, block_logs, weights, query_decayed, key_decayed, state_low = span_terms(query_blocks, key_blocks, value_blocks, log_blocks)
    grad_float = grad_blocks.astype(jnp.float32)
    query_float = query_blocks.astype(jnp.float32)
    key_float = key_blocks.astype(jnp.float32)
    value_float = value_blocks.astype(jnp.float32)
    qgrad_terms = jnp.einsum('nihd,nihe->nhde', query_decayed.astype(jnp.float32), grad_float)

    def retreat(state_back, paired):
        factor, grad_term = paired
        return (factor[:, None, None] * state_back + grad_term, state_back)
    start_state = jnp.zeros((qgrad_terms.shape[1], qgrad_terms.shape[2], qgrad_terms.shape[3]), jnp.float32)
    _, state_grad = lax.scan(retreat, start_state, (jnp.exp(block_logs).T, qgrad_terms), reverse=True)
    state_grad = state_grad.astype(jnp.bfloat16).astype(jnp.float32)
    grad_weights = (jnp.einsum('nihe,njhe->hnij', grad_float, value_float) * decays).astype(jnp.bfloat16)
    grad_weights = grad_weights.astype(jnp.float32)
    low_float = state_low.astype(jnp.float32)
    grad_query = jnp.einsum('hnij,njhd->nihd', grad_weights, key_float)
    grad_query = grad_query + query_scale * jnp.einsum('nihe,nhde->nihd', grad_float, low_float)
    grad_key = jnp.einsum('hnij,nihd->njhd', grad_weights, query_float)
    grad_key = grad_key + key_scale * jnp.einsum('njhe,nhde->njhd', value_float, state_grad)
    grad_value = jnp.einsum('hnij,nihe->njhe', weights.astype(jnp.float32), grad_float)
    grad_value = grad_value + jnp.einsum('njhd,nhde->njhe', key_decayed.astype(jnp.float32), state_grad)
    return (grad_query.astype(jnp.bfloat16), grad_key.astype(jnp.bfloat16), grad_value.astype(jnp.bfloat16))

def reference(queries, keys, values, log_decay, gain, grad_out):
    groups = HEAD_TOTAL // 16 if HEAD_TOTAL % 16 == 0 else 1
    size_group = HEAD_TOTAL // groups
    query_split = split_heads(queries, groups)
    key_split = split_heads(keys, groups)
    value_split = split_heads(values, groups)
    log_split = log_decay.reshape(groups, size_group, TOKEN_TOTAL // SPAN, SPAN)
    attention = merge_heads(lax.map(forward_group, (query_split, key_split, value_split, log_split)))
    attn_float = attention.astype(jnp.float32)
    inverse = lax.rsqrt(lax.optimization_barrier(jnp.mean(attn_float * attn_float, axis=1)) + 1e-06)[:, None]
    normed = attn_float * inverse
    output = (normed * gain).astype(jnp.bfloat16)
    grad_float = grad_out.astype(jnp.float32)
    grad_gain = lax.optimization_barrier(jnp.sum(grad_float * normed, axis=0))
    grad_normed = grad_float * gain
    inner_mean = lax.optimization_barrier(jnp.mean(grad_normed * normed, axis=1))[:, None]
    grad_attn = (inverse * (grad_normed - normed * inner_mean)).astype(jnp.bfloat16)
    grad_split = split_heads(grad_attn, groups)
    grad_query, grad_key, grad_value = lax.map(backward_group, (query_split, key_split, value_split, log_split, grad_split))
    return (output, merge_heads(grad_query), merge_heads(grad_key), merge_heads(grad_value), grad_gain)
```

```python
import functools

import jax
import jax.numpy as jnp
from jax import lax
from jax.experimental import pallas as pl
from jax.experimental.pallas import tpu as pltpu
from jax.sharding import PartitionSpec as P

HEAD_TOTAL = 64
DH = 128
SPAN = 128
HALF = DH // 2
ROWS = 8
PIECE = HALF + ROWS
GROUP = 4
F32 = jnp.float32
BF16 = jnp.bfloat16
EXACT = lax.Precision.HIGHEST
VMEM = pl.BlockSpec(memory_space=pltpu.VMEM)
SMEM = pl.BlockSpec(memory_space=pltpu.SMEM)
HBM = pl.BlockSpec(memory_space=pltpu.HBM)
ANY = pl.BlockSpec(memory_space=pl.ANY)


def dot(a, b, contract, precision=None):
    return lax.dot_general(
        a, b, ((contract[:1], contract[1:]), ((), ())), precision=precision, preferred_element_type=F32
    )


def nn(a, b):
    return dot(a, b, (1, 0))


def nt(a, b):
    return dot(a, b, (1, 1))


def params(mib):
    return pltpu.CompilerParams(vmem_limit_bytes=mib * 1024 * 1024)


def cost(flops, nbytes):
    return pl.CostEstimate(flops=int(flops), bytes_accessed=int(nbytes), transcendentals=0)


def head_rows(ref, head):
    return ref[pl.ds(pl.multiple_of(head * ROWS, ROWS), ROWS), :]


def head_lanes(head, count=1):
    return pl.ds(pl.multiple_of(head * DH, DH), count * DH)


def span(n):
    return slice(n * SPAN, (n + 1) * SPAN)


def last_lane(rows):
    return jnp.broadcast_to(rows[:, SPAN - 1 :], rows.shape)


def middle_lane(rows):
    return jnp.broadcast_to(rows[:, SPAN // 2 - 1 : SPAN // 2], rows.shape)


def masks():
    i = lax.broadcasted_iota(jnp.int32, (SPAN, SPAN), 0)
    j = lax.broadcasted_iota(jnp.int32, (SPAN, SPAN), 1)
    return i >= j, i <= j


def join_rows(rows, blocks):
    return jnp.concatenate([rows[n : n + 1] for n in range(blocks)], axis=1)


def piece_store(ref, at, state, extra):
    ref[2 * at, :HALF, :] = state[:HALF]
    ref[2 * at, HALF:, :] = extra
    ref[2 * at + 1, :HALF, :] = state[HALF:]
    ref[2 * at + 1, HALF:, :] = extra


def piece_state(keep_ref, taken_ref, at, half):
    kept = at < half
    place = 2 * jnp.where(kept, at, at - half)
    low = jnp.where(kept, keep_ref[place, :HALF, :], taken_ref[place, :HALF, :])
    high = jnp.where(kept, keep_ref[place + 1, :HALF, :], taken_ref[place + 1, :HALF, :])
    return jnp.concatenate([low, high], axis=0)


def extra_rows(decay, gain_row=None):
    place = lax.broadcasted_iota(jnp.int32, (ROWS, DH), 0)
    rest = 0.0 if gain_row is None else jnp.where(place == 1, gain_row, 0.0)
    return jnp.where(place == 0, decay, rest)


def state_body(core_ref, log_ref, k_hbm, v_hbm, send_ref, own_ref, cum_ref, before_ref, total_ref, k_ref, v_ref, sems):
    heads, rows = log_ref.shape
    blocks, half = rows // SPAN, heads // 2
    core = core_ref[0]
    copies = []
    for g in range(heads // GROUP):
        first = lax.rem((1 - core) * half + g * GROUP, heads)
        lanes = head_lanes(first, GROUP)
        pair = [
            pltpu.make_async_copy(k_hbm.at[:, lanes], k_ref.at[:, lanes], sems.at[0, g]),
            pltpu.make_async_copy(v_hbm.at[:, lanes], v_ref.at[:, lanes], sems.at[1, g]),
        ]
        for copy in pair:
            copy.start()
        copies.append((first, pair))

    _, triangle = masks()
    triangle = triangle.astype(F32)
    cum_ref[...] = jnp.zeros_like(cum_ref)
    before_ref[...] = jnp.zeros_like(before_ref)
    before = jnp.zeros((heads, SPAN), F32)
    for n in range(blocks):
        cum = dot(log_ref[:, span(n)], triangle, (1, 0), EXACT)
        for h in range(heads):
            cum_ref[h * ROWS + n : h * ROWS + n + 1, :] = cum[h : h + 1]
            before_ref[h * ROWS + n : h * ROWS + n + 1, :] = before[h : h + 1]
        before = before + last_lane(cum)
    for h in range(heads):
        total_ref[h * ROWS : (h + 1) * ROWS, :] = jnp.broadcast_to(before[h : h + 1], (ROWS, SPAN))

    for g, (first, pair) in enumerate(copies):
        for copy in pair:
            copy.wait()
        for at in range(GROUP):
            head = first + at
            lanes = head_lanes(head)
            total = head_rows(total_ref, head)
            scale = jnp.exp(total - head_rows(before_ref, head) - head_rows(cum_ref, head))
            decayed = (k_ref[:, lanes].T.astype(F32) * join_rows(scale, blocks)).astype(BF16)
            state = nn(decayed, v_ref[:, lanes])
            place = (g * GROUP + at) % half
            piece_store(send_ref if g * GROUP < half else own_ref, place, state, extra_rows(jnp.exp(total)))


def local_state(core, log_decay, keys, values):
    heads, rows = log_decay.shape
    pieces = jax.ShapeDtypeStruct((heads, PIECE, DH), F32)
    table = jax.ShapeDtypeStruct((heads * ROWS, SPAN), F32)
    like = jax.ShapeDtypeStruct(keys.shape, BF16)
    return pl.pallas_call(
        state_body,
        in_specs=[SMEM, VMEM, HBM, HBM],
        out_specs=[VMEM] * 7,
        out_shape=[pieces, pieces, table, table, table, like, like],
        scratch_shapes=[pltpu.SemaphoreType.DMA((2, heads // GROUP))],
        compiler_params=params(8),
        cost_estimate=cost(2 * heads * rows * DH * DH, 4 * rows * heads * DH),
        name="local_state",
    )(core, log_decay, keys, values)


def scan_body(reverse, in_ref, after_ref, out_ref):
    count = in_ref.shape[0]
    state = jnp.zeros((HALF, DH), F32)
    extra = jnp.zeros((ROWS, DH), F32)
    for lap in range(count):
        at = count - 1 - lap if reverse else lap
        out_ref[at, :HALF, :] = state
        state = in_ref[at, HALF : HALF + 1, :] * state + in_ref[at, :HALF, :]
        extra = extra + in_ref[at, HALF:, :]
    for at in range(count):
        out_ref[at, HALF:, :] = extra


def scan_pieces(pieces, after, reverse):
    count = pieces.shape[0]
    return pl.pallas_call(
        functools.partial(scan_body, reverse),
        in_specs=[VMEM, ANY],
        out_specs=VMEM,
        out_shape=jax.ShapeDtypeStruct(pieces.shape, F32),
        compiler_params=params(8),
        cost_estimate=cost(2 * count * HALF * DH, 8 * count * HALF * DH),
        name="scan_pieces",
    )(pieces, after)


def scan_over_seq(send, own, core, reverse, during_out, during_back):
    count = lax.axis_size("seq")
    chips = [list(range(c, count, 2)) for c in range(2)]
    pairs = [(i, i ^ 1) for i in range(count)]
    got = lax.ppermute(send, "seq", pairs)
    near_here = jnp.logical_xor(core == 0, reverse)
    near = jnp.where(near_here, own, got)
    far = jnp.where(near_here, got, own)
    row = lax.broadcasted_iota(jnp.int32, (1, PIECE, 1), 1)
    both = jnp.where(row <= HALF, far[:, HALF : HALF + 1], 1.0) * near + jnp.where(row == HALF, 0.0, far)
    shared = lax.all_to_all(both, "seq", 0, 0, axis_index_groups=chips)
    meanwhile = during_out(both)
    scanned = scan_pieces(shared, meanwhile[-1], reverse)
    entering = lax.all_to_all(scanned, "seq", 0, 0, axis_index_groups=chips)
    meanwhile = during_back(scanned, meanwhile)
    passed = jnp.where(row < HALF, near[:, HALF : HALF + 1] * entering + near, entering)
    keep = jnp.where(near_here, entering, passed)
    give = jnp.where(near_here, passed, entering)
    taken = lax.ppermute(give, "seq", pairs)
    return keep, taken, meanwhile


def attend_body(first_head, count, loads, *refs):
    _, k_ref, v_ref, cum_ref, before_ref = refs[:5]
    refs = refs[5:]
    blocks = k_ref.shape[0] // SPAN
    if loads:
        q_hbm, local_ref, low_ref, turned_ref, q_ref, q_sems = refs
        copies = []
        for g in range(q_hbm.shape[1] // (GROUP * DH)):
            lanes = slice(g * GROUP * DH, (g + 1) * GROUP * DH)
            copies.append(pltpu.make_async_copy(q_hbm.at[:, lanes], q_ref.at[:, lanes], q_sems.at[g]))
            copies[-1].start()
    else:
        q_ref, go_hbm, _, _, _, local_ref, low_ref, turned_ref, go_ref, go_sem = refs
        go_copy = pltpu.make_async_copy(go_hbm, go_ref, go_sem)
        go_copy.start()
    mask, _ = masks()

    def one(head):
        lanes = head_lanes(head)
        cum = head_rows(cum_ref, head)
        end, mid = last_lane(cum), middle_lane(cum)
        before = head_rows(before_ref, head)
        query_col = jnp.exp(cum - mid).T
        key_col = jnp.exp(mid - cum).T
        query_row = jnp.exp(cum + before)
        mid_scale, end_scale, rest_scale = jnp.exp(mid), jnp.exp(end), jnp.exp(end - mid)
        q_up = [(q_ref[span(n), lanes].astype(F32) * query_col[:, n : n + 1]).astype(BF16) for n in range(blocks)]
        k_up = [(k_ref[span(n), lanes].astype(F32) * key_col[:, n : n + 1]).astype(BF16) for n in range(blocks)]
        turned_ref[head] = (q_ref[:, lanes].T.astype(F32) * join_rows(query_row, blocks)).astype(BF16)
        weights = [jnp.where(mask, nt(q_up[n], k_up[n]), 0.0).astype(BF16) for n in range(blocks)]
        updates = [nn(k_up[n].T, v_ref[span(n), lanes]) for n in range(blocks - 1)]
        state = jnp.zeros((DH, DH), F32)
        lows = []
        for n in range(blocks):
            lows.append((mid_scale[n : n + 1] * state).astype(BF16))
            low_ref[head, n] = lows[n]
            if n < blocks - 1:
                state = end_scale[n : n + 1] * state + rest_scale[n : n + 1] * updates[n]
        for n in range(blocks):
            total = nn(
                jnp.concatenate([weights[n], q_up[n]], axis=1),
                jnp.concatenate([v_ref[span(n), lanes], lows[n]], axis=0),
            )
            local_ref[span(n), lanes] = total.astype(BF16)

    if loads:
        for g, copy in enumerate(copies):
            copy.wait()
            if g * GROUP < count:

                @pl.loop(0, GROUP)
                def _(at):
                    one(first_head + g * GROUP + at)
    else:

        @pl.loop(0, count)
        def _(at):
            one(first_head + at)

        go_copy.wait()


def attend_first(after, keys, values, cum, before, queries):
    rows, width = keys.shape
    heads, blocks = width // DH, rows // SPAN
    like = jax.ShapeDtypeStruct((rows, width), BF16)
    return pl.pallas_call(
        functools.partial(attend_body, 0, heads // 2, True),
        in_specs=[ANY, VMEM, VMEM, VMEM, VMEM, HBM],
        out_specs=[VMEM] * 4,
        out_shape=[
            like,
            jax.ShapeDtypeStruct((heads, blocks, DH, DH), BF16),
            jax.ShapeDtypeStruct((heads, DH, rows), BF16),
            like,
        ],
        scratch_shapes=[pltpu.SemaphoreType.DMA((heads // GROUP,))],
        compiler_params=params(8),
        cost_estimate=cost(5 * rows * width * DH, 6 * rows * width),
        name="attend_first",
    )(after, keys, values, cum, before, queries)


def attend_second(after, keys, values, cum, before, queries, grad_out, local, lows, turned):
    rows, width = keys.shape
    heads = width // DH
    return pl.pallas_call(
        functools.partial(attend_body, heads // 2, heads // 2, False),
        in_specs=[ANY, VMEM, VMEM, VMEM, VMEM, VMEM, HBM, VMEM, VMEM, VMEM],
        out_specs=[VMEM] * 4,
        out_shape=[jax.ShapeDtypeStruct(a.shape, a.dtype) for a in (local, lows, turned, grad_out)],
        input_output_aliases={7: 0, 8: 1, 9: 2},
        scratch_shapes=[pltpu.SemaphoreType.DMA],
        compiler_params=params(8),
        cost_estimate=cost(5 * rows * width * DH, 6 * rows * width),
        name="attend_second",
    )(after, keys, values, cum, before, queries, grad_out, local, lows, turned)


def enter_body(core_ref, q_ref, local_ref, go_ref, gain_ref, keep_ref, taken_ref, cum_ref, before_ref,
               attn_ref, low_ref, stats_ref, square_ref, inner_ref):
    rows, width = q_ref.shape
    heads, blocks = width // DH, rows // SPAN
    half = heads // 2
    core = core_ref[0]
    square_ref[...] = jnp.zeros_like(square_ref)
    inner_ref[...] = jnp.zeros_like(inner_ref)

    @pl.loop(0, heads // GROUP)
    def _(g):
        first = lax.rem(core * half + g * GROUP, heads)
        lows, scales, gains = [], [], []
        for at in range(GROUP):
            low = piece_state(keep_ref, taken_ref, g * GROUP + at, half).astype(BF16)
            low_ref[first + at] = low
            lows.append(low)
            scales.append(jnp.exp(head_rows(cum_ref, first + at) + head_rows(before_ref, first + at)).T)
            gains.append(gain_ref[:, head_lanes(first + at)])
        for n in range(blocks):
            square = jnp.zeros((SPAN, DH), F32)
            inner = jnp.zeros((SPAN, DH), F32)
            for at in range(GROUP):
                lanes = head_lanes(first + at)
                carried = nn(q_ref[span(n), lanes], lows[at]) * scales[at][:, n : n + 1]
                attn = (local_ref[span(n), lanes].astype(F32) + carried).astype(BF16)
                attn_ref[span(n), lanes] = attn
                attn = attn.astype(F32)
                square += attn * attn
                inner += go_ref[span(n), lanes].astype(F32) * gains[at] * attn
            square_ref[span(n), :] += square
            inner_ref[span(n), :] += inner

    ones = jnp.ones((8, DH), F32)
    stats_ref[0:1, :] = dot(ones, square_ref[...], (1, 1), EXACT)[0:1]
    stats_ref[1:2, :] = dot(ones, inner_ref[...], (1, 1), EXACT)[0:1]


def attend_entering(core, queries, local, grad_out, gain, keep, taken, cum, before):
    rows, width = queries.shape
    heads = width // DH
    return pl.pallas_call(
        enter_body,
        in_specs=[SMEM] + [VMEM] * 8,
        out_specs=[VMEM] * 3,
        out_shape=[
            jax.ShapeDtypeStruct((rows, width), BF16),
            jax.ShapeDtypeStruct((heads, DH, DH), BF16),
            jax.ShapeDtypeStruct((2, rows), F32),
        ],
        scratch_shapes=[pltpu.VMEM((rows, DH), F32), pltpu.VMEM((rows, DH), F32)],
        compiler_params=params(8),
        cost_estimate=cost(2 * rows * width * DH, 8 * rows * width),
        name="attend_entering",
    )(core, queries, local, grad_out, gain, keep, taken, cum, before)


def columns(row, ref, blocks):
    for n in range(blocks):
        ref[span(n), :] = jnp.broadcast_to(row[:, span(n)], (SPAN, SPAN)).T


def inverse_row(stats_ref):
    return lax.rsqrt(stats_ref[0:1, :] / (HEAD_TOTAL * DH) + 1e-06)


def norm_body(core_ref, turned_ref, attn_ref, go_ref, gain_ref, stats_ref, total_ref, ga_ref, send_ref, own_ref, inverse_ref,
              factor_ref):
    rows, width = attn_ref.shape
    heads, blocks = width // DH, rows // SPAN
    half = heads // 2
    core = core_ref[0]
    inverse = inverse_row(stats_ref)
    columns(inverse, inverse_ref, blocks)
    columns(inverse * inverse * inverse * (stats_ref[1:2, :] / (HEAD_TOTAL * DH)), factor_ref, blocks)

    for out, offset in ((send_ref, 0), (own_ref, half)):

        @pl.loop(0, half // 2)
        def _(g):
            for at in range(2):
                place = 2 * g + at
                head = lax.rem((1 - core) * half + offset + place, heads)
                lanes = head_lanes(head)
                gain = gain_ref[:, lanes]
                gain_sum = jnp.zeros((8, DH), F32)
                grads = []
                for n in range(blocks):
                    attn = attn_ref[span(n), lanes].astype(F32)
                    scaled = go_ref[span(n), lanes].astype(F32) * inverse_ref[span(n), :]
                    gain_sum += jnp.sum((scaled * attn).reshape(SPAN // 8, 8, DH), axis=0)
                    grad = (scaled * gain - attn * factor_ref[span(n), :]).astype(BF16)
                    ga_ref[span(n), lanes] = grad
                    grads.append(grad)
                state = nn(turned_ref[head], jnp.concatenate(grads, axis=0))
                extra = extra_rows(jnp.exp(head_rows(total_ref, head)), jnp.sum(gain_sum, axis=0, keepdims=True))
                piece_store(out, place, state, extra)


def norm_backward(core, turned, attn, grad_out, gain, stats, total):
    rows, width = attn.shape
    heads = width // DH
    pieces = jax.ShapeDtypeStruct((heads, PIECE, DH), F32)
    return pl.pallas_call(
        norm_body,
        in_specs=[SMEM] + [VMEM] * 6,
        out_specs=[VMEM] * 3,
        out_shape=[jax.ShapeDtypeStruct((rows, width), BF16), pieces, pieces],
        scratch_shapes=[pltpu.VMEM((rows, DH), F32), pltpu.VMEM((rows, DH), F32)],
        compiler_params=params(8),
        cost_estimate=cost(2 * rows * width * DH, 8 * rows * width),
        name="norm_backward",
    )(core, turned, attn, grad_out, gain, stats, total)


def grads_body(first_head, count, chained, *refs):
    _, q_ref, k_ref, v_ref, ga_ref, attn_ref, gain_ref, stats_ref, low_ref, enter_ref, cum_ref, before_ref = refs[:12]
    refs = refs[12 + (4 if chained else 0) :]
    out_hbm, gq_hbm, lk_ref, lv_ref, out_ref, gq_ref, inverse_ref, sems = refs
    blocks = q_ref.shape[0] // SPAN
    mask, turned_mask = masks()
    columns(inverse_row(stats_ref), inverse_ref, blocks)

    def one(head, place):
        lanes, here = head_lanes(head), head_lanes(place)
        cum = head_rows(cum_ref, head)
        end, mid = last_lane(cum), middle_lane(cum)
        query_col = jnp.exp(cum - mid).T
        key_col = jnp.exp(mid - cum).T
        mid_scale, end_scale, rest_scale = jnp.exp(mid), jnp.exp(end), jnp.exp(end - mid)
        enter_scale = jnp.exp(mid + head_rows(before_ref, head))
        entering = enter_ref[head].astype(F32)
        gain = gain_ref[:, lanes]
        q_up = [(q_ref[span(n), lanes].astype(F32) * query_col[:, n : n + 1]).astype(BF16) for n in range(blocks)]
        updates = [nn(q_up[n].T, ga_ref[span(n), lanes]) for n in range(blocks)]
        back = jnp.zeros((DH, DH), F32)
        lows = [None] * blocks
        for n in reversed(range(blocks)):
            lows[n] = (rest_scale[n : n + 1] * back).astype(BF16)
            if n > 0:
                back = end_scale[n : n + 1] * back + mid_scale[n : n + 1] * updates[n]
        for n in range(blocks):
            k, v, ga = k_ref[span(n), lanes], v_ref[span(n), lanes], ga_ref[span(n), lanes]
            k_up = (k.astype(F32) * key_col[:, n : n + 1]).astype(BF16)
            out_ref[span(n), here] = (attn_ref[span(n), lanes].astype(F32) * inverse_ref[span(n), :] * gain).astype(BF16)
            scores = jnp.where(mask, nt(ga, v), 0.0).astype(BF16)
            turned_scores = jnp.where(turned_mask, nt(v, ga), 0.0).astype(BF16)
            turned_weights = jnp.where(turned_mask, nt(k_up, q_up[n]), 0.0).astype(BF16)
            state = (low_ref[head, n].astype(F32) + enter_scale[n : n + 1] * entering).astype(BF16)
            grad_q = (nn(scores, k_up) + nt(ga, state)) * query_col[:, n : n + 1]
            gq_ref[span(n), here] = grad_q.astype(BF16)
            grad_k = (nn(turned_scores, q_up[n]) + nt(v, lows[n])) * key_col[:, n : n + 1]
            lk_ref[span(n), lanes] = grad_k.astype(BF16)
            grad_v = nn(
                jnp.concatenate([turned_weights, k_up], axis=1), jnp.concatenate([ga, lows[n]], axis=0)
            )
            lv_ref[span(n), lanes] = grad_v.astype(BF16)

    copies = []
    for g in range(count // GROUP):

        @pl.loop(0, GROUP)
        def _(at):
            one(first_head + g * GROUP + at, g * GROUP + at)

        here = slice(g * GROUP * DH, (g + 1) * GROUP * DH)
        there = slice((first_head + g * GROUP) * DH, (first_head + (g + 1) * GROUP) * DH)
        for which, (source, target) in enumerate(((out_ref, out_hbm), (gq_ref, gq_hbm))):
            copies.append(pltpu.make_async_copy(source.at[:, here], target.at[:, there], sems.at[which, g]))
            copies[-1].start()
    for copy in copies:
        copy.wait()


def grads_local(after, first_head, count, inputs, chained):
    rows, width = inputs[0].shape
    like = jax.ShapeDtypeStruct((rows, width), BF16)
    kinds = [HBM, HBM, VMEM, VMEM]
    return pl.pallas_call(
        functools.partial(grads_body, first_head, count, bool(chained)),
        in_specs=[ANY] + [VMEM] * 11 + (kinds if chained else []),
        out_specs=kinds,
        out_shape=[like] * 4,
        input_output_aliases={12 + i: i for i in range(4)} if chained else {},
        scratch_shapes=[
            pltpu.VMEM((rows, count * DH), BF16),
            pltpu.VMEM((rows, count * DH), BF16),
            pltpu.VMEM((rows, DH), F32),
            pltpu.SemaphoreType.DMA((2, count // GROUP)),
        ],
        compiler_params=params(12),
        cost_estimate=cost(11 * rows * width * DH, 12 * rows * width),
        name="grads_second" if chained else "grads_first",
    )(after, *inputs, *chained)


def leave_body(core_ref, k_ref, v_ref, lk_ref, lv_ref, keep_ref, taken_ref, cum_ref, before_ref, total_ref,
               gk_hbm, gv_hbm, gg_ref, gk_ref, gv_ref, sems):
    rows, width = k_ref.shape
    heads, blocks = width // DH, rows // SPAN
    half = heads // 2
    core = core_ref[0]
    copies = []
    for g in range(heads // GROUP):
        first = lax.rem(core * half + g * GROUP, heads)

        @pl.loop(0, GROUP)
        def _(at):
            head = first + at
            lanes = head_lanes(head)
            low = piece_state(keep_ref, taken_ref, g * GROUP + at, half).astype(BF16)
            place = 2 * ((g * GROUP) % half + at)
            gg_ref[:, lanes] = (keep_ref if g * GROUP < half else taken_ref)[place, HALF + 1 : HALF + 2, :]
            scale = jnp.exp(head_rows(total_ref, head) - head_rows(before_ref, head) - head_rows(cum_ref, head)).T
            for n in range(blocks):
                factor = scale[:, n : n + 1]
                grad_k = lk_ref[span(n), lanes].astype(F32) + factor * nt(v_ref[span(n), lanes], low)
                grad_v = lv_ref[span(n), lanes].astype(F32) + factor * nn(k_ref[span(n), lanes], low)
                gk_ref[span(n), lanes] = grad_k.astype(BF16)
                gv_ref[span(n), lanes] = grad_v.astype(BF16)

        lanes = head_lanes(first, GROUP)
        for which, (source, target) in enumerate(((gk_ref, gk_hbm), (gv_ref, gv_hbm))):
            copies.append(pltpu.make_async_copy(source.at[:, lanes], target.at[:, lanes], sems.at[which, g]))
            copies[-1].start()
    for copy in copies:
        copy.wait()


def grads_leaving(core, keys, values, local_k, local_v, keep, taken, cum, before, total):
    rows, width = keys.shape
    like = jax.ShapeDtypeStruct((rows, width), BF16)
    return pl.pallas_call(
        leave_body,
        in_specs=[SMEM] + [VMEM] * 9,
        out_specs=[HBM, HBM, VMEM],
        out_shape=[like, like, jax.ShapeDtypeStruct((1, width), F32)],
        scratch_shapes=[
            pltpu.VMEM((rows, width), BF16),
            pltpu.VMEM((rows, width), BF16),
            pltpu.SemaphoreType.DMA((2, width // DH // GROUP)),
        ],
        compiler_params=params(12),
        cost_estimate=cost(4 * rows * width * DH, 12 * rows * width),
        name="grads_leaving",
    )(core, keys, values, local_k, local_v, keep, taken, cum, before, total)


def per_device(queries, keys, values, log_decay, gain, grad_out):
    core = lax.rem(lax.axis_index("seq"), 2)
    core_arg = core.astype(jnp.int32).reshape(1)
    gain_row = gain.reshape(1, -1)
    heads = log_decay.shape[0]
    send, own, cum, before, total, keys, values = local_state(core_arg, log_decay, keys, values)

    def attend_out(after):
        return attend_first(after, keys, values, cum, before, queries)

    def attend_back(after, done):
        local, lows, turned, held = done
        return (*attend_second(after, keys, values, cum, before, held, grad_out, local, lows, turned), held)

    keep, taken, (local, lows, turned, grad_out, queries) = scan_over_seq(
        send, own, core, False, attend_out, attend_back
    )
    attn, entering, stats = attend_entering(
        core_arg, queries, local, grad_out, gain_row, keep, taken, cum, before
    )
    stats = lax.psum(stats, "head")
    grad_attn, send, own = norm_backward(core_arg, turned, attn, grad_out, gain_row, stats, total)
    inputs = (queries, keys, values, grad_attn, attn, gain_row, stats, lows, entering, cum, before)

    def grads_out(after):
        return grads_local(after, 0, heads // 2, inputs, ())

    def grads_back(after, done):
        return grads_local(after, heads // 2, heads // 2, inputs, done)

    keep, taken, (output, grad_q, local_k, local_v) = scan_over_seq(send, own, core, True, grads_out, grads_back)
    grad_k, grad_v, grad_gain = grads_leaving(
        core_arg, keys, values, local_k, local_v, keep, taken, cum, before, total
    )
    return output, grad_q, grad_k, grad_v, grad_gain.reshape(-1)


def solution(mesh):
    tokens, heads = P("seq", "head"), P("head")
    return jax.shard_map(
        per_device,
        mesh=mesh,
        in_specs=(tokens, tokens, tokens, P("head", "seq"), heads, tokens),
        out_specs=(tokens, tokens, tokens, tokens, heads),
        check_vma=False,
    )
```

```python
import functools

import jax
import jax.numpy as jnp
from jax import lax
from jax.experimental import pallas as pl
from jax.experimental.pallas import tpu as pltpu
from jax.sharding import PartitionSpec as P

HEAD_TOTAL = 64
DH = 128
SPAN = 128
ROWS = 8
PIECE = DH + ROWS
GROUP = 4
PAIR = 2
ALONG_X, ALONG_Z = 4, 4
F32 = jnp.float32
BF16 = jnp.bfloat16
EXACT = lax.Precision.HIGHEST
VMEM = pl.BlockSpec(memory_space=pltpu.VMEM)
SMEM = pl.BlockSpec(memory_space=pltpu.SMEM)
HBM = pl.BlockSpec(memory_space=pltpu.HBM)
ANY = pl.BlockSpec(memory_space=pl.ANY)


def dot(a, b, contract, precision=None):
    return lax.dot_general(
        a, b, ((contract[:1], contract[1:]), ((), ())), precision=precision, preferred_element_type=F32
    )


def nn(a, b):
    return dot(a, b, (1, 0))


def nt(a, b):
    return dot(a, b, (1, 1))


def params(mib):
    return pltpu.CompilerParams(vmem_limit_bytes=mib * 1024 * 1024)


def cost(flops, nbytes):
    return pl.CostEstimate(flops=int(flops), bytes_accessed=int(nbytes), transcendentals=0)


def head_rows(ref, head):
    return ref[pl.ds(pl.multiple_of(head * ROWS, ROWS), ROWS), :]


def head_lanes(head, count=1):
    return pl.ds(pl.multiple_of(head * DH, DH), count * DH)


def span(n):
    return slice(n * SPAN, (n + 1) * SPAN)


def last_lane(rows):
    return jnp.broadcast_to(rows[:, SPAN - 1 :], rows.shape)


def middle_lane(rows):
    return jnp.broadcast_to(rows[:, SPAN // 2 - 1 : SPAN // 2], rows.shape)


def masks():
    i = lax.broadcasted_iota(jnp.int32, (SPAN, SPAN), 0)
    j = lax.broadcasted_iota(jnp.int32, (SPAN, SPAN), 1)
    return i >= j, i <= j


def join_rows(rows, blocks):
    return jnp.concatenate([rows[n : n + 1] for n in range(blocks)], axis=1)


def piece_store(ref, at, state, extra):
    ref[at, :DH, :] = state
    ref[at, DH:, :] = extra


def piece_state(keep_ref, taken_ref, at, half):
    kept = at < half
    place = jnp.where(kept, at, at - half)
    return jnp.where(kept, keep_ref[place, :DH, :], taken_ref[place, :DH, :])


def extra_rows(decay, gain_row=None):
    place = lax.broadcasted_iota(jnp.int32, (ROWS, DH), 0)
    rest = 0.0 if gain_row is None else jnp.where(place == 1, gain_row, 0.0)
    return jnp.where(place == 0, decay, rest)


def state_body(core_ref, log_ref, k_hbm, v_hbm, send_ref, own_ref, cum_ref, before_ref, total_ref, k_ref, v_ref, sems):
    heads, rows = log_ref.shape
    blocks, half = rows // SPAN, heads // 2
    core = core_ref[0]
    copies = []
    for g in range(heads // GROUP):
        first = lax.rem((1 - core) * half + g * GROUP, heads)
        lanes = head_lanes(first, GROUP)
        pair = [
            pltpu.make_async_copy(k_hbm.at[:, lanes], k_ref.at[:, lanes], sems.at[0, g]),
            pltpu.make_async_copy(v_hbm.at[:, lanes], v_ref.at[:, lanes], sems.at[1, g]),
        ]
        for copy in pair:
            copy.start()
        copies.append((first, pair))

    _, triangle = masks()
    triangle = triangle.astype(F32)
    cum_ref[...] = jnp.zeros_like(cum_ref)
    before_ref[...] = jnp.zeros_like(before_ref)
    before = jnp.zeros((heads, SPAN), F32)
    for n in range(blocks):
        cum = dot(log_ref[:, span(n)], triangle, (1, 0), EXACT)
        for h in range(heads):
            cum_ref[h * ROWS + n : h * ROWS + n + 1, :] = cum[h : h + 1]
            before_ref[h * ROWS + n : h * ROWS + n + 1, :] = before[h : h + 1]
        before = before + last_lane(cum)
    for h in range(heads):
        total_ref[h * ROWS : (h + 1) * ROWS, :] = jnp.broadcast_to(before[h : h + 1], (ROWS, SPAN))

    for g, (first, pair) in enumerate(copies):
        for copy in pair:
            copy.wait()
        totals = [head_rows(total_ref, first + at) for at in range(GROUP)]
        scales = [
            jnp.exp(totals[at] - head_rows(before_ref, first + at) - head_rows(cum_ref, first + at)) for at in range(GROUP)
        ]
        decayed = [
            (k_ref[:, head_lanes(first + at)].T.astype(F32) * join_rows(scales[at], blocks)).astype(BF16)
            for at in range(GROUP)
        ]
        states = [nn(decayed[at], v_ref[:, head_lanes(first + at)]) for at in range(GROUP)]
        for at in range(GROUP):
            place = (g * GROUP + at) % half
            out = send_ref if g * GROUP < half else own_ref
            piece_store(out, place, states[at], extra_rows(jnp.exp(totals[at])))


def local_state(position, log_decay, keys, values):
    heads, rows = log_decay.shape
    pieces = jax.ShapeDtypeStruct((heads // 2, PIECE, DH), F32)
    table = jax.ShapeDtypeStruct((heads * ROWS, SPAN), F32)
    like = jax.ShapeDtypeStruct(keys.shape, BF16)
    return pl.pallas_call(
        state_body,
        in_specs=[SMEM, VMEM, HBM, HBM],
        out_specs=[VMEM] * 7,
        out_shape=[pieces, pieces, table, table, table, like, like],
        scratch_shapes=[pltpu.SemaphoreType.DMA((2, heads // GROUP))],
        compiler_params=params(16),
        cost_estimate=cost(2 * heads * rows * DH * DH, 4 * rows * heads * DH),
        name="local_state",
    )(position, log_decay, keys, values)


def first_row():
    return lax.broadcasted_iota(jnp.int32, (ROWS, DH), 0) == 0


def join_extra(a, b):
    return jnp.where(first_row(), a * b, a + b)


def cores_body(reverse, position_ref, own_ref, got_ref, *out_refs):
    z = position_ref[1]
    near_here = (position_ref[0] == 0) != reverse
    each = own_ref.shape[0] // ALONG_Z
    for shift, out_ref in enumerate(out_refs):
        for j in range(each):
            head = lax.rem(z + shift, ALONG_Z) * each + j
            own, got = own_ref[head], got_ref[head]
            near, far = jnp.where(near_here, own, got), jnp.where(near_here, got, own)
            piece_store(out_ref, j, far[DH : DH + 1] * near[:DH] + far[:DH], join_extra(near[DH:], far[DH:]))


def along_z_body(reverse, position_ref, *refs):
    in_refs, (_, total_ref, prefix_ref, slots) = refs[:ALONG_Z], refs[ALONG_Z:]
    z = position_ref[1]
    for shift, ref in enumerate(in_refs):
        slots[lax.rem(z - shift + ALONG_Z, ALONG_Z)] = ref[...]
    for j in range(total_ref.shape[0]):
        state = jnp.zeros((DH, DH), F32)
        extra = jnp.where(first_row(), 1.0, 0.0)
        for lap in range(ALONG_Z):
            at = ALONG_Z - 1 - lap if reverse else lap
            prefix_ref[at, j, :DH, :] = state
            prefix_ref[at, j, DH:, :] = extra
            state = slots[at, j, DH : DH + 1, :] * state + slots[at, j, :DH, :]
            extra = join_extra(extra, slots[at, j, DH:, :])
        piece_store(total_ref, j, state, extra)


def along_x_body(reverse, position_ref, *refs):
    in_refs, prefix_ref, out_refs, slots = refs[:ALONG_X], refs[ALONG_X], refs[ALONG_X + 2 : -1], refs[-1]
    z, x = position_ref[1], position_ref[2]
    for shift, ref in enumerate(in_refs):
        slots[lax.rem(x - shift + ALONG_X, ALONG_X)] = ref[...]
    for j in range(prefix_ref.shape[1]):
        state = jnp.zeros((DH, DH), F32)
        extra = jnp.zeros((ROWS, DH), F32)
        for lap in range(ALONG_X):
            at = ALONG_X - 1 - lap if reverse else lap
            taken = (at > x) if reverse else (at < x)
            state = jnp.where(taken, slots[at, j, DH : DH + 1, :] * state + slots[at, j, :DH, :], state)
            extra = extra + slots[at, j, DH:, :]
        for shift, out_ref in enumerate(out_refs):
            at = lax.rem(z + shift, ALONG_Z)
            piece_store(out_ref, j, prefix_ref[at, j, :DH, :] + prefix_ref[at, j, DH : DH + 1, :] * state, extra)


def entering_body(reverse, position_ref, *refs):
    in_refs, (own_ref, got_ref, _, keep_ref, give_ref) = refs[:ALONG_Z], refs[ALONG_Z:]
    z = position_ref[1]
    near_here = (position_ref[0] == 0) != reverse
    each = own_ref.shape[0] // ALONG_Z
    for shift, ref in enumerate(in_refs):
        for j in range(each):
            head = lax.rem(z - shift + ALONG_Z, ALONG_Z) * each + j
            near = jnp.where(near_here, own_ref[head], got_ref[head])
            entering, extra = ref[j, :DH, :], ref[j, DH:, :]
            passed = near[DH : DH + 1] * entering + near[:DH]
            piece_store(keep_ref, head, jnp.where(near_here, entering, passed), extra)
            piece_store(give_ref, head, jnp.where(near_here, passed, entering), extra)


def scan_step(body, name, reverse, position, arrays, after, out_counts, scratch):
    shapes = [jax.ShapeDtypeStruct(shape, F32) for shape in out_counts]
    afters = [] if after is None else [after]
    return pl.pallas_call(
        functools.partial(body, reverse),
        in_specs=[SMEM] + [VMEM] * len(arrays) + [ANY] * len(afters),
        out_specs=[VMEM] * len(shapes),
        out_shape=shapes,
        scratch_shapes=scratch,
        compiler_params=params(4),
        cost_estimate=cost(10**6, 10**6),
        name=name,
    )(position, *arrays, *afters)


def scan_over_seq(send, own, position, reverse, works):
    count = lax.axis_size("seq")
    heads = own.shape[0]
    each = heads // ALONG_Z

    def index(x, z, c):
        return (x % ALONG_X * ALONG_Z + z % ALONG_Z) * 2 + c

    every = [(x, z, c) for x in range(ALONG_X) for z in range(ALONG_Z) for c in range(2)]
    across = [(i, i ^ 1) for i in range(count)]
    by_z = [[(index(x, z, c), index(x, z + s, c)) for x, z, c in every] for s in range(ALONG_Z)]
    by_x = [[(index(x, z, c), index(x + s, z, c)) for x, z, c in every] for s in range(ALONG_X)]
    piece = (each, PIECE, DH)

    got = lax.ppermute(send, "seq", across)
    parts = scan_step(cores_body, "join_cores", reverse, position, [own, got], None, [piece] * ALONG_Z, [])
    arrived = [parts[0]] + [lax.ppermute(parts[s], "seq", by_z[s]) for s in range(1, ALONG_Z)]
    done = works[0](parts[0], ())
    total, prefix = scan_step(
        along_z_body, "join_z", reverse, position, arrived, done[-1],
        [piece, (ALONG_Z,) + piece], [pltpu.VMEM((ALONG_Z,) + piece, F32)],
    )
    totals = [total] + [lax.ppermute(total, "seq", by_x[s]) for s in range(1, ALONG_X)]
    done = works[1](total, done)
    parts = scan_step(
        along_x_body, "join_x", reverse, position, totals + [prefix], done[-1],
        [piece] * ALONG_Z, [pltpu.VMEM((ALONG_X,) + piece, F32)],
    )
    arrived = [parts[0]] + [lax.ppermute(parts[s], "seq", by_z[s]) for s in range(1, ALONG_Z)]
    done = works[2](parts[0], done)
    keep, give = scan_step(
        entering_body, "entering", reverse, position, arrived + [own, got], done[-1], [own.shape] * 2, []
    )
    return keep, lax.ppermute(give, "seq", across), done


def attend_pair(heads, q_ref, k_ref, v_ref, cum_ref, before_ref, local_ref, low_ref, turned_ref, mask):
    blocks = k_ref.shape[0] // SPAN
    each = range(len(heads))
    steps = [(a, n) for n in range(blocks) for a in each]
    lanes = [head_lanes(h) for h in heads]
    cums = [head_rows(cum_ref, h) for h in heads]
    mids = [middle_lane(c) for c in cums]
    ends = [last_lane(c) for c in cums]
    query_col = [jnp.exp(c - m).T for c, m in zip(cums, mids)]
    key_col = [jnp.exp(m - c).T for c, m in zip(cums, mids)]
    query_row = [jnp.exp(c + head_rows(before_ref, h)) for c, h in zip(cums, heads)]
    mid_scale, end_scale = [jnp.exp(m) for m in mids], [jnp.exp(e) for e in ends]
    rest_scale = [jnp.exp(e - m) for e, m in zip(ends, mids)]
    q_up = {(a, n): (q_ref[span(n), lanes[a]].astype(F32) * query_col[a][:, n : n + 1]).astype(BF16) for a, n in steps}
    k_up = {(a, n): (k_ref[span(n), lanes[a]].astype(F32) * key_col[a][:, n : n + 1]).astype(BF16) for a, n in steps}
    scores = {s: nt(q_up[s], k_up[s]) for s in steps}
    updates = {(a, n): nn(k_up[a, n].T, v_ref[span(n), lanes[a]]) for a, n in steps if n < blocks - 1}
    weights = {s: jnp.where(mask, scores[s], 0.0).astype(BF16) for s in steps}
    lows = {}
    for a in each:
        state = jnp.zeros((DH, DH), F32)
        for n in range(blocks):
            lows[a, n] = (mid_scale[a][n : n + 1] * state).astype(BF16)
            low_ref[heads[a], n] = lows[a, n]
            if n < blocks - 1:
                state = end_scale[a][n : n + 1] * state + rest_scale[a][n : n + 1] * updates[a, n]
    totals = {
        (a, n): nn(
            jnp.concatenate([weights[a, n], q_up[a, n]], axis=1),
            jnp.concatenate([v_ref[span(n), lanes[a]], lows[a, n]], axis=0),
        )
        for a, n in steps
    }
    for a, n in steps:
        local_ref[span(n), lanes[a]] = totals[a, n].astype(BF16)
    for a in each:
        turned_ref[heads[a]] = (q_ref[:, lanes[a]].T.astype(F32) * join_rows(query_row[a], blocks)).astype(BF16)


def attend_body(first, count, load, *refs):
    k_ref, v_ref, cum_ref, before_ref = refs[1:5]
    refs = refs[5:]
    copies = []
    if load == "queries":
        q_hbm, local_ref, low_ref, turned_ref, q_ref, sems = refs
        for g in range(q_hbm.shape[1] // (GROUP * DH)):
            lanes = slice(g * GROUP * DH, (g + 1) * GROUP * DH)
            copies.append(pltpu.make_async_copy(q_hbm.at[:, lanes], q_ref.at[:, lanes], sems.at[g]))
    elif load == "grad_out":
        q_ref, go_hbm, _, _, _, local_ref, low_ref, turned_ref, go_ref, sems = refs
        copies.append(pltpu.make_async_copy(go_hbm, go_ref, sems.at[0]))
    else:
        q_ref, _, _, _, local_ref, low_ref, turned_ref = refs
    for copy in copies:
        copy.start()
    mask, _ = masks()

    def pairs(start, stop):
        @pl.loop(start // PAIR, stop // PAIR)
        def _(at):
            heads = [at * PAIR + a for a in range(PAIR)]
            attend_pair(heads, q_ref, k_ref, v_ref, cum_ref, before_ref, local_ref, low_ref, turned_ref, mask)

    if load == "queries":
        for g, copy in enumerate(copies):
            copy.wait()
            if g * GROUP < count:
                pairs(g * GROUP, min((g + 1) * GROUP, count))
    else:
        pairs(first, first + count)
        for copy in copies:
            copy.wait()


def attend(after, first, count, load, keys, values, cum, before, queries, grad_out, done):
    rows, width = keys.shape
    heads, blocks = width // DH, rows // SPAN
    like = jax.ShapeDtypeStruct((rows, width), BF16)
    outs = [
        like,
        jax.ShapeDtypeStruct((heads, blocks, DH, DH), BF16),
        jax.ShapeDtypeStruct((heads, DH, rows), BF16),
    ]
    arrays, specs = [after, keys, values, cum, before, queries], [ANY, VMEM, VMEM, VMEM, VMEM]
    specs.append(HBM if load == "queries" else VMEM)
    if load == "grad_out":
        arrays.append(grad_out)
        specs.append(HBM)
    aliases = {len(arrays) + i: i for i in range(len(done))}
    if load is not None:
        outs.append(like)
    return pl.pallas_call(
        functools.partial(attend_body, first, count, load),
        in_specs=specs + [VMEM] * len(done),
        out_specs=[VMEM] * len(outs),
        out_shape=outs,
        input_output_aliases=aliases,
        scratch_shapes=[] if load is None else [pltpu.SemaphoreType.DMA((heads // GROUP,))],
        compiler_params=params(12),
        cost_estimate=cost(10 * rows * count * DH * DH, 12 * rows * count * DH),
        name=f"attend_{first}",
    )(*arrays, *done)


def enter_body(position_ref, q_ref, local_ref, go_ref, gain_ref, keep_ref, taken_ref, cum_ref, before_ref,
               attn_ref, low_ref, stats_ref, square_ref, inner_ref):
    rows, width = q_ref.shape
    heads, blocks = width // DH, rows // SPAN
    half = heads // 2
    core = position_ref[0]
    square_ref[...] = jnp.zeros_like(square_ref)
    inner_ref[...] = jnp.zeros_like(inner_ref)

    @pl.loop(0, heads // GROUP)
    def _(g):
        first = lax.rem(core * half + g * GROUP, heads)
        lanes = [head_lanes(first + at) for at in range(GROUP)]
        carried, scales, gains = [], [], []
        for at in range(GROUP):
            low = piece_state(keep_ref, taken_ref, g * GROUP + at, half).astype(BF16)
            low_ref[first + at] = low
            carried.append(nn(q_ref[:, lanes[at]], low))
            scales.append(jnp.exp(head_rows(cum_ref, first + at) + head_rows(before_ref, first + at)).T)
            gains.append(gain_ref[:, lanes[at]])
        for n in range(blocks):
            square = jnp.zeros((SPAN, DH), F32)
            inner = jnp.zeros((SPAN, DH), F32)
            for at in range(GROUP):
                entered = carried[at][span(n)] * scales[at][:, n : n + 1]
                attn = (local_ref[span(n), lanes[at]].astype(F32) + entered).astype(BF16)
                attn_ref[span(n), lanes[at]] = attn
                attn = attn.astype(F32)
                square += attn * attn
                inner += go_ref[span(n), lanes[at]].astype(F32) * gains[at] * attn
            square_ref[span(n), :] += square
            inner_ref[span(n), :] += inner

    ones = jnp.ones((8, DH), F32)
    stats_ref[0:1, :] = dot(ones, square_ref[...], (1, 1), EXACT)[0:1]
    stats_ref[1:2, :] = dot(ones, inner_ref[...], (1, 1), EXACT)[0:1]


def attend_entering(position, queries, local, grad_out, gain, keep, taken, cum, before):
    rows, width = queries.shape
    heads = width // DH
    return pl.pallas_call(
        enter_body,
        in_specs=[SMEM] + [VMEM] * 8,
        out_specs=[VMEM] * 3,
        out_shape=[
            jax.ShapeDtypeStruct((rows, width), BF16),
            jax.ShapeDtypeStruct((heads, DH, DH), BF16),
            jax.ShapeDtypeStruct((2, rows), F32),
        ],
        scratch_shapes=[pltpu.VMEM((rows, DH), F32), pltpu.VMEM((rows, DH), F32)],
        compiler_params=params(12),
        cost_estimate=cost(2 * rows * width * DH, 8 * rows * width),
        name="attend_entering",
    )(position, queries, local, grad_out, gain, keep, taken, cum, before)


def columns(row, ref, blocks):
    for n in range(blocks):
        ref[span(n), :] = jnp.broadcast_to(row[:, span(n)], (SPAN, SPAN)).T


def norm_body(position_ref, turned_ref, attn_ref, go_ref, gain_ref, total_ref, *refs):
    stats_refs, (ga_ref, send_ref, own_ref, row_ref, inverse_ref, factor_ref) = refs[:-6], refs[-6:]
    rows, width = attn_ref.shape
    heads, blocks = width // DH, rows // SPAN
    half = heads // 2
    core = position_ref[0]
    stats = functools.reduce(jnp.add, [ref[...] for ref in stats_refs]) / (HEAD_TOTAL * DH)
    inverse = lax.rsqrt(stats[0:1] + 1e-06)
    row_ref[...] = inverse
    columns(inverse, inverse_ref, blocks)
    columns(inverse * inverse * inverse * stats[1:2], factor_ref, blocks)

    for out, offset in ((send_ref, 0), (own_ref, half)):

        @pl.loop(0, half // GROUP)
        def _(g):
            places = [g * GROUP + at for at in range(GROUP)]
            heads_now = [lax.rem((1 - core) * half + offset + place, heads) for place in places]
            lanes = [head_lanes(head) for head in heads_now]
            gains = [gain_ref[:, lane] for lane in lanes]
            gain_sums = [jnp.zeros((8, DH), F32) for _ in places]
            grads = [[] for _ in places]
            for n in range(blocks):
                for at in range(GROUP):
                    attn = attn_ref[span(n), lanes[at]].astype(F32)
                    scaled = go_ref[span(n), lanes[at]].astype(F32) * inverse_ref[span(n), :]
                    gain_sums[at] += jnp.sum((scaled * attn).reshape(SPAN // 8, 8, DH), axis=0)
                    grad = (scaled * gains[at] - attn * factor_ref[span(n), :]).astype(BF16)
                    ga_ref[span(n), lanes[at]] = grad
                    grads[at].append(grad)
            states = [nn(turned_ref[heads_now[at]], jnp.concatenate(grads[at], axis=0)) for at in range(GROUP)]
            for at in range(GROUP):
                decay = jnp.exp(head_rows(total_ref, heads_now[at]))
                piece_store(out, places[at], states[at], extra_rows(decay, jnp.sum(gain_sums[at], axis=0, keepdims=True)))


def norm_backward(position, turned, attn, grad_out, gain, total, stats):
    rows, width = attn.shape
    heads = width // DH
    pieces = jax.ShapeDtypeStruct((heads // 2, PIECE, DH), F32)
    return pl.pallas_call(
        norm_body,
        in_specs=[SMEM] + [VMEM] * (5 + len(stats)),
        out_specs=[VMEM] * 4,
        out_shape=[jax.ShapeDtypeStruct((rows, width), BF16), pieces, pieces, jax.ShapeDtypeStruct((1, rows), F32)],
        scratch_shapes=[pltpu.VMEM((rows, DH), F32), pltpu.VMEM((rows, DH), F32)],
        compiler_params=params(12),
        cost_estimate=cost(2 * rows * width * DH, 8 * rows * width),
        name="norm_backward",
    )(position, turned, attn, grad_out, gain, total, *stats)


def grads_pair(heads, places, refs, out_ref, gq_ref, lk_ref, lv_ref, inverse_ref, both_masks):
    q_ref, k_ref, v_ref, ga_ref, attn_ref, gain_ref, _, low_ref, enter_ref, cum_ref, before_ref = refs
    mask, turned_mask = both_masks
    blocks = k_ref.shape[0] // SPAN
    each = range(len(heads))
    steps = [(a, n) for n in range(blocks) for a in each]
    lanes = [head_lanes(h) for h in heads]
    here = [head_lanes(p) for p in places]
    cums = [head_rows(cum_ref, h) for h in heads]
    mids = [middle_lane(c) for c in cums]
    ends = [last_lane(c) for c in cums]
    query_col = [jnp.exp(c - m).T for c, m in zip(cums, mids)]
    key_col = [jnp.exp(m - c).T for c, m in zip(cums, mids)]
    mid_scale, end_scale = [jnp.exp(m) for m in mids], [jnp.exp(e) for e in ends]
    rest_scale = [jnp.exp(e - m) for e, m in zip(ends, mids)]
    enter_scale = [jnp.exp(m + head_rows(before_ref, h)) for m, h in zip(mids, heads)]
    entering = [enter_ref[h].astype(F32) for h in heads]

    def at(ref, a, n):
        return ref[span(n), lanes[a]]

    q_up = {(a, n): (at(q_ref, a, n).astype(F32) * query_col[a][:, n : n + 1]).astype(BF16) for a, n in steps}
    updates = {(a, n): nn(q_up[a, n].T, at(ga_ref, a, n)) for a, n in steps if n > 0}
    k_up = {(a, n): (at(k_ref, a, n).astype(F32) * key_col[a][:, n : n + 1]).astype(BF16) for a, n in steps}
    states = {
        (a, n): (low_ref[heads[a], n].astype(F32) + enter_scale[a][n : n + 1] * entering[a]).astype(BF16)
        for a, n in steps
    }
    from_query = {
        (a, n): nt(at(ga_ref, a, n), jnp.concatenate([at(v_ref, a, n), states[a, n]], axis=0)) for a, n in steps
    }
    lows = {}
    for a in each:
        back = jnp.zeros((DH, DH), F32)
        for n in reversed(range(blocks)):
            lows[a, n] = (rest_scale[a][n : n + 1] * back).astype(BF16)
            if n > 0:
                back = end_scale[a][n : n + 1] * back + mid_scale[a][n : n + 1] * updates[a, n]
    turned_weights = {s: nt(k_up[s], q_up[s]) for s in steps}
    from_key = {
        (a, n): nt(at(v_ref, a, n), jnp.concatenate([at(ga_ref, a, n), lows[a, n]], axis=0)) for a, n in steps
    }
    scores = {s: jnp.where(mask, from_query[s][:, :SPAN], 0.0).astype(BF16) for s in steps}
    grad_q = {s: nn(scores[s], k_up[s]) + from_query[s][:, SPAN:] for s in steps}
    turned_weights = {s: jnp.where(turned_mask, turned_weights[s], 0.0).astype(BF16) for s in steps}
    grad_v = {
        (a, n): nn(
            jnp.concatenate([turned_weights[a, n], k_up[a, n]], axis=1),
            jnp.concatenate([at(ga_ref, a, n), lows[a, n]], axis=0),
        )
        for a, n in steps
    }
    turned_scores = {s: jnp.where(turned_mask, from_key[s][:, :SPAN], 0.0).astype(BF16) for s in steps}
    grad_k = {s: nn(turned_scores[s], q_up[s]) + from_key[s][:, SPAN:] for s in steps}
    for a, n in steps:
        gq_ref[span(n), here[a]] = (grad_q[a, n] * query_col[a][:, n : n + 1]).astype(BF16)
        lv_ref[span(n), lanes[a]] = grad_v[a, n].astype(BF16)
        lk_ref[span(n), lanes[a]] = (grad_k[a, n] * key_col[a][:, n : n + 1]).astype(BF16)
        normed = at(attn_ref, a, n).astype(F32) * inverse_ref[span(n), :]
        out_ref[span(n), here[a]] = (normed * gain_ref[:, lanes[a]]).astype(BF16)


def grads_body(first, count, chained, *refs):
    inputs = refs[1:12]
    refs = refs[12 + (4 if chained else 0) :]
    out_hbm, gq_hbm, lk_ref, lv_ref, out_ref, gq_ref, inverse_ref, sems = refs
    blocks = inputs[0].shape[0] // SPAN
    both_masks = masks()
    columns(inputs[6][...], inverse_ref, blocks)

    def copies(at):
        here, there = head_lanes(at * PAIR, PAIR), head_lanes(first + at * PAIR, PAIR)
        return [
            pltpu.make_async_copy(out_ref.at[:, here], out_hbm.at[:, there], sems.at[0, at]),
            pltpu.make_async_copy(gq_ref.at[:, here], gq_hbm.at[:, there], sems.at[1, at]),
        ]

    @pl.loop(0, count // PAIR)
    def _(at):
        places = [at * PAIR + a for a in range(PAIR)]
        heads = [first + p for p in places]
        grads_pair(heads, places, inputs, out_ref, gq_ref, lk_ref, lv_ref, inverse_ref, both_masks)
        for copy in copies(at):
            copy.start()

    @pl.loop(0, count // PAIR)
    def _(at):
        for copy in copies(at):
            copy.wait()


def grads_local(after, first, count, inputs, done):
    rows, width = inputs[0].shape
    like = jax.ShapeDtypeStruct((rows, width), BF16)
    kinds = [HBM, HBM, VMEM, VMEM]
    return pl.pallas_call(
        functools.partial(grads_body, first, count, bool(done)),
        in_specs=[ANY] + [VMEM] * 11 + (kinds if done else []),
        out_specs=kinds,
        out_shape=[like] * 4,
        input_output_aliases={12 + i: i for i in range(4)} if done else {},
        scratch_shapes=[
            pltpu.VMEM((rows, count * DH), BF16),
            pltpu.VMEM((rows, count * DH), BF16),
            pltpu.VMEM((rows, DH), F32),
            pltpu.SemaphoreType.DMA((2, count // PAIR)),
        ],
        compiler_params=params(16),
        cost_estimate=cost(22 * rows * count * DH * DH, 24 * rows * count * DH),
        name=f"grads_{first}",
    )(after, *inputs, *done)


def leave_body(position_ref, k_ref, v_ref, lk_ref, lv_ref, keep_ref, taken_ref, cum_ref, before_ref, total_ref,
               gk_hbm, gv_hbm, gg_ref, gk_ref, gv_ref, sems):
    rows, width = k_ref.shape
    heads, blocks = width // DH, rows // SPAN
    half = heads // 2
    core = position_ref[0]

    def copies(at):
        lanes = head_lanes(lax.rem(core * half + at * PAIR, heads), PAIR)
        return [
            pltpu.make_async_copy(gk_ref.at[:, lanes], gk_hbm.at[:, lanes], sems.at[0, at]),
            pltpu.make_async_copy(gv_ref.at[:, lanes], gv_hbm.at[:, lanes], sems.at[1, at]),
        ]

    @pl.loop(0, heads // PAIR)
    def _(at):
        first = lax.rem(core * half + at * PAIR, heads)
        lanes = [head_lanes(first + a) for a in range(PAIR)]
        lows = [piece_state(keep_ref, taken_ref, at * PAIR + a, half).astype(BF16) for a in range(PAIR)]
        from_v = [nt(v_ref[:, lanes[a]], lows[a]) for a in range(PAIR)]
        from_k = [nn(k_ref[:, lanes[a]], lows[a]) for a in range(PAIR)]
        scales = [
            jnp.exp(
                head_rows(total_ref, first + a) - head_rows(before_ref, first + a) - head_rows(cum_ref, first + a)
            ).T
            for a in range(PAIR)
        ]
        for n in range(blocks):
            for a in range(PAIR):
                factor = scales[a][:, n : n + 1]
                grad_k = lk_ref[span(n), lanes[a]].astype(F32) + factor * from_v[a][span(n)]
                grad_v = lv_ref[span(n), lanes[a]].astype(F32) + factor * from_k[a][span(n)]
                gk_ref[span(n), lanes[a]] = grad_k.astype(BF16)
                gv_ref[span(n), lanes[a]] = grad_v.astype(BF16)
        for copy in copies(at):
            copy.start()
        kept = at * PAIR < half
        for a in range(PAIR):
            place = jnp.where(kept, at * PAIR + a, at * PAIR + a - half)
            row = slice(DH + 1, DH + 2)
            gg_ref[:, lanes[a]] = jnp.where(kept, keep_ref[place, row, :], taken_ref[place, row, :])

    @pl.loop(0, heads // PAIR)
    def _(at):
        for copy in copies(at):
            copy.wait()


def grads_leaving(position, keys, values, local_k, local_v, keep, taken, cum, before, total):
    rows, width = keys.shape
    like = jax.ShapeDtypeStruct((rows, width), BF16)
    return pl.pallas_call(
        leave_body,
        in_specs=[SMEM] + [VMEM] * 9,
        out_specs=[HBM, HBM, VMEM],
        out_shape=[like, like, jax.ShapeDtypeStruct((1, width), F32)],
        scratch_shapes=[
            pltpu.VMEM((rows, width), BF16),
            pltpu.VMEM((rows, width), BF16),
            pltpu.SemaphoreType.DMA((2, width // DH // PAIR)),
        ],
        compiler_params=params(16),
        cost_estimate=cost(4 * rows * width * DH, 12 * rows * width),
        name="grads_leaving",
    )(position, keys, values, local_k, local_v, keep, taken, cum, before, total)


def per_device(queries, keys, values, log_decay, gain, grad_out):
    place = lax.axis_index("seq")
    position = jnp.stack([place % 2, place // 2 % ALONG_Z, place // (2 * ALONG_Z)]).astype(jnp.int32)
    gain_row = gain.reshape(1, -1)
    keys, values, queries, grad_out = (
        pltpu.with_memory_space_constraint(a, pltpu.HBM) for a in (keys, values, queries, grad_out)
    )
    send, own, cum, before, total, keys, values = local_state(position, log_decay, keys, values)

    def attend_part(first, count, load):
        def run(after, done):
            held = done[3] if done else queries
            more = done[4:] if done else ()
            outs = attend(after, first, count, load, keys, values, cum, before, held, grad_out, done[:3])
            if load == "queries":
                return (*outs[:3], outs[3], outs[0])
            if load == "grad_out":
                return (*outs[:3], held, outs[3])
            return (*outs[:3], held, more[0])

        return run

    keep, taken, (local, lows, turned, queries, grad_out) = scan_over_seq(
        send, own, position, False, [attend_part(0, 6, "queries"), attend_part(6, 6, "grad_out"), attend_part(12, 4, None)]
    )
    attn, entering, stats = attend_entering(
        position, queries, local, grad_out, gain_row, keep, taken, cum, before
    )
    count = lax.axis_size("head")
    stats = [stats] + [
        lax.ppermute(stats, "head", [(i, (i + s) % count) for i in range(count)]) for s in range(1, count)
    ]
    grad_attn, send, own, inverse = norm_backward(position, turned, attn, grad_out, gain_row, total, stats)
    inputs = (queries, keys, values, grad_attn, attn, gain_row, inverse, lows, entering, cum, before)

    def grads_part(first, count):
        return lambda after, done: grads_local(after, first, count, inputs, done)

    keep, taken, (output, grad_q, local_k, local_v) = scan_over_seq(
        send, own, position, True, [grads_part(0, 6), grads_part(6, 6), grads_part(12, 4)]
    )
    grad_k, grad_v, grad_gain = grads_leaving(
        position, keys, values, local_k, local_v, keep, taken, cum, before, total
    )
    return output, grad_q, grad_k, grad_v, grad_gain.reshape(-1)


def solution(mesh):
    tokens, heads = P("seq", "head"), P("head")
    return jax.shard_map(
        per_device,
        mesh=mesh,
        in_specs=(tokens, tokens, tokens, P("head", "seq"), heads, tokens),
        out_specs=(tokens, tokens, tokens, tokens, heads),
        check_vma=False,
    )
```

```python
import functools

import jax
import jax.numpy as jnp
from jax import lax
from jax.experimental import pallas as pl
from jax.experimental.pallas import tpu as pltpu
from jax.sharding import PartitionSpec as P

HEAD_TOTAL = 64
DH = 128
SPAN = 128
ROWS = 8
PIECE = DH + ROWS
GROUP = 4
PAIR = 2
ALONG_X, ALONG_Z = 4, 4
F32 = jnp.float32
BF16 = jnp.bfloat16
EXACT = lax.Precision.HIGHEST
VMEM = pl.BlockSpec(memory_space=pltpu.VMEM)
SMEM = pl.BlockSpec(memory_space=pltpu.SMEM)
HBM = pl.BlockSpec(memory_space=pltpu.HBM)
ANY = pl.BlockSpec(memory_space=pl.ANY)


def dot(a, b, contract, precision=None):
    return lax.dot_general(
        a, b, ((contract[:1], contract[1:]), ((), ())), precision=precision, preferred_element_type=F32
    )


def nn(a, b):
    return dot(a, b, (1, 0))


def nt(a, b):
    return dot(a, b, (1, 1))


def params(mib):
    return pltpu.CompilerParams(vmem_limit_bytes=mib * 1024 * 1024)


def cost(flops, nbytes):
    return pl.CostEstimate(flops=int(flops), bytes_accessed=int(nbytes), transcendentals=0)


def head_rows(ref, head):
    return ref[pl.ds(pl.multiple_of(head * ROWS, ROWS), ROWS), :]


def head_lanes(head, count=1):
    return pl.ds(pl.multiple_of(head * DH, DH), count * DH)


def span(n):
    return slice(n * SPAN, (n + 1) * SPAN)


def last_lane(rows):
    return jnp.broadcast_to(rows[:, SPAN - 1 :], rows.shape)


def middle_lane(rows):
    return jnp.broadcast_to(rows[:, SPAN // 2 - 1 : SPAN // 2], rows.shape)


def masks():
    i = lax.broadcasted_iota(jnp.int32, (SPAN, SPAN), 0)
    j = lax.broadcasted_iota(jnp.int32, (SPAN, SPAN), 1)
    return i >= j, i <= j


def join_rows(rows, blocks):
    return jnp.concatenate([rows[n : n + 1] for n in range(blocks)], axis=1)


def piece_store(ref, at, state, extra):
    ref[at, :DH, :] = state
    ref[at, DH:, :] = extra


def extra_rows(decay, gain_row=None):
    place = lax.broadcasted_iota(jnp.int32, (ROWS, DH), 0)
    rest = 0.0 if gain_row is None else jnp.where(place == 1, gain_row, 0.0)
    return jnp.where(place == 0, decay, rest)


def half_heads(position_ref, of_other, at, heads):
    half = heads // 2
    start = (1 - position_ref[0]) if of_other else position_ref[0]
    return start * half + at


def decay_tables(log_ref, cum_ref, before_ref, total_ref):
    heads, rows = log_ref.shape
    _, triangle = masks()
    triangle = triangle.astype(F32)
    cum_ref[...] = jnp.zeros_like(cum_ref)
    before_ref[...] = jnp.zeros_like(before_ref)
    before = jnp.zeros((heads, SPAN), F32)
    for n in range(rows // SPAN):
        cum = dot(log_ref[:, span(n)], triangle, (1, 0), EXACT)
        for h in range(heads):
            cum_ref[h * ROWS + n : h * ROWS + n + 1, :] = cum[h : h + 1]
            before_ref[h * ROWS + n : h * ROWS + n + 1, :] = before[h : h + 1]
        before = before + last_lane(cum)
    for h in range(heads):
        total_ref[h * ROWS : (h + 1) * ROWS, :] = jnp.broadcast_to(before[h : h + 1], (ROWS, SPAN))


def state_body(of_other, position_ref, *refs):
    if of_other:
        k_hbm, v_hbm, log_hbm, out_ref, k_ref, v_ref, cum_ref, before_ref, total_ref, sems, log_ref, log_sem = refs
    else:
        k_ref, v_ref, cum_ref, before_ref, total_ref, out_ref = refs
    rows, width = k_ref.shape
    heads, blocks = width // DH, rows // SPAN
    copies = []
    if of_other:
        log_copy = pltpu.make_async_copy(log_hbm, log_ref, log_sem)
        log_copy.start()
        for g in range(heads // GROUP):
            lanes = head_lanes(lax.rem(half_heads(position_ref, True, g * GROUP, heads), heads), GROUP)
            for which, (source, target) in enumerate(((k_hbm, k_ref), (v_hbm, v_ref))):
                copies.append(pltpu.make_async_copy(source.at[:, lanes], target.at[:, lanes], sems.at[which, g]))
                copies[-1].start()
        log_copy.wait()
        decay_tables(log_ref, cum_ref, before_ref, total_ref)

    for g in range(heads // 2 // GROUP):
        first = half_heads(position_ref, of_other, g * GROUP, heads)
        if of_other:
            copies[2 * g].wait()
            copies[2 * g + 1].wait()
        totals = [head_rows(total_ref, first + at) for at in range(GROUP)]
        scales = [
            jnp.exp(totals[at] - head_rows(before_ref, first + at) - head_rows(cum_ref, first + at)) for at in range(GROUP)
        ]
        decayed = [
            (k_ref[:, head_lanes(first + at)].T.astype(F32) * join_rows(scales[at], blocks)).astype(BF16)
            for at in range(GROUP)
        ]
        states = [nn(decayed[at], v_ref[:, head_lanes(first + at)]) for at in range(GROUP)]
        for at in range(GROUP):
            piece_store(out_ref, g * GROUP + at, states[at], extra_rows(jnp.exp(totals[at])))
    for copy in copies[heads // GROUP :]:
        copy.wait()


def local_state(of_other, position, keys, values, more):
    rows, width = keys.shape
    heads = width // DH
    pieces = jax.ShapeDtypeStruct((heads // 2, PIECE, DH), F32)
    table = jax.ShapeDtypeStruct((heads * ROWS, SPAN), F32)
    like = jax.ShapeDtypeStruct(keys.shape, BF16)
    if of_other:
        specs, outs = [HBM] * 3, [pieces, like, like, table, table, table]
        scratch = [
            pltpu.SemaphoreType.DMA((2, heads // GROUP)),
            pltpu.VMEM(more[0].shape, F32),
            pltpu.SemaphoreType.DMA,
        ]
    else:
        specs, outs, scratch = [VMEM] * 5, [pieces], []
    return pl.pallas_call(
        functools.partial(state_body, of_other),
        in_specs=[SMEM] + specs,
        out_specs=[VMEM] * len(outs),
        out_shape=outs,
        scratch_shapes=scratch,
        compiler_params=params(4),
        cost_estimate=cost(heads * rows * DH * DH, 2 * rows * heads * DH),
        name="state_given" if of_other else "state_kept",
    )(position, keys, values, *more)


def first_row():
    return lax.broadcasted_iota(jnp.int32, (ROWS, DH), 0) == 0


def join_extra(a, b):
    return jnp.where(first_row(), a * b, a + b)


def cores_body(reverse, position_ref, own_ref, got_ref, *out_refs):
    z = position_ref[1]
    near_here = (position_ref[0] == 0) != reverse
    each = own_ref.shape[0] // ALONG_Z
    for shift, out_ref in enumerate(out_refs):
        for j in range(each):
            head = lax.rem(z + shift, ALONG_Z) * each + j
            own, got = own_ref[head], got_ref[head]
            near, far = jnp.where(near_here, own, got), jnp.where(near_here, got, own)
            piece_store(out_ref, j, far[DH : DH + 1] * near[:DH] + far[:DH], join_extra(near[DH:], far[DH:]))


def along_z_body(reverse, position_ref, *refs):
    in_refs, (_, total_ref, prefix_ref, slots) = refs[:ALONG_Z], refs[ALONG_Z:]
    z = position_ref[1]
    for shift, ref in enumerate(in_refs):
        slots[lax.rem(z - shift + ALONG_Z, ALONG_Z)] = ref[...]
    for j in range(total_ref.shape[0]):
        state = jnp.zeros((DH, DH), F32)
        extra = jnp.where(first_row(), 1.0, 0.0)
        for lap in range(ALONG_Z):
            at = ALONG_Z - 1 - lap if reverse else lap
            prefix_ref[at, j, :DH, :] = state
            prefix_ref[at, j, DH:, :] = extra
            state = slots[at, j, DH : DH + 1, :] * state + slots[at, j, :DH, :]
            extra = join_extra(extra, slots[at, j, DH:, :])
        piece_store(total_ref, j, state, extra)


def along_x_body(reverse, position_ref, *refs):
    in_refs, prefix_ref, out_refs, slots = refs[:ALONG_X], refs[ALONG_X], refs[ALONG_X + 2 : -1], refs[-1]
    z, x = position_ref[1], position_ref[2]
    for shift, ref in enumerate(in_refs):
        slots[lax.rem(x - shift + ALONG_X, ALONG_X)] = ref[...]
    for j in range(prefix_ref.shape[1]):
        state = jnp.zeros((DH, DH), F32)
        extra = jnp.zeros((ROWS, DH), F32)
        for lap in range(ALONG_X):
            at = ALONG_X - 1 - lap if reverse else lap
            taken = (at > x) if reverse else (at < x)
            state = jnp.where(taken, slots[at, j, DH : DH + 1, :] * state + slots[at, j, :DH, :], state)
            extra = extra + slots[at, j, DH:, :]
        for shift, out_ref in enumerate(out_refs):
            at = lax.rem(z + shift, ALONG_Z)
            piece_store(out_ref, j, prefix_ref[at, j, :DH, :] + prefix_ref[at, j, DH : DH + 1, :] * state, extra)


def entering_body(reverse, position_ref, *refs):
    in_refs, (own_ref, got_ref, _, keep_ref, give_ref) = refs[:ALONG_Z], refs[ALONG_Z:]
    z = position_ref[1]
    near_here = (position_ref[0] == 0) != reverse
    each = own_ref.shape[0] // ALONG_Z
    for shift, ref in enumerate(in_refs):
        for j in range(each):
            head = lax.rem(z - shift + ALONG_Z, ALONG_Z) * each + j
            near = jnp.where(near_here, own_ref[head], got_ref[head])
            entering, extra = ref[j, :DH, :], ref[j, DH:, :]
            passed = near[DH : DH + 1] * entering + near[:DH]
            piece_store(keep_ref, head, jnp.where(near_here, entering, passed), extra)
            piece_store(give_ref, head, jnp.where(near_here, passed, entering), extra)


def scan_step(body, name, reverse, position, arrays, after, out_counts, scratch):
    shapes = [jax.ShapeDtypeStruct(shape, F32) for shape in out_counts]
    afters = [] if after is None else [after]
    return pl.pallas_call(
        functools.partial(body, reverse),
        in_specs=[SMEM] + [VMEM] * len(arrays) + [ANY] * len(afters),
        out_specs=[VMEM] * len(shapes),
        out_shape=shapes,
        scratch_shapes=scratch,
        compiler_params=params(3),
        cost_estimate=cost(10**6, 10**6),
        name=name,
    )(position, *arrays, *afters)


def scan_over_seq(send, own, position, reverse, works):
    count = lax.axis_size("seq")
    heads = own.shape[0]
    each = heads // ALONG_Z

    def index(x, z, c):
        return (x % ALONG_X * ALONG_Z + z % ALONG_Z) * 2 + c

    every = [(x, z, c) for x in range(ALONG_X) for z in range(ALONG_Z) for c in range(2)]
    across = [(i, i ^ 1) for i in range(count)]
    by_z = [[(index(x, z, c), index(x, z + s, c)) for x, z, c in every] for s in range(ALONG_Z)]
    by_x = [[(index(x, z, c), index(x + s, z, c)) for x, z, c in every] for s in range(ALONG_X)]
    piece = (each, PIECE, DH)

    got = lax.ppermute(send, "seq", across)
    parts = scan_step(cores_body, "join_cores", reverse, position, [own, got], None, [piece] * ALONG_Z, [])
    arrived = [parts[0]] + [lax.ppermute(parts[s], "seq", by_z[s]) for s in range(1, ALONG_Z)]
    done = works[0](parts[0], ())
    total, prefix = scan_step(
        along_z_body, "join_z", reverse, position, arrived, done[-1],
        [piece, (ALONG_Z,) + piece], [pltpu.VMEM((ALONG_Z,) + piece, F32)],
    )
    totals = [total] + [lax.ppermute(total, "seq", by_x[s]) for s in range(1, ALONG_X)]
    done = works[1](total, done)
    parts = scan_step(
        along_x_body, "join_x", reverse, position, totals + [prefix], done[-1],
        [piece] * ALONG_Z, [pltpu.VMEM((ALONG_X,) + piece, F32)],
    )
    arrived = [parts[0]] + [lax.ppermute(parts[s], "seq", by_z[s]) for s in range(1, ALONG_Z)]
    done = works[2](parts[0], done)
    keep, give = scan_step(
        entering_body, "entering", reverse, position, arrived + [own, got], done[-1], [own.shape] * 2, []
    )
    return keep, lax.ppermute(give, "seq", across), done


def attend_pair(heads, q_ref, k_ref, v_ref, cum_ref, outs, both_masks):
    local_ref, low_ref, turned_ref, qs_ref, ks_ref, vs_ref, weights_ref = outs
    mask, turned_mask = both_masks
    blocks = k_ref.shape[0] // SPAN
    each = range(len(heads))
    steps = [(a, n) for n in range(blocks) for a in each]
    lanes = [head_lanes(h) for h in heads]
    cums = [head_rows(cum_ref, h) for h in heads]
    mids = [middle_lane(c) for c in cums]
    ends = [last_lane(c) for c in cums]
    query_col = [jnp.exp(c - m).T for c, m in zip(cums, mids)]
    key_col = [jnp.exp(m - c).T for c, m in zip(cums, mids)]
    mid_scale, end_scale = [jnp.exp(m) for m in mids], [jnp.exp(e) for e in ends]
    rest_scale = [jnp.exp(e - m) for e, m in zip(ends, mids)]
    q_up = {(a, n): (q_ref[span(n), lanes[a]].astype(F32) * query_col[a][:, n : n + 1]).astype(BF16) for a, n in steps}
    k_up = {(a, n): (k_ref[span(n), lanes[a]].astype(F32) * key_col[a][:, n : n + 1]).astype(BF16) for a, n in steps}
    v_up = {(a, n): (v_ref[span(n), lanes[a]].astype(F32) * key_col[a][:, n : n + 1]).astype(BF16) for a, n in steps}
    scores = {s: nt(q_up[s], k_up[s]) for s in steps}
    updates = {(a, n): nn(k_up[a, n].T, v_ref[span(n), lanes[a]]) for a, n in steps if n < blocks - 1}
    weights = {s: jnp.where(mask, scores[s], 0.0).astype(BF16) for s in steps}
    lows = {}
    for a in each:
        state = jnp.zeros((DH, DH), F32)
        for n in range(blocks):
            lows[a, n] = (mid_scale[a][n : n + 1] * state).astype(BF16)
            low_ref[heads[a], n] = lows[a, n]
            if n < blocks - 1:
                state = end_scale[a][n : n + 1] * state + rest_scale[a][n : n + 1] * updates[a, n]
    totals = {
        (a, n): nn(
            jnp.concatenate([weights[a, n], q_up[a, n]], axis=1),
            jnp.concatenate([v_ref[span(n), lanes[a]], lows[a, n]], axis=0),
        )
        for a, n in steps
    }
    turned_weights = {s: nt(k_up[s], q_up[s]) for s in steps}
    for a, n in steps:
        local_ref[span(n), lanes[a]] = totals[a, n].astype(BF16)
        qs_ref[span(n), lanes[a]] = q_up[a, n]
        ks_ref[span(n), lanes[a]] = k_up[a, n]
        vs_ref[span(n), lanes[a]] = v_up[a, n]
        weights_ref[heads[a], n] = jnp.where(turned_mask, turned_weights[a, n], 0.0).astype(BF16)
    for a in each:
        turned_ref[heads[a]] = jnp.concatenate([q_up[a, n].T for n in range(blocks)], axis=1)


def attend_body(first, count, load, *refs):
    k_ref, v_ref, cum_ref = refs[1:4]
    refs = refs[4:]
    copies = []
    if load == "queries":
        q_hbm, outs, (q_ref, sems) = refs[0], refs[1:8], refs[8:]
        for g in range(q_hbm.shape[1] // (GROUP * DH)):
            lanes = slice(g * GROUP * DH, (g + 1) * GROUP * DH)
            copies.append(pltpu.make_async_copy(q_hbm.at[:, lanes], q_ref.at[:, lanes], sems.at[g]))
    elif load == "grad_out":
        q_ref, go_hbm, outs, (go_ref, sems) = refs[0], refs[1], refs[9:16], refs[16:]
        copies.append(pltpu.make_async_copy(go_hbm, go_ref, sems.at[0]))
    else:
        q_ref, outs = refs[0], refs[8:15]
    for copy in copies:
        copy.start()
    both_masks = masks()

    def pairs(start, stop):
        @pl.loop(start // PAIR, stop // PAIR)
        def _(at):
            heads = [at * PAIR + a for a in range(PAIR)]
            attend_pair(heads, q_ref, k_ref, v_ref, cum_ref, outs, both_masks)

    if load == "queries":
        for g, copy in enumerate(copies):
            copy.wait()
            if g * GROUP < count:
                pairs(g * GROUP, min((g + 1) * GROUP, count))
    else:
        pairs(first, first + count)
        for copy in copies:
            copy.wait()


def attend(after, first, count, load, keys, values, cum, queries, grad_out, done):
    rows, width = keys.shape
    heads, blocks = width // DH, rows // SPAN
    like = jax.ShapeDtypeStruct((rows, width), BF16)
    squares = jax.ShapeDtypeStruct((heads, blocks, DH, DH), BF16)
    outs = [like, squares, jax.ShapeDtypeStruct((heads, DH, rows), BF16), like, like, like, squares]
    arrays, specs = [after, keys, values, cum, queries], [ANY, VMEM, VMEM, VMEM]
    specs.append(HBM if load == "queries" else VMEM)
    if load == "grad_out":
        arrays.append(grad_out)
        specs.append(HBM)
    aliases = {len(arrays) + i: i for i in range(len(done))}
    if load is not None:
        outs.append(like)
    return pl.pallas_call(
        functools.partial(attend_body, first, count, load),
        in_specs=specs + [VMEM] * len(done),
        out_specs=[VMEM] * len(outs),
        out_shape=outs,
        input_output_aliases=aliases,
        scratch_shapes=[] if load is None else [pltpu.SemaphoreType.DMA((heads // GROUP,))],
        compiler_params=params(6),
        cost_estimate=cost(10 * rows * count * DH * DH, 12 * rows * count * DH),
        name=f"attend_{first}",
    )(*arrays, *done)


def enter_body(of_other, position_ref, q_ref, local_ref, go_ref, gain_ref, state_ref, cum_ref, before_ref, *refs):
    if of_other:
        attn_ref, low_ref, stats_ref, square_ref, inner_ref = refs[4:]
    else:
        attn_ref, low_ref, square_ref, inner_ref = refs
    rows, width = q_ref.shape
    heads, blocks = width // DH, rows // SPAN
    if not of_other:
        square_ref[...] = jnp.zeros_like(square_ref)
        inner_ref[...] = jnp.zeros_like(inner_ref)

    @pl.loop(0, heads // 2 // GROUP)
    def _(g):
        first = half_heads(position_ref, of_other, g * GROUP, heads)
        lanes = [head_lanes(first + at) for at in range(GROUP)]
        carried, scales, gains = [], [], []
        for at in range(GROUP):
            low = state_ref[g * GROUP + at, :DH, :].astype(BF16)
            low_ref[first + at] = low
            carried.append(nn(q_ref[:, lanes[at]], low))
            scales.append(jnp.exp(middle_lane(head_rows(cum_ref, first + at)) + head_rows(before_ref, first + at)))
            gains.append(gain_ref[:, lanes[at]])
        for n in range(blocks):
            square = square_ref[span(n), :]
            inner = inner_ref[span(n), :]
            for at in range(GROUP):
                entered = carried[at][span(n)] * scales[at][n : n + 1]
                attn = (local_ref[span(n), lanes[at]].astype(F32) + entered).astype(BF16)
                attn_ref[span(n), lanes[at]] = attn
                attn = attn.astype(F32)
                square += attn * attn
                inner += go_ref[span(n), lanes[at]].astype(F32) * gains[at] * attn
            square_ref[span(n), :] = square
            inner_ref[span(n), :] = inner

    if of_other:
        ones = jnp.ones((8, DH), F32)
        stats_ref[0:1, :] = dot(ones, square_ref[...], (1, 1), EXACT)[0:1]
        stats_ref[1:2, :] = dot(ones, inner_ref[...], (1, 1), EXACT)[0:1]


def attend_entering(of_other, position, queries, local, grad_out, gain, state, cum, before, done):
    rows, width = queries.shape
    heads = width // DH
    sums = jax.ShapeDtypeStruct((rows, DH), F32)
    outs = [jax.ShapeDtypeStruct((rows, width), BF16), jax.ShapeDtypeStruct((heads, DH, DH), BF16)]
    if of_other:
        outs, aliases = outs + [jax.ShapeDtypeStruct((2, rows), F32), sums, sums], {8: 0, 9: 1, 10: 3, 11: 4}
    else:
        outs, aliases = outs + [sums, sums], {}
    return pl.pallas_call(
        functools.partial(enter_body, of_other),
        in_specs=[SMEM] + [VMEM] * (7 + len(done)),
        out_specs=[VMEM] * len(outs),
        out_shape=outs,
        input_output_aliases=aliases,
        compiler_params=params(4),
        cost_estimate=cost(rows * width * DH, 4 * rows * width),
        name="enter_taken" if of_other else "enter_kept",
    )(position, queries, local, grad_out, gain, state, cum, before, *done)


def columns(row, ref, blocks):
    for n in range(blocks):
        ref[span(n), :] = jnp.broadcast_to(row[:, span(n)], (SPAN, SPAN)).T


def norm_body(of_other, position_ref, turned_ref, attn_ref, go_ref, gain_ref, cum_ref, before_ref, total_ref, *refs):
    rows, width = attn_ref.shape
    heads, blocks = width // DH, rows // SPAN
    if of_other:
        stats_refs, (ga_ref, out_ref, inverse_ref, factor_ref) = refs[:-4], refs[-4:]
        stats = functools.reduce(jnp.add, [ref[...] for ref in stats_refs]) / (HEAD_TOTAL * DH)
        inverse = lax.rsqrt(stats[0:1] + 1e-06)
        columns(inverse, inverse_ref, blocks)
        columns(inverse * inverse * inverse * stats[1:2], factor_ref, blocks)
    else:
        inverse_ref, factor_ref, _, ga_ref, out_ref = refs

    @pl.loop(0, heads // 2 // GROUP)
    def _(g):
        places = [g * GROUP + at for at in range(GROUP)]
        heads_now = [half_heads(position_ref, of_other, place, heads) for place in places]
        lanes = [head_lanes(head) for head in heads_now]
        gains = [gain_ref[:, lane] for lane in lanes]
        gain_sums = [jnp.zeros((8, DH), F32) for _ in places]
        grads = [[] for _ in places]
        for n in range(blocks):
            for at in range(GROUP):
                attn = attn_ref[span(n), lanes[at]].astype(F32)
                scaled = go_ref[span(n), lanes[at]].astype(F32) * inverse_ref[span(n), :]
                gain_sums[at] += jnp.sum((scaled * attn).reshape(SPAN // 8, 8, DH), axis=0)
                grad = (scaled * gains[at] - attn * factor_ref[span(n), :]).astype(BF16)
                ga_ref[span(n), lanes[at]] = grad
                grads[at].append(grad)
        updates = [
            [nn(turned_ref[heads_now[at], :, span(n)], grads[at][n]) for n in range(blocks)] for at in range(GROUP)
        ]
        scales = [jnp.exp(middle_lane(head_rows(cum_ref, h)) + head_rows(before_ref, h)) for h in heads_now]
        states = [sum(scales[at][n : n + 1] * updates[at][n] for n in range(blocks)) for at in range(GROUP)]
        for at in range(GROUP):
            decay = jnp.exp(head_rows(total_ref, heads_now[at]))
            piece_store(out_ref, places[at], states[at], extra_rows(decay, jnp.sum(gain_sums[at], axis=0, keepdims=True)))


def norm_backward(of_other, position, turned, attn, grad_out, gain, cum, before, total, more):
    rows, width = attn.shape
    heads = width // DH
    pieces = jax.ShapeDtypeStruct((heads // 2, PIECE, DH), F32)
    cols = jax.ShapeDtypeStruct((rows, DH), F32)
    outs = [jax.ShapeDtypeStruct((rows, width), BF16), pieces] + ([cols, cols] if of_other else [])
    return pl.pallas_call(
        functools.partial(norm_body, of_other),
        in_specs=[SMEM] + [VMEM] * (7 + len(more)),
        out_specs=[VMEM] * len(outs),
        out_shape=outs,
        input_output_aliases={} if of_other else {10: 0},
        compiler_params=params(5),
        cost_estimate=cost(rows * width * DH, 4 * rows * width),
        name="norm_given" if of_other else "norm_kept",
    )(position, turned, attn, grad_out, gain, cum, before, total, *more)


def grads_pair(heads, places, refs, out_ref, gq_ref, lk_ref, lv_ref, both_masks):
    q_ref, k_ref, turned_ref, ks_ref, vs_ref, weights_ref, ga_ref, attn_ref = refs[:8]
    gain_ref, inverse_ref, low_ref, enter_ref, cum_ref, before_ref = refs[8:]
    mask, _ = both_masks
    blocks = k_ref.shape[0] // SPAN
    each = range(len(heads))
    steps = [(a, n) for n in range(blocks) for a in each]
    lanes = [head_lanes(h) for h in heads]
    here = [head_lanes(p) for p in places]
    cums = [head_rows(cum_ref, h) for h in heads]
    mids = [middle_lane(c) for c in cums]
    ends = [last_lane(c) for c in cums]
    query_col = [jnp.exp(c - m).T for c, m in zip(cums, mids)]
    mid_scale, end_scale = [jnp.exp(m) for m in mids], [jnp.exp(e) for e in ends]
    rest_scale = [jnp.exp(e - m) for e, m in zip(ends, mids)]
    enter_scale = [jnp.exp(m + head_rows(before_ref, h)) for m, h in zip(mids, heads)]
    entering = [enter_ref[h].astype(F32) for h in heads]

    def at(ref, a, n):
        return ref[span(n), lanes[a]]

    updates = {(a, n): nn(turned_ref[heads[a], :, span(n)], at(ga_ref, a, n)) for a, n in steps if n > 0}
    ga_up = {(a, n): (at(ga_ref, a, n).astype(F32) * query_col[a][:, n : n + 1]).astype(BF16) for a, n in steps}
    states = {
        (a, n): (low_ref[heads[a], n].astype(F32) + enter_scale[a][n : n + 1] * entering[a]).astype(BF16)
        for a, n in steps
    }
    from_query = {
        (a, n): nt(ga_up[a, n], jnp.concatenate([at(vs_ref, a, n), states[a, n]], axis=0)) for a, n in steps
    }
    lows = {}
    for a in each:
        back = jnp.zeros((DH, DH), F32)
        for n in reversed(range(blocks)):
            lows[a, n] = (rest_scale[a][n : n + 1] * back).astype(BF16)
            if n > 0:
                back = end_scale[a][n : n + 1] * back + mid_scale[a][n : n + 1] * updates[a, n]
    scores = {s: jnp.where(mask, from_query[s][:, :SPAN], 0.0).astype(BF16) for s in steps}
    from_key = {(a, n): nt(at(vs_ref, a, n), lows[a, n]) for a, n in steps}
    grad_v = {
        (a, n): nn(
            jnp.concatenate([weights_ref[heads[a], n], at(ks_ref, a, n)], axis=1),
            jnp.concatenate([at(ga_ref, a, n), lows[a, n]], axis=0),
        )
        for a, n in steps
    }
    grad_q = {(a, n): nn(scores[a, n], at(k_ref, a, n)) + from_query[a, n][:, SPAN:] for a, n in steps}
    grad_k = {(a, n): nn(scores[a, n].T, at(q_ref, a, n)) + from_key[a, n] for a, n in steps}
    for a, n in steps:
        gq_ref[span(n), here[a]] = grad_q[a, n].astype(BF16)
        lv_ref[span(n), lanes[a]] = grad_v[a, n].astype(BF16)
        lk_ref[span(n), lanes[a]] = grad_k[a, n].astype(BF16)
        normed = at(attn_ref, a, n).astype(F32) * inverse_ref[span(n), :]
        out_ref[span(n), here[a]] = (normed * gain_ref[:, lanes[a]]).astype(BF16)


def grads_body(first, count, chained, *refs):
    inputs = refs[1:15]
    refs = refs[15 + (4 if chained else 0) :]
    out_hbm, gq_hbm, lk_ref, lv_ref, out_ref, gq_ref, sems = refs
    both_masks = masks()

    def copies(at):
        here, there = head_lanes(at * PAIR, PAIR), head_lanes(first + at * PAIR, PAIR)
        return [
            pltpu.make_async_copy(out_ref.at[:, here], out_hbm.at[:, there], sems.at[0, at]),
            pltpu.make_async_copy(gq_ref.at[:, here], gq_hbm.at[:, there], sems.at[1, at]),
        ]

    @pl.loop(0, count // PAIR)
    def _(at):
        places = [at * PAIR + a for a in range(PAIR)]
        heads = [first + p for p in places]
        grads_pair(heads, places, inputs, out_ref, gq_ref, lk_ref, lv_ref, both_masks)
        for copy in copies(at):
            copy.start()

    @pl.loop(0, count // PAIR)
    def _(at):
        for copy in copies(at):
            copy.wait()


def grads_local(after, first, count, inputs, done):
    rows, width = inputs[0].shape
    like = jax.ShapeDtypeStruct((rows, width), BF16)
    kinds = [HBM, HBM, VMEM, VMEM]
    return pl.pallas_call(
        functools.partial(grads_body, first, count, bool(done)),
        in_specs=[ANY] + [VMEM] * 14 + (kinds if done else []),
        out_specs=kinds,
        out_shape=[like] * 4,
        input_output_aliases={15 + i: i for i in range(4)} if done else {},
        scratch_shapes=[
            pltpu.VMEM((rows, count * DH), BF16),
            pltpu.VMEM((rows, count * DH), BF16),
            pltpu.SemaphoreType.DMA((2, count // PAIR)),
        ],
        compiler_params=params(8),
        cost_estimate=cost(22 * rows * count * DH * DH, 24 * rows * count * DH),
        name=f"grads_{first}",
    )(after, *inputs, *done)


def leave_body(of_other, position_ref, k_ref, v_ref, lk_ref, lv_ref, state_ref, cum_ref, before_ref, total_ref, *refs):
    rows, width = k_ref.shape
    heads, blocks = width // DH, rows // SPAN
    half = heads // 2
    copies = []
    if of_other:
        kept_k_ref, kept_v_ref, kept_gain_ref, gk_hbm, gv_hbm, gg_ref, gk_ref, gv_ref, sems, kept_sems = refs
        there = head_lanes(half_heads(position_ref, False, 0, heads), half)
        for which, (source, target) in enumerate(((kept_k_ref, gk_hbm), (kept_v_ref, gv_hbm))):
            copies.append(pltpu.make_async_copy(source, target.at[:, there], kept_sems.at[which]))
            copies[-1].start()
        gg_ref[...] = kept_gain_ref[...]
    else:
        gk_ref, gv_ref, gg_ref = refs
    for g in range(half // GROUP):

        @pl.loop(g * GROUP // PAIR, (g + 1) * GROUP // PAIR)
        def _(at):
            first = half_heads(position_ref, of_other, at * PAIR, heads)
            lanes = [head_lanes(first + a) for a in range(PAIR)]
            here = [head_lanes(at * PAIR + a) for a in range(PAIR)]
            lows = [state_ref[at * PAIR + a, :DH, :].astype(BF16) for a in range(PAIR)]
            from_v = [nt(v_ref[:, lanes[a]], lows[a]) for a in range(PAIR)]
            from_k = [nn(k_ref[:, lanes[a]], lows[a]) for a in range(PAIR)]
            scales = [
                jnp.exp(
                    head_rows(total_ref, first + a)
                    - head_rows(before_ref, first + a)
                    - middle_lane(head_rows(cum_ref, first + a))
                )
                for a in range(PAIR)
            ]
            for n in range(blocks):
                for a in range(PAIR):
                    factor = scales[a][n : n + 1]
                    grad_k = lk_ref[span(n), lanes[a]].astype(F32) + factor * from_v[a][span(n)]
                    grad_v = lv_ref[span(n), lanes[a]].astype(F32) + factor * from_k[a][span(n)]
                    gk_ref[span(n), here[a]] = grad_k.astype(BF16)
                    gv_ref[span(n), here[a]] = grad_v.astype(BF16)
            for a in range(PAIR):
                gg_ref[:, lanes[a]] = state_ref[at * PAIR + a, DH + 1 : DH + 2, :]

        if of_other:
            here = slice(g * GROUP * DH, (g + 1) * GROUP * DH)
            there = head_lanes(half_heads(position_ref, True, g * GROUP, heads), GROUP)
            for which, (source, target) in enumerate(((gk_ref, gk_hbm), (gv_ref, gv_hbm))):
                copies.append(pltpu.make_async_copy(source.at[:, here], target.at[:, there], sems.at[which, g]))
                copies[-1].start()
    for copy in copies:
        copy.wait()


def grads_leaving(of_other, position, keys, values, local_k, local_v, state, cum, before, total, done):
    rows, width = keys.shape
    heads = width // DH
    like = jax.ShapeDtypeStruct((rows, width if of_other else width // 2), BF16)
    kept = pltpu.VMEM((rows, width // 2), BF16)
    sems = [pltpu.SemaphoreType.DMA((2, heads // 2 // GROUP)), pltpu.SemaphoreType.DMA((2,))]
    return pl.pallas_call(
        functools.partial(leave_body, of_other),
        in_specs=[SMEM] + [VMEM] * (8 + len(done)),
        out_specs=[HBM, HBM, VMEM] if of_other else [VMEM] * 3,
        out_shape=[like, like, jax.ShapeDtypeStruct((1, width), F32)],
        scratch_shapes=[kept, kept] + sems if of_other else [],
        compiler_params=params(6),
        cost_estimate=cost(2 * rows * width * DH, 6 * rows * width),
        name="leave_taken" if of_other else "leave_kept",
    )(position, keys, values, local_k, local_v, state, cum, before, total, *done)


def per_device(queries, keys, values, log_decay, gain, grad_out):
    place = lax.axis_index("seq")
    position = jnp.stack([place % 2, place // 2 % ALONG_Z, place // (2 * ALONG_Z)]).astype(jnp.int32)
    gain_row = gain.reshape(1, -1)
    keys, values, queries, grad_out, log_decay = (
        pltpu.with_memory_space_constraint(a, pltpu.HBM) for a in (keys, values, queries, grad_out, log_decay)
    )
    send, keys, values, cum, before, total = local_state(True, position, keys, values, (log_decay,))
    (own,) = local_state(False, position, keys, values, (cum, before, total))

    def attend_part(first, count, load):
        def run(after, done):
            held = done[7] if done else queries
            outs = attend(after, first, count, load, keys, values, cum, held, grad_out, done[:7])
            if load == "queries":
                return (*outs[:7], outs[7], outs[0])
            if load == "grad_out":
                return (*outs[:7], held, outs[7], outs[0])
            return (*outs[:7], held, done[8], outs[0])

        return run

    keep, taken, (local, lows, turned, q_up, k_up, v_up, weights, queries, grad_out, _) = scan_over_seq(
        send, own, position, False, [attend_part(0, 4, "queries"), attend_part(4, 6, "grad_out"), attend_part(10, 6, None)]
    )
    table = (cum, before)
    done = attend_entering(False, position, q_up, local, grad_out, gain_row, keep, *table, ())
    attn, entering, stats = attend_entering(True, position, q_up, local, grad_out, gain_row, taken, *table, done)[:3]
    count = lax.axis_size("head")
    stats = [stats] + [
        lax.ppermute(stats, "head", [(i, (i + s) % count) for i in range(count)]) for s in range(1, count)
    ]
    shared = (position, turned, attn, grad_out, gain_row, cum, before, total)
    grad_attn, send, inverse, factor = norm_backward(True, *shared, stats)
    grad_attn, own = norm_backward(False, *shared, (inverse, factor, grad_attn))
    inputs = (queries, keys, turned, k_up, v_up, weights, grad_attn, attn, gain_row, inverse, lows, entering, cum, before)

    def grads_part(first, count):
        return lambda after, done: grads_local(after, first, count, inputs, done)

    keep, taken, (output, grad_q, local_k, local_v) = scan_over_seq(
        send, own, position, True, [grads_part(0, 6), grads_part(6, 6), grads_part(12, 4)]
    )
    shared = (position, k_up, v_up, local_k, local_v)
    done = grads_leaving(False, *shared, keep, cum, before, total, ())
    grad_k, grad_v, grad_gain = grads_leaving(True, *shared, taken, cum, before, total, done)
    return output, grad_q, grad_k, grad_v, grad_gain.reshape(-1)


def solution(mesh):
    tokens, heads = P("seq", "head"), P("head")
    return jax.shard_map(
        per_device,
        mesh=mesh,
        in_specs=(tokens, tokens, tokens, P("head", "seq"), heads, tokens),
        out_specs=(tokens, tokens, tokens, tokens, heads),
        check_vma=False,
    )
```

```python
import functools

import jax
import jax.numpy as jnp
from jax import lax
from jax.experimental import pallas as pl
from jax.experimental.pallas import tpu as pltpu
from jax.sharding import PartitionSpec as P

HEAD_TOTAL = 64
DH = 128
SPAN = 128
ROWS = 8
PIECE = DH + ROWS
GROUP = 4
PAIR = 2
ALONG_X, ALONG_Z = 4, 4
F32 = jnp.float32
BF16 = jnp.bfloat16
EXACT = lax.Precision.HIGHEST
VMEM = pl.BlockSpec(memory_space=pltpu.VMEM)
HBM = pl.BlockSpec(memory_space=pltpu.HBM)
ANY = pl.BlockSpec(memory_space=pl.ANY)


def dot(a, b, contract, precision=None):
    return lax.dot_general(
        a, b, ((contract[:1], contract[1:]), ((), ())), precision=precision, preferred_element_type=F32
    )


def nn(a, b):
    return dot(a, b, (1, 0))


def nt(a, b):
    return dot(a, b, (1, 1))


def params(mib):
    return pltpu.CompilerParams(vmem_limit_bytes=mib * 1024 * 1024)


def cost(flops, nbytes):
    return pl.CostEstimate(flops=int(flops), bytes_accessed=int(nbytes), transcendentals=0)


def head_rows(ref, head):
    return ref[pl.ds(pl.multiple_of(head * ROWS, ROWS), ROWS), :]


def head_lanes(head, count=1):
    return pl.ds(pl.multiple_of(head * DH, DH), count * DH)


def span(n):
    return slice(n * SPAN, (n + 1) * SPAN)


def last_lane(rows):
    return jnp.broadcast_to(rows[:, SPAN - 1 :], rows.shape)


def middle_lane(rows):
    return jnp.broadcast_to(rows[:, SPAN // 2 - 1 : SPAN // 2], rows.shape)


def masks():
    i = lax.broadcasted_iota(jnp.int32, (SPAN, SPAN), 0)
    j = lax.broadcasted_iota(jnp.int32, (SPAN, SPAN), 1)
    return i >= j, i <= j


def join_rows(rows, blocks):
    return jnp.concatenate([rows[n : n + 1] for n in range(blocks)], axis=1)


def piece_store(ref, at, state, extra):
    ref[at, :DH, :] = state
    ref[at, DH:, :] = extra


def extra_rows(decay, gain_row=None):
    place = lax.broadcasted_iota(jnp.int32, (ROWS, DH), 0)
    rest = 0.0 if gain_row is None else jnp.where(place == 1, gain_row, 0.0)
    return jnp.where(place == 0, decay, rest)


def position():
    place = lax.axis_index("seq")
    return lax.rem(place, 2), lax.rem(place // 2, ALONG_Z), place // (2 * ALONG_Z)


def half_heads(core, of_other, at, heads):
    half = heads // 2
    start = (1 - core) if of_other else core
    return start * half + at


def decay_tables(log_ref, cum_ref, before_ref, total_ref):
    heads, rows = log_ref.shape
    _, triangle = masks()
    triangle = triangle.astype(F32)
    cum_ref[...] = jnp.zeros_like(cum_ref)
    before_ref[...] = jnp.zeros_like(before_ref)
    before = jnp.zeros((heads, SPAN), F32)
    for n in range(rows // SPAN):
        cum = dot(log_ref[:, span(n)], triangle, (1, 0), EXACT)
        for h in range(heads):
            cum_ref[h * ROWS + n : h * ROWS + n + 1, :] = cum[h : h + 1]
            before_ref[h * ROWS + n : h * ROWS + n + 1, :] = before[h : h + 1]
        before = before + last_lane(cum)
    for h in range(heads):
        total_ref[h * ROWS : (h + 1) * ROWS, :] = jnp.broadcast_to(before[h : h + 1], (ROWS, SPAN))


def state_body(of_other, *refs):
    core, _, _ = position()
    if of_other:
        k_hbm, v_hbm, log_hbm, out_ref, k_ref, v_ref, cum_ref, before_ref, total_ref, sems, log_ref, log_sem = refs
    else:
        k_ref, v_ref, cum_ref, before_ref, total_ref, out_ref = refs
    rows, width = k_ref.shape
    heads, blocks = width // DH, rows // SPAN
    copies = []
    if of_other:
        log_copy = pltpu.make_async_copy(log_hbm, log_ref, log_sem)
        log_copy.start()
        for g in range(heads // GROUP):
            lanes = head_lanes(lax.rem(half_heads(core, True, g * GROUP, heads), heads), GROUP)
            for which, (source, target) in enumerate(((k_hbm, k_ref), (v_hbm, v_ref))):
                copies.append(pltpu.make_async_copy(source.at[:, lanes], target.at[:, lanes], sems.at[which, g]))
                copies[-1].start()
        log_copy.wait()
        decay_tables(log_ref, cum_ref, before_ref, total_ref)

    for g in range(heads // 2 // GROUP):
        first = half_heads(core, of_other, g * GROUP, heads)
        if of_other:
            copies[2 * g].wait()
            copies[2 * g + 1].wait()
        totals = [head_rows(total_ref, first + at) for at in range(GROUP)]
        scales = [
            jnp.exp(totals[at] - head_rows(before_ref, first + at) - head_rows(cum_ref, first + at)) for at in range(GROUP)
        ]
        decayed = [
            (k_ref[:, head_lanes(first + at)].T.astype(F32) * join_rows(scales[at], blocks)).astype(BF16)
            for at in range(GROUP)
        ]
        states = [nn(decayed[at], v_ref[:, head_lanes(first + at)]) for at in range(GROUP)]
        for at in range(GROUP):
            piece_store(out_ref, g * GROUP + at, states[at], extra_rows(jnp.exp(totals[at])))
    for copy in copies[heads // GROUP :]:
        copy.wait()


def local_state(of_other, keys, values, more):
    rows, width = keys.shape
    heads = width // DH
    pieces = jax.ShapeDtypeStruct((heads // 2, PIECE, DH), F32)
    table = jax.ShapeDtypeStruct((heads * ROWS, SPAN), F32)
    like = jax.ShapeDtypeStruct(keys.shape, BF16)
    if of_other:
        specs, outs = [HBM] * 3, [pieces, like, like, table, table, table]
        scratch = [
            pltpu.SemaphoreType.DMA((2, heads // GROUP)),
            pltpu.VMEM(more[0].shape, F32),
            pltpu.SemaphoreType.DMA,
        ]
    else:
        specs, outs, scratch = [VMEM] * 5, [pieces], []
    return pl.pallas_call(
        functools.partial(state_body, of_other),
        in_specs=specs,
        out_specs=[VMEM] * len(outs),
        out_shape=outs,
        scratch_shapes=scratch,
        compiler_params=params(4),
        cost_estimate=cost(heads * rows * DH * DH, 2 * rows * heads * DH),
        name="state_given" if of_other else "state_kept",
    )(keys, values, *more)


def arrival_order(count):
    return [0] + sorted(range(1, count), key=lambda s: -min(s, count - s))


def first_row():
    return lax.broadcasted_iota(jnp.int32, (ROWS, DH), 0) == 0


def join_extra(a, b):
    return jnp.where(first_row(), a * b, a + b)


def cores_body(reverse, own_ref, got_ref, *out_refs):
    core, z, _ = position()
    near_here = (core == 0) != reverse
    each = own_ref.shape[0] // ALONG_Z
    for shift, out_ref in enumerate(out_refs):
        for j in range(each):
            head = lax.rem(z + shift, ALONG_Z) * each + j
            own, got = own_ref[head], got_ref[head]
            near, far = jnp.where(near_here, own, got), jnp.where(near_here, got, own)
            piece_store(out_ref, j, far[DH : DH + 1] * near[:DH] + far[:DH], join_extra(near[DH:], far[DH:]))


def along_z_body(reverse, *refs):
    in_refs, (_, total_ref, prefix_ref, slots) = refs[:ALONG_Z], refs[ALONG_Z:]
    _, z, _ = position()
    for shift, ref in zip(arrival_order(len(in_refs)), in_refs):
        slots[lax.rem(z - shift + ALONG_Z, ALONG_Z)] = ref[...]
    for j in range(total_ref.shape[0]):
        state = jnp.zeros((DH, DH), F32)
        extra = jnp.where(first_row(), 1.0, 0.0)
        for lap in range(ALONG_Z):
            at = ALONG_Z - 1 - lap if reverse else lap
            prefix_ref[at, j, :DH, :] = state
            prefix_ref[at, j, DH:, :] = extra
            state = slots[at, j, DH : DH + 1, :] * state + slots[at, j, :DH, :]
            extra = join_extra(extra, slots[at, j, DH:, :])
        piece_store(total_ref, j, state, extra)


def along_x_body(reverse, *refs):
    in_refs, prefix_ref, out_refs, slots = refs[:ALONG_X], refs[ALONG_X], refs[ALONG_X + 2 : -1], refs[-1]
    _, z, x = position()
    for shift, ref in zip(arrival_order(len(in_refs)), in_refs):
        slots[lax.rem(x - shift + ALONG_X, ALONG_X)] = ref[...]
    for j in range(prefix_ref.shape[1]):
        state = jnp.zeros((DH, DH), F32)
        extra = jnp.zeros((ROWS, DH), F32)
        for lap in range(ALONG_X):
            at = ALONG_X - 1 - lap if reverse else lap
            taken = (at > x) if reverse else (at < x)
            state = jnp.where(taken, slots[at, j, DH : DH + 1, :] * state + slots[at, j, :DH, :], state)
            extra = extra + slots[at, j, DH:, :]
        for shift, out_ref in enumerate(out_refs):
            at = lax.rem(z + shift, ALONG_Z)
            piece_store(out_ref, j, prefix_ref[at, j, :DH, :] + prefix_ref[at, j, DH : DH + 1, :] * state, extra)


def entering_body(reverse, *refs):
    in_refs, (own_ref, got_ref, _, keep_ref, give_ref) = refs[:ALONG_Z], refs[ALONG_Z:]
    core, z, _ = position()
    near_here = (core == 0) != reverse
    each = own_ref.shape[0] // ALONG_Z
    for shift, ref in zip(arrival_order(len(in_refs)), in_refs):
        for j in range(each):
            head = lax.rem(z - shift + ALONG_Z, ALONG_Z) * each + j
            near = jnp.where(near_here, own_ref[head], got_ref[head])
            entering, extra = ref[j, :DH, :], ref[j, DH:, :]
            passed = near[DH : DH + 1] * entering + near[:DH]
            piece_store(keep_ref, head, jnp.where(near_here, entering, passed), extra)
            piece_store(give_ref, head, jnp.where(near_here, passed, entering), extra)


def scan_step(body, name, reverse, arrays, after, out_counts, scratch):
    shapes = [jax.ShapeDtypeStruct(shape, F32) for shape in out_counts]
    afters = [] if after is None else [after]
    return pl.pallas_call(
        functools.partial(body, reverse),
        in_specs=[VMEM] * len(arrays) + [ANY] * len(afters),
        out_specs=[VMEM] * len(shapes),
        out_shape=shapes,
        scratch_shapes=scratch,
        compiler_params=params(3),
        cost_estimate=cost(10**6, 10**6),
        name=name,
    )(*arrays, *afters)


def scan_over_seq(send, own, reverse, works):
    count = lax.axis_size("seq")
    heads = own.shape[0]
    each = heads // ALONG_Z

    def index(x, z, c):
        return (x % ALONG_X * ALONG_Z + z % ALONG_Z) * 2 + c

    every = [(x, z, c) for x in range(ALONG_X) for z in range(ALONG_Z) for c in range(2)]
    across = [(i, i ^ 1) for i in range(count)]
    by_z = [[(index(x, z, c), index(x, z + s, c)) for x, z, c in every] for s in range(ALONG_Z)]
    by_x = [[(index(x, z, c), index(x + s, z, c)) for x, z, c in every] for s in range(ALONG_X)]
    piece = (each, PIECE, DH)

    def shifted(arrays, moves):
        return [lax.ppermute(arrays[s], "seq", moves[s]) if s else arrays[0] for s in arrival_order(len(moves))]

    got = lax.ppermute(send, "seq", across)
    parts = scan_step(cores_body, "join_cores", reverse, [own, got], None, [piece] * ALONG_Z, [])
    arrived = shifted(parts, by_z)
    done = works[0](parts[0], ())
    total, prefix = scan_step(
        along_z_body, "join_z", reverse, arrived, done[-1],
        [piece, (ALONG_Z,) + piece], [pltpu.VMEM((ALONG_Z,) + piece, F32)],
    )
    totals = shifted([total] * ALONG_X, by_x)
    done = works[1](total, done)
    parts = scan_step(
        along_x_body, "join_x", reverse, totals + [prefix], done[-1],
        [piece] * ALONG_Z, [pltpu.VMEM((ALONG_X,) + piece, F32)],
    )
    arrived = shifted(parts, by_z)
    done = works[2](parts[0], done)
    keep, give = scan_step(
        entering_body, "entering", reverse, arrived + [own, got], done[-1], [own.shape] * 2, []
    )
    return keep, lax.ppermute(give, "seq", across), done


def block_picks(blocks):
    part = lax.broadcasted_iota(jnp.int32, (4 * ROWS, blocks * SPAN), 0)
    place = lax.broadcasted_iota(jnp.int32, (4 * ROWS, blocks * SPAN), 1)
    return (lax.rem(part, ROWS) == place // SPAN).astype(BF16)


def spread(rows, picks):
    high = rows.astype(BF16).astype(F32)
    middle = (rows - high).astype(BF16).astype(F32)
    parts = jnp.concatenate([high, middle, rows - high - middle, jnp.zeros_like(rows)], axis=0)
    return nn(parts.T.astype(BF16), picks)


def staggered(stages, steps):
    for at in range(len(steps) + len(stages) - 1):
        for back, stage in enumerate(stages):
            if 0 <= at - back < len(steps):
                stage(*steps[at - back])


def attend_heads(heads, q_ref, k_ref, v_ref, cum_ref, outs, both_masks, picks):
    local_ref, low_ref, turned_ref, qs_ref, ks_ref, vs_ref, weights_ref = outs
    mask, turned_mask = both_masks
    blocks = k_ref.shape[0] // SPAN
    each = range(len(heads))
    steps = [(a, n) for n in range(blocks) for a in each]
    lanes = [head_lanes(h) for h in heads]
    cums = [head_rows(cum_ref, h) for h in heads]
    mids = [middle_lane(c) for c in cums]
    ends = [last_lane(c) for c in cums]
    shifts = [spread(c - m, picks) for c, m in zip(cums, mids)]
    mid_scale, end_scale = [jnp.exp(m) for m in mids], [jnp.exp(e) for e in ends]
    rest_scale = [jnp.exp(e - m) for e, m in zip(ends, mids)]
    q_up, k_up, q_turned, k_turned, scores, turned_weights, updates, weights, lows, totals = ({} for _ in range(10))
    state = {a: jnp.zeros((DH, DH), F32) for a in each}

    def scale(a, n):
        shift = shifts[a][:, span(n)]
        up, down = jnp.exp(shift), jnp.exp(-shift)
        q_up[a, n] = (q_ref[span(n), lanes[a]].astype(F32) * up).astype(BF16)
        k_up[a, n] = (k_ref[span(n), lanes[a]].astype(F32) * down).astype(BF16)
        vs_ref[span(n), lanes[a]] = (v_ref[span(n), lanes[a]].astype(F32) * down).astype(BF16)
        qs_ref[span(n), lanes[a]] = q_up[a, n]
        ks_ref[span(n), lanes[a]] = k_up[a, n]

    def turn(a, n):
        k_turned[a, n] = k_up[a, n].T
        q_turned[a, n] = q_up[a, n].T
        turned_ref[heads[a], :, span(n)] = q_turned[a, n]

    def multiply(a, n):
        scores[a, n] = nn(q_up[a, n], k_turned[a, n])
        turned_weights[a, n] = nn(k_up[a, n], q_turned[a, n])
        if n < blocks - 1:
            updates[a, n] = nn(k_turned[a, n], v_ref[span(n), lanes[a]])

    def mask_out(a, n):
        weights[a, n] = jnp.where(mask, scores[a, n], 0.0).astype(BF16)
        weights_ref[heads[a], n] = jnp.where(turned_mask, turned_weights[a, n], 0.0).astype(BF16)
        lows[a, n] = (mid_scale[a][n : n + 1] * state[a]).astype(BF16)
        low_ref[heads[a], n] = lows[a, n]
        if n < blocks - 1:
            state[a] = end_scale[a][n : n + 1] * state[a] + rest_scale[a][n : n + 1] * updates[a, n]

    def combine(a, n):
        v = v_ref[span(n), lanes[a]]
        if n == 0:
            totals[a, n] = nn(weights[a, n], v)
        else:
            left = jnp.concatenate([weights[a, n], q_up[a, n]], axis=1)
            totals[a, n] = nn(left, jnp.concatenate([v, lows[a, n]], axis=0))

    def store(a, n):
        local_ref[span(n), lanes[a]] = totals[a, n].astype(BF16)

    staggered([scale, turn, multiply, mask_out, combine, store], steps)


def attend_body(first, count, load, *refs):
    k_ref, v_ref, cum_ref = refs[1:4]
    refs = refs[4:]
    copies = []
    if load == "queries":
        q_hbm, outs, (q_ref, sems) = refs[0], refs[1:8], refs[8:]
        for g in range(q_hbm.shape[1] // (GROUP * DH)):
            lanes = slice(g * GROUP * DH, (g + 1) * GROUP * DH)
            copies.append(pltpu.make_async_copy(q_hbm.at[:, lanes], q_ref.at[:, lanes], sems.at[g]))
    elif load == "grad_out":
        q_ref, go_hbm, outs, (go_ref, sems) = refs[0], refs[1], refs[9:16], refs[16:]
        copies.append(pltpu.make_async_copy(go_hbm, go_ref, sems.at[0]))
    else:
        q_ref, outs = refs[0], refs[8:15]
    for copy in copies:
        copy.start()
    both_masks = masks()
    picks = block_picks(k_ref.shape[0] // SPAN)
    held = []
    for at, copy in enumerate(copies):
        if load == "queries" and at * GROUP < first + count:
            copy.wait()
        else:
            held.append(copy)
    attend_heads([first + a for a in range(count)], q_ref, k_ref, v_ref, cum_ref, outs, both_masks, picks)
    for copy in held:
        copy.wait()


def attend(after, first, count, load, keys, values, cum, queries, grad_out, done):
    rows, width = keys.shape
    heads, blocks = width // DH, rows // SPAN
    like = jax.ShapeDtypeStruct((rows, width), BF16)
    squares = jax.ShapeDtypeStruct((heads, blocks, DH, DH), BF16)
    outs = [like, squares, jax.ShapeDtypeStruct((heads, DH, rows), BF16), like, like, like, squares]
    arrays, specs = [after, keys, values, cum, queries], [ANY, VMEM, VMEM, VMEM]
    specs.append(HBM if load == "queries" else VMEM)
    if load == "grad_out":
        arrays.append(grad_out)
        specs.append(HBM)
    aliases = {len(arrays) + i: i for i in range(len(done))}
    if load is not None:
        outs.append(like)
    return pl.pallas_call(
        functools.partial(attend_body, first, count, load),
        in_specs=specs + [VMEM] * len(done),
        out_specs=[VMEM] * len(outs),
        out_shape=outs,
        input_output_aliases=aliases,
        scratch_shapes=[] if load is None else [pltpu.SemaphoreType.DMA((heads // GROUP,))],
        compiler_params=params(6),
        cost_estimate=cost(10 * rows * count * DH * DH, 12 * rows * count * DH),
        name=f"attend_{first}",
    )(*arrays, *done)


def enter_body(of_other, q_ref, local_ref, go_ref, gain_ref, state_ref, cum_ref, before_ref, *refs):
    if of_other:
        attn_ref, low_ref, stats_ref, square_ref, inner_ref = refs[4:]
    else:
        attn_ref, low_ref, square_ref, inner_ref = refs
    core, _, _ = position()
    rows, width = q_ref.shape
    heads, blocks = width // DH, rows // SPAN
    if not of_other:
        square_ref[...] = jnp.zeros_like(square_ref)
        inner_ref[...] = jnp.zeros_like(inner_ref)

    for g in range(heads // 2 // GROUP):
        first = half_heads(core, of_other, g * GROUP, heads)
        lanes = [head_lanes(first + at) for at in range(GROUP)]
        carried, scales, gains = [], [], []
        for at in range(GROUP):
            low = state_ref[g * GROUP + at, :DH, :].astype(BF16)
            low_ref[first + at] = low
            carried.append(nn(q_ref[:, lanes[at]], low))
            scales.append(jnp.exp(middle_lane(head_rows(cum_ref, first + at)) + head_rows(before_ref, first + at)))
            gains.append(gain_ref[:, lanes[at]])
        for n in range(blocks):
            square = square_ref[span(n), :]
            inner = inner_ref[span(n), :]
            for at in range(GROUP):
                entered = carried[at][span(n)] * scales[at][n : n + 1]
                attn = (local_ref[span(n), lanes[at]].astype(F32) + entered).astype(BF16)
                attn_ref[span(n), lanes[at]] = attn
                attn = attn.astype(F32)
                square += attn * attn
                inner += go_ref[span(n), lanes[at]].astype(F32) * gains[at] * attn
            square_ref[span(n), :] = square
            inner_ref[span(n), :] = inner

    if of_other:
        ones = jnp.ones((8, DH), F32)
        stats_ref[0:1, :] = dot(ones, square_ref[...], (1, 1), EXACT)[0:1]
        stats_ref[1:2, :] = dot(ones, inner_ref[...], (1, 1), EXACT)[0:1]


def attend_entering(of_other, queries, local, grad_out, gain, state, cum, before, done):
    rows, width = queries.shape
    heads = width // DH
    sums = jax.ShapeDtypeStruct((rows, DH), F32)
    outs = [jax.ShapeDtypeStruct((rows, width), BF16), jax.ShapeDtypeStruct((heads, DH, DH), BF16)]
    if of_other:
        outs, aliases = outs + [jax.ShapeDtypeStruct((2, rows), F32), sums, sums], {7: 0, 8: 1, 9: 3, 10: 4}
    else:
        outs, aliases = outs + [sums, sums], {}
    return pl.pallas_call(
        functools.partial(enter_body, of_other),
        in_specs=[VMEM] * (7 + len(done)),
        out_specs=[VMEM] * len(outs),
        out_shape=outs,
        input_output_aliases=aliases,
        compiler_params=params(4),
        cost_estimate=cost(rows * width * DH, 4 * rows * width),
        name="enter_taken" if of_other else "enter_kept",
    )(queries, local, grad_out, gain, state, cum, before, *done)


def columns(row, ref, blocks):
    for n in range(blocks):
        ref[span(n), :] = jnp.broadcast_to(row[:, span(n)], (SPAN, SPAN)).T


def norm_body(of_other, turned_ref, attn_ref, go_ref, gain_ref, cum_ref, before_ref, total_ref, *refs):
    core, _, _ = position()
    rows, width = attn_ref.shape
    heads, blocks = width // DH, rows // SPAN
    if of_other:
        stats_refs, (ga_ref, out_ref, inverse_ref, factor_ref) = refs[:-4], refs[-4:]
        stats = functools.reduce(jnp.add, [ref[...] for ref in stats_refs]) / (HEAD_TOTAL * DH)
        inverse = lax.rsqrt(stats[0:1] + 1e-06)
        columns(inverse, inverse_ref, blocks)
        columns(inverse * inverse * inverse * stats[1:2], factor_ref, blocks)
    else:
        inverse_ref, factor_ref, _, ga_ref, out_ref = refs

    for g in range(heads // 2 // GROUP):
        places = [g * GROUP + at for at in range(GROUP)]
        heads_now = [half_heads(core, of_other, place, heads) for place in places]
        lanes = [head_lanes(head) for head in heads_now]
        gains = [gain_ref[:, lane] for lane in lanes]
        gain_sums = [jnp.zeros((8, DH), F32) for _ in places]
        grads = [[] for _ in places]
        for n in range(blocks):
            for at in range(GROUP):
                attn = attn_ref[span(n), lanes[at]].astype(F32)
                scaled = go_ref[span(n), lanes[at]].astype(F32) * inverse_ref[span(n), :]
                gain_sums[at] += jnp.sum((scaled * attn).reshape(SPAN // 8, 8, DH), axis=0)
                grad = (scaled * gains[at] - attn * factor_ref[span(n), :]).astype(BF16)
                ga_ref[span(n), lanes[at]] = grad
                grads[at].append(grad)
        updates = [
            [nn(turned_ref[heads_now[at], :, span(n)], grads[at][n]) for n in range(blocks)] for at in range(GROUP)
        ]
        scales = [jnp.exp(middle_lane(head_rows(cum_ref, h)) + head_rows(before_ref, h)) for h in heads_now]
        states = [sum(scales[at][n : n + 1] * updates[at][n] for n in range(blocks)) for at in range(GROUP)]
        for at in range(GROUP):
            decay = jnp.exp(head_rows(total_ref, heads_now[at]))
            piece_store(out_ref, places[at], states[at], extra_rows(decay, jnp.sum(gain_sums[at], axis=0, keepdims=True)))


def norm_backward(of_other, turned, attn, grad_out, gain, cum, before, total, more):
    rows, width = attn.shape
    heads = width // DH
    pieces = jax.ShapeDtypeStruct((heads // 2, PIECE, DH), F32)
    cols = jax.ShapeDtypeStruct((rows, DH), F32)
    outs = [jax.ShapeDtypeStruct((rows, width), BF16), pieces] + ([cols, cols] if of_other else [])
    return pl.pallas_call(
        functools.partial(norm_body, of_other),
        in_specs=[VMEM] * (7 + len(more)),
        out_specs=[VMEM] * len(outs),
        out_shape=outs,
        input_output_aliases={} if of_other else {9: 0},
        compiler_params=params(5),
        cost_estimate=cost(rows * width * DH, 4 * rows * width),
        name="norm_given" if of_other else "norm_kept",
    )(turned, attn, grad_out, gain, cum, before, total, *more)


def grads_heads(heads, places, refs, out_ref, gq_ref, lk_ref, lv_ref, both_masks, picks, send):
    q_ref, k_ref, turned_ref, ks_ref, vs_ref, weights_ref, ga_ref, attn_ref = refs[:8]
    gain_ref, inverse_ref, low_ref, enter_ref, cum_ref, before_ref = refs[8:]
    mask, _ = both_masks
    blocks = k_ref.shape[0] // SPAN
    each = range(len(heads))
    steps = [(a, n) for n in range(blocks) for a in each]
    lanes = [head_lanes(h) for h in heads]
    here = [head_lanes(p) for p in places]
    cums = [head_rows(cum_ref, h) for h in heads]
    mids = [middle_lane(c) for c in cums]
    ends = [last_lane(c) for c in cums]
    query_scale = [jnp.exp(spread(c - m, picks)) for c, m in zip(cums, mids)]
    mid_scale, end_scale = [jnp.exp(m) for m in mids], [jnp.exp(e) for e in ends]
    rest_scale = [jnp.exp(e - m) for e, m in zip(ends, mids)]
    enter_scale = [jnp.exp(m + head_rows(before_ref, h)) for m, h in zip(mids, heads)]
    entering = [enter_ref[h].astype(F32) for h in heads]

    def at(ref, a, n):
        return ref[span(n), lanes[a]]

    ga_up, v_turned, states, scores, updates, weights, lows, lows_turned, grad_q, grad_k, grad_v = ({} for _ in range(11))
    back = {a: jnp.zeros((DH, DH), F32) for a in each}

    def scale(a, n):
        ga_up[a, n] = (at(ga_ref, a, n).astype(F32) * query_scale[a][:, span(n)]).astype(BF16)
        v_turned[a, n] = at(vs_ref, a, n).T
        state = low_ref[heads[a], n].astype(F32) + enter_scale[a][n : n + 1] * entering[a]
        states[a, n] = state.astype(BF16).T

    def multiply(a, n):
        scores[a, n] = nn(ga_up[a, n], v_turned[a, n])
        if n > 0:
            updates[a, n] = nn(turned_ref[heads[a], :, span(n)], at(ga_ref, a, n))

    def mask_out(a, n):
        scores[a, n] = jnp.where(mask, scores[a, n], 0.0).astype(BF16)
        weights[a, n] = scores[a, n].T
        if n < blocks - 1:
            lows[a, n] = (rest_scale[a][n : n + 1] * back[a]).astype(BF16)
            lows_turned[a, n] = lows[a, n].T
        if n > 0:
            back[a] = end_scale[a][n : n + 1] * back[a] + mid_scale[a][n : n + 1] * updates[a, n]

    def combine(a, n):
        left = jnp.concatenate([scores[a, n], ga_up[a, n]], axis=1)
        grad_q[a, n] = nn(left, jnp.concatenate([at(k_ref, a, n), states[a, n]], axis=0))
        left_k, right_k = weights[a, n], at(q_ref, a, n)
        left_v, right_v = weights_ref[heads[a], n], at(ga_ref, a, n)
        if n < blocks - 1:
            left_k = jnp.concatenate([left_k, at(vs_ref, a, n)], axis=1)
            right_k = jnp.concatenate([right_k, lows_turned[a, n]], axis=0)
            left_v = jnp.concatenate([left_v, at(ks_ref, a, n)], axis=1)
            right_v = jnp.concatenate([right_v, lows[a, n]], axis=0)
        grad_k[a, n] = nn(left_k, right_k)
        grad_v[a, n] = nn(left_v, right_v)

    def store(a, n):
        gq_ref[span(n), here[a]] = grad_q[a, n].astype(BF16)
        lv_ref[span(n), lanes[a]] = grad_v[a, n].astype(BF16)
        lk_ref[span(n), lanes[a]] = grad_k[a, n].astype(BF16)
        normed = at(attn_ref, a, n).astype(F32) * inverse_ref[span(n), :]
        out_ref[span(n), here[a]] = (normed * gain_ref[:, lanes[a]]).astype(BF16)
        if a == 0:
            send(n)

    staggered([scale, multiply, mask_out, combine, store], steps[::-1])


def grads_body(first, count, chained, *refs):
    inputs = refs[1:15]
    refs = refs[15 + (4 if chained else 0) :]
    out_hbm, gq_hbm, lk_ref, lv_ref, out_ref, gq_ref, sems = refs
    both_masks = masks()
    picks = block_picks(inputs[0].shape[0] // SPAN)

    copies = []

    def send(n):
        lanes = slice(first * DH, (first + count) * DH)
        for which, (source, target) in enumerate(((out_ref, out_hbm), (gq_ref, gq_hbm))):
            copies.append(pltpu.make_async_copy(source.at[span(n), :], target.at[span(n), lanes], sems.at[which, n]))
            copies[-1].start()

    heads, places = [first + a for a in range(count)], list(range(count))
    grads_heads(heads, places, inputs, out_ref, gq_ref, lk_ref, lv_ref, both_masks, picks, send)
    for copy in copies:
        copy.wait()


def grads_local(after, first, count, inputs, done):
    rows, width = inputs[0].shape
    like = jax.ShapeDtypeStruct((rows, width), BF16)
    kinds = [HBM, HBM, VMEM, VMEM]
    return pl.pallas_call(
        functools.partial(grads_body, first, count, bool(done)),
        in_specs=[ANY] + [VMEM] * 14 + (kinds if done else []),
        out_specs=kinds,
        out_shape=[like] * 4,
        input_output_aliases={15 + i: i for i in range(4)} if done else {},
        scratch_shapes=[
            pltpu.VMEM((rows, count * DH), BF16),
            pltpu.VMEM((rows, count * DH), BF16),
            pltpu.SemaphoreType.DMA((2, rows // SPAN)),
        ],
        compiler_params=params(8),
        cost_estimate=cost(22 * rows * count * DH * DH, 24 * rows * count * DH),
        name=f"grads_{first}",
    )(after, *inputs, *done)


def leave_body(of_other, k_ref, v_ref, lk_ref, lv_ref, state_ref, cum_ref, before_ref, total_ref, *refs):
    core, _, _ = position()
    rows, width = k_ref.shape
    heads, blocks = width // DH, rows // SPAN
    half = heads // 2
    copies = []
    if of_other:
        kept_k_ref, kept_v_ref, kept_gain_ref, gk_hbm, gv_hbm, gg_ref, gk_ref, gv_ref, sems, kept_sems = refs
        there = head_lanes(half_heads(core, False, 0, heads), half)
        for which, (source, target) in enumerate(((kept_k_ref, gk_hbm), (kept_v_ref, gv_hbm))):
            copies.append(pltpu.make_async_copy(source, target.at[:, there], kept_sems.at[which]))
            copies[-1].start()
        gg_ref[...] = kept_gain_ref[...]
    else:
        gk_ref, gv_ref, gg_ref = refs
    for g in range(half // GROUP):

        for at in range(g * GROUP // PAIR, (g + 1) * GROUP // PAIR):
            first = half_heads(core, of_other, at * PAIR, heads)
            lanes = [head_lanes(first + a) for a in range(PAIR)]
            here = [head_lanes(at * PAIR + a) for a in range(PAIR)]
            lows = [state_ref[at * PAIR + a, :DH, :].astype(BF16) for a in range(PAIR)]
            from_v = [nt(v_ref[:, lanes[a]], lows[a]) for a in range(PAIR)]
            from_k = [nn(k_ref[:, lanes[a]], lows[a]) for a in range(PAIR)]
            scales = [
                jnp.exp(
                    head_rows(total_ref, first + a)
                    - head_rows(before_ref, first + a)
                    - middle_lane(head_rows(cum_ref, first + a))
                )
                for a in range(PAIR)
            ]
            for n in range(blocks):
                for a in range(PAIR):
                    factor = scales[a][n : n + 1]
                    grad_k = lk_ref[span(n), lanes[a]].astype(F32) + factor * from_v[a][span(n)]
                    grad_v = lv_ref[span(n), lanes[a]].astype(F32) + factor * from_k[a][span(n)]
                    gk_ref[span(n), here[a]] = grad_k.astype(BF16)
                    gv_ref[span(n), here[a]] = grad_v.astype(BF16)
            for a in range(PAIR):
                gg_ref[:, lanes[a]] = state_ref[at * PAIR + a, DH + 1 : DH + 2, :]

        if of_other:
            here = slice(g * GROUP * DH, (g + 1) * GROUP * DH)
            there = head_lanes(half_heads(core, True, g * GROUP, heads), GROUP)
            for which, (source, target) in enumerate(((gk_ref, gk_hbm), (gv_ref, gv_hbm))):
                copies.append(pltpu.make_async_copy(source.at[:, here], target.at[:, there], sems.at[which, g]))
                copies[-1].start()
    for copy in copies:
        copy.wait()


def grads_leaving(of_other, keys, values, local_k, local_v, state, cum, before, total, done):
    rows, width = keys.shape
    heads = width // DH
    like = jax.ShapeDtypeStruct((rows, width if of_other else width // 2), BF16)
    kept = pltpu.VMEM((rows, width // 2), BF16)
    sems = [pltpu.SemaphoreType.DMA((2, heads // 2 // GROUP)), pltpu.SemaphoreType.DMA((2,))]
    return pl.pallas_call(
        functools.partial(leave_body, of_other),
        in_specs=[VMEM] * (8 + len(done)),
        out_specs=[HBM, HBM, VMEM] if of_other else [VMEM] * 3,
        out_shape=[like, like, jax.ShapeDtypeStruct((1, width), F32)],
        scratch_shapes=[kept, kept] + sems if of_other else [],
        compiler_params=params(6),
        cost_estimate=cost(2 * rows * width * DH, 6 * rows * width),
        name="leave_taken" if of_other else "leave_kept",
    )(keys, values, local_k, local_v, state, cum, before, total, *done)


def per_device(queries, keys, values, log_decay, gain, grad_out):
    gain_row = gain.reshape(1, -1)
    keys, values, queries, grad_out, log_decay = (
        pltpu.with_memory_space_constraint(a, pltpu.HBM) for a in (keys, values, queries, grad_out, log_decay)
    )
    send, keys, values, cum, before, total = local_state(True, keys, values, (log_decay,))
    (own,) = local_state(False, keys, values, (cum, before, total))

    def attend_part(first, count, load):
        def run(after, done):
            held = done[7] if done else queries
            outs = attend(after, first, count, load, keys, values, cum, held, grad_out, done[:7])
            if load == "queries":
                return (*outs[:7], outs[7], outs[0])
            if load == "grad_out":
                return (*outs[:7], held, outs[7], outs[0])
            return (*outs[:7], held, done[8], outs[0])

        return run

    keep, taken, (local, lows, turned, q_up, k_up, v_up, weights, queries, grad_out, _) = scan_over_seq(
        send, own, False, [attend_part(0, 6, "queries"), attend_part(6, 6, "grad_out"), attend_part(12, 4, None)]
    )
    table = (cum, before)
    done = attend_entering(False, q_up, local, grad_out, gain_row, keep, *table, ())
    attn, entering, stats = attend_entering(True, q_up, local, grad_out, gain_row, taken, *table, done)[:3]
    count = lax.axis_size("head")
    stats = [stats] + [
        lax.ppermute(stats, "head", [(i, (i + s) % count) for i in range(count)]) for s in arrival_order(count)[1:]
    ]
    shared = (turned, attn, grad_out, gain_row, cum, before, total)
    grad_attn, send, inverse, factor = norm_backward(True, *shared, stats)
    grad_attn, own = norm_backward(False, *shared, (inverse, factor, grad_attn))
    inputs = (queries, keys, turned, k_up, v_up, weights, grad_attn, attn, gain_row, inverse, lows, entering, cum, before)

    def grads_part(first, count):
        return lambda after, done: grads_local(after, first, count, inputs, done)

    keep, taken, (output, grad_q, local_k, local_v) = scan_over_seq(
        send, own, True, [grads_part(0, 6), grads_part(6, 6), grads_part(12, 4)]
    )
    shared = (k_up, v_up, local_k, local_v)
    done = grads_leaving(False, *shared, keep, cum, before, total, ())
    grad_k, grad_v, grad_gain = grads_leaving(True, *shared, taken, cum, before, total, done)
    return output, grad_q, grad_k, grad_v, grad_gain.reshape(-1)


def solution(mesh):
    tokens, heads = P("seq", "head"), P("head")
    return jax.shard_map(
        per_device,
        mesh=mesh,
        in_specs=(tokens, tokens, tokens, P("head", "seq"), heads, tokens),
        out_specs=(tokens, tokens, tokens, tokens, heads),
        check_vma=False,
    )
```

```python
import functools

import jax
import jax.numpy as jnp
from jax import lax
from jax.experimental import pallas as pl
from jax.experimental.pallas import tpu as pltpu
from jax.sharding import PartitionSpec as P

HEAD_TOTAL = 64
DH = 128
SPAN = 128
ROWS = 8
STATES = 2 * DH
PIECE = STATES + ROWS
GROUP = 4
PAIR = 2
ALONG_X, ALONG_Z = 4, 4
F32 = jnp.float32
BF16 = jnp.bfloat16
EXACT = lax.Precision.HIGHEST
VMEM = pl.BlockSpec(memory_space=pltpu.VMEM)
HBM = pl.BlockSpec(memory_space=pltpu.HBM)
ANY = pl.BlockSpec(memory_space=pl.ANY)


def dot(a, b, contract, precision=None):
    return lax.dot_general(
        a, b, ((contract[:1], contract[1:]), ((), ())), precision=precision, preferred_element_type=F32
    )


def nn(a, b):
    return dot(a, b, (1, 0))


def nt(a, b):
    return dot(a, b, (1, 1))


def params(mib):
    return pltpu.CompilerParams(vmem_limit_bytes=mib * 1024 * 1024)


def cost(flops, nbytes):
    return pl.CostEstimate(flops=int(flops), bytes_accessed=int(nbytes), transcendentals=0)


def head_rows(ref, head):
    return ref[pl.ds(pl.multiple_of(head * ROWS, ROWS), ROWS), :]


def head_lanes(head, count=1):
    return pl.ds(pl.multiple_of(head * DH, DH), count * DH)


def span(n):
    return slice(n * SPAN, (n + 1) * SPAN)


def last_lane(rows):
    return jnp.broadcast_to(rows[:, SPAN - 1 :], rows.shape)


def middle_lane(rows):
    return jnp.broadcast_to(rows[:, SPAN // 2 - 1 : SPAN // 2], rows.shape)


def masks():
    i = lax.broadcasted_iota(jnp.int32, (SPAN, SPAN), 0)
    j = lax.broadcasted_iota(jnp.int32, (SPAN, SPAN), 1)
    return i >= j, i <= j


def join_rows(rows, blocks):
    return jnp.concatenate([rows[n : n + 1] for n in range(blocks)], axis=1)


def piece_store(ref, at, state, extra):
    pair, which = divmod(at, 2)
    ref[pair, which * DH : (which + 1) * DH, :] = state
    ref[pair, STATES + 4 * which : STATES + 4 * which + 4, :] = extra[:4]


def piece_state(ref, at):
    pair, which = divmod(at, 2)
    return ref[pair, which * DH : (which + 1) * DH, :]


def each_state(piece):
    return [(slice(w * DH, (w + 1) * DH), slice(STATES + 4 * w, STATES + 4 * w + 1)) for w in range(2)]


def extra_rows(decay, gain_row=None):
    place = lax.broadcasted_iota(jnp.int32, (ROWS, DH), 0)
    rest = 0.0 if gain_row is None else jnp.where(place == 1, gain_row, 0.0)
    return jnp.where(place == 0, decay, rest)


def position():
    place = lax.axis_index("seq")
    return lax.rem(place, 2), lax.rem(place // 2, ALONG_Z), place // (2 * ALONG_Z)


def half_heads(core, of_other, at, heads):
    half = heads // 2
    start = (1 - core) if of_other else core
    return start * half + at


def decay_tables(log_ref, cum_ref, before_ref, total_ref):
    heads, rows = log_ref.shape
    _, triangle = masks()
    triangle = triangle.astype(F32)
    cum_ref[...] = jnp.zeros_like(cum_ref)
    before_ref[...] = jnp.zeros_like(before_ref)
    before = jnp.zeros((heads, SPAN), F32)
    for n in range(rows // SPAN):
        cum = dot(log_ref[:, span(n)], triangle, (1, 0), EXACT)
        for h in range(heads):
            cum_ref[h * ROWS + n : h * ROWS + n + 1, :] = cum[h : h + 1]
            before_ref[h * ROWS + n : h * ROWS + n + 1, :] = before[h : h + 1]
        before = before + last_lane(cum)
    for h in range(heads):
        total_ref[h * ROWS : (h + 1) * ROWS, :] = jnp.broadcast_to(before[h : h + 1], (ROWS, SPAN))


def state_body(of_other, *refs):
    core, _, _ = position()
    if of_other:
        k_hbm, v_hbm, log_hbm, out_ref, k_ref, v_ref, cum_ref, before_ref, total_ref, sems, log_ref, log_sem = refs
    else:
        k_ref, v_ref, cum_ref, before_ref, total_ref, out_ref = refs
    rows, width = k_ref.shape
    heads, blocks = width // DH, rows // SPAN
    copies = []
    if of_other:
        log_copy = pltpu.make_async_copy(log_hbm, log_ref, log_sem)
        log_copy.start()
        for g in range(heads // GROUP):
            lanes = head_lanes(lax.rem(half_heads(core, True, g * GROUP, heads), heads), GROUP)
            for which, (source, target) in enumerate(((k_hbm, k_ref), (v_hbm, v_ref))):
                copies.append(pltpu.make_async_copy(source.at[:, lanes], target.at[:, lanes], sems.at[which, g]))
                copies[-1].start()
        log_copy.wait()
        decay_tables(log_ref, cum_ref, before_ref, total_ref)

    for g in range(heads // 2 // GROUP):
        first = half_heads(core, of_other, g * GROUP, heads)
        if of_other:
            copies[2 * g].wait()
            copies[2 * g + 1].wait()
        totals = [head_rows(total_ref, first + at) for at in range(GROUP)]
        scales = [
            jnp.exp(totals[at] - head_rows(before_ref, first + at) - head_rows(cum_ref, first + at)) for at in range(GROUP)
        ]
        decayed = [
            (k_ref[:, head_lanes(first + at)].T.astype(F32) * join_rows(scales[at], blocks)).astype(BF16)
            for at in range(GROUP)
        ]
        states = [nn(decayed[at], v_ref[:, head_lanes(first + at)]) for at in range(GROUP)]
        for at in range(GROUP):
            piece_store(out_ref, g * GROUP + at, states[at], extra_rows(jnp.exp(totals[at])))
    for copy in copies[heads // GROUP :]:
        copy.wait()


def local_state(of_other, keys, values, more):
    rows, width = keys.shape
    heads = width // DH
    pieces = jax.ShapeDtypeStruct((heads // 4, PIECE, DH), F32)
    table = jax.ShapeDtypeStruct((heads * ROWS, SPAN), F32)
    like = jax.ShapeDtypeStruct(keys.shape, BF16)
    if of_other:
        specs, outs = [HBM] * 3, [pieces, like, like, table, table, table]
        scratch = [
            pltpu.SemaphoreType.DMA((2, heads // GROUP)),
            pltpu.VMEM(more[0].shape, F32),
            pltpu.SemaphoreType.DMA,
        ]
    else:
        specs, outs, scratch = [VMEM] * 5, [pieces], []
    return pl.pallas_call(
        functools.partial(state_body, of_other),
        in_specs=specs,
        out_specs=[VMEM] * len(outs),
        out_shape=outs,
        scratch_shapes=scratch,
        compiler_params=params(4),
        cost_estimate=cost(heads * rows * DH * DH, 2 * rows * heads * DH),
        name="state_given" if of_other else "state_kept",
    )(keys, values, *more)


def arrival_order(count):
    return [0] + sorted(range(1, count), key=lambda s: -min(s, count - s))


def join_extra(a, b):
    decays = lax.broadcasted_iota(jnp.int32, (ROWS, DH), 0) % 4 == 0
    return jnp.where(decays, a * b, a + b)


def cores_body(reverse, own_ref, got_ref, *out_refs):
    core, z, _ = position()
    near_here = (core == 0) != reverse
    for shift, out_ref in enumerate(out_refs):
        pair = lax.rem(z + shift, ALONG_Z)
        own, got = own_ref[pair], got_ref[pair]
        near, far = jnp.where(near_here, own, got), jnp.where(near_here, got, own)
        for rows, decay in each_state(near):
            out_ref[rows, :] = far[decay] * near[rows] + far[rows]
        out_ref[STATES:, :] = join_extra(near[STATES:], far[STATES:])


def along_z_body(reverse, *refs):
    in_refs, (_, total_ref, prefix_ref, slots) = refs[:ALONG_Z], refs[ALONG_Z:]
    _, z, _ = position()
    for shift, ref in zip(arrival_order(len(in_refs)), in_refs):
        slots[lax.rem(z - shift + ALONG_Z, ALONG_Z)] = ref[...]
    laps = [ALONG_Z - 1 - lap if reverse else lap for lap in range(ALONG_Z)]
    for rows, decay in each_state(total_ref):
        state = jnp.zeros((DH, DH), F32)
        for at in laps:
            prefix_ref[at, rows, :] = state
            state = slots[at, decay, :] * state + slots[at, rows, :]
        total_ref[rows, :] = state
    extra = jnp.where(lax.broadcasted_iota(jnp.int32, (ROWS, DH), 0) % 4 == 0, 1.0, 0.0)
    for at in laps:
        prefix_ref[at, STATES:, :] = extra
        extra = join_extra(extra, slots[at, STATES:, :])
    total_ref[STATES:, :] = extra


def along_x_body(reverse, *refs):
    in_refs, prefix_ref, out_refs, slots = refs[:ALONG_X], refs[ALONG_X], refs[ALONG_X + 2 : -1], refs[-1]
    _, z, x = position()
    for shift, ref in zip(arrival_order(len(in_refs)), in_refs):
        slots[lax.rem(x - shift + ALONG_X, ALONG_X)] = ref[...]
    for rows, decay in each_state(prefix_ref):
        state = jnp.zeros((DH, DH), F32)
        for lap in range(ALONG_X):
            at = ALONG_X - 1 - lap if reverse else lap
            taken = (at > x) if reverse else (at < x)
            state = jnp.where(taken, slots[at, decay, :] * state + slots[at, rows, :], state)
        for shift, out_ref in enumerate(out_refs):
            at = lax.rem(z + shift, ALONG_Z)
            out_ref[rows, :] = prefix_ref[at, rows, :] + prefix_ref[at, decay, :] * state
    if reverse:
        extra = sum(slots[at, STATES:, :] for at in range(ALONG_X))
        for out_ref in out_refs:
            out_ref[STATES:, :] = extra


def entering_body(reverse, *refs):
    in_refs, (own_ref, got_ref, _, keep_ref, give_ref) = refs[:ALONG_Z], refs[ALONG_Z:]
    core, z, _ = position()
    near_here = (core == 0) != reverse
    for shift, ref in zip(arrival_order(len(in_refs)), in_refs):
        pair = lax.rem(z - shift + ALONG_Z, ALONG_Z)
        near = jnp.where(near_here, own_ref[pair], got_ref[pair])
        for rows, decay in each_state(near):
            entering = ref[rows, :]
            passed = near[decay] * entering + near[rows]
            keep_ref[pair, rows, :] = jnp.where(near_here, entering, passed)
            give_ref[pair, rows, :] = jnp.where(near_here, passed, entering)
        if reverse:
            keep_ref[pair, STATES:, :] = ref[STATES:, :]
            give_ref[pair, STATES:, :] = ref[STATES:, :]


def scan_step(body, name, reverse, arrays, after, out_counts, scratch):
    shapes = [jax.ShapeDtypeStruct(shape, F32) for shape in out_counts]
    afters = [] if after is None else [after]
    return pl.pallas_call(
        functools.partial(body, reverse),
        in_specs=[VMEM] * len(arrays) + [ANY] * len(afters),
        out_specs=[VMEM] * len(shapes),
        out_shape=shapes,
        scratch_shapes=scratch,
        compiler_params=params(3),
        cost_estimate=cost(10**6, 10**6),
        name=name,
    )(*arrays, *afters)


def scan_over_seq(send, own, reverse, works):
    count = lax.axis_size("seq")

    def index(x, z, c):
        return (x % ALONG_X * ALONG_Z + z % ALONG_Z) * 2 + c

    every = [(x, z, c) for x in range(ALONG_X) for z in range(ALONG_Z) for c in range(2)]
    across = [(i, i ^ 1) for i in range(count)]
    by_z = [[(index(x, z, c), index(x, z + s, c)) for x, z, c in every] for s in range(ALONG_Z)]
    by_x = [[(index(x, z, c), index(x + s, z, c)) for x, z, c in every] for s in range(ALONG_X)]
    piece = (PIECE, DH)
    back = (PIECE if reverse else STATES, DH)

    def shifted(arrays, moves):
        return [lax.ppermute(arrays[s], "seq", moves[s]) if s else arrays[0] for s in arrival_order(len(moves))]

    got = lax.ppermute(send, "seq", across)
    parts = scan_step(cores_body, "join_cores", reverse, [own, got], None, [piece] * ALONG_Z, [])
    arrived = shifted(parts, by_z)
    done = works[0](parts[0], ())
    total, prefix = scan_step(
        along_z_body, "join_z", reverse, arrived, done[-1],
        [piece, (ALONG_Z,) + piece], [pltpu.VMEM((ALONG_Z,) + piece, F32)],
    )
    totals = shifted([total] * ALONG_X, by_x)
    done = works[1](total, done)
    parts = scan_step(
        along_x_body, "join_x", reverse, totals + [prefix], done[-1],
        [back] * ALONG_Z, [pltpu.VMEM((ALONG_X,) + piece, F32)],
    )
    arrived = shifted(parts, by_z)
    done = works[2](parts[0], done)
    keep, give = scan_step(
        entering_body, "entering", reverse, arrived + [own, got], done[-1], [own.shape[:1] + back] * 2, []
    )
    return keep, lax.ppermute(give, "seq", across), done


def block_picks(blocks):
    part = lax.broadcasted_iota(jnp.int32, (4 * ROWS, blocks * SPAN), 0)
    place = lax.broadcasted_iota(jnp.int32, (4 * ROWS, blocks * SPAN), 1)
    return (lax.rem(part, ROWS) == place // SPAN).astype(BF16)


def spread(rows, picks):
    high = rows.astype(BF16).astype(F32)
    middle = (rows - high).astype(BF16).astype(F32)
    parts = jnp.concatenate([high, middle, rows - high - middle, jnp.zeros_like(rows)], axis=0)
    return nn(parts.T.astype(BF16), picks)


def staggered(stages, steps):
    for at in range(len(steps) + len(stages) - 1):
        for back, stage in enumerate(stages):
            if 0 <= at - back < len(steps):
                stage(*steps[at - back])


def attend_heads(heads, q_ref, k_ref, v_ref, cum_ref, outs, both_masks, picks):
    local_ref, low_ref, turned_ref, qs_ref, ks_ref, vs_ref, weights_ref = outs
    mask, turned_mask = both_masks
    blocks = k_ref.shape[0] // SPAN
    each = range(len(heads))
    steps = [(a, n) for n in range(blocks) for a in each]
    lanes = [head_lanes(h) for h in heads]
    cums = [head_rows(cum_ref, h) for h in heads]
    mids = [middle_lane(c) for c in cums]
    ends = [last_lane(c) for c in cums]
    shifts = [spread(c - m, picks) for c, m in zip(cums, mids)]
    mid_scale, end_scale = [jnp.exp(m) for m in mids], [jnp.exp(e) for e in ends]
    rest_scale = [jnp.exp(e - m) for e, m in zip(ends, mids)]
    q_up, k_up, q_turned, k_turned, scores, turned_weights, updates, weights, lows, totals = ({} for _ in range(10))
    state = {a: jnp.zeros((DH, DH), F32) for a in each}

    def scale(a, n):
        shift = shifts[a][:, span(n)]
        up, down = jnp.exp(shift), jnp.exp(-shift)
        q_up[a, n] = (q_ref[span(n), lanes[a]].astype(F32) * up).astype(BF16)
        k_up[a, n] = (k_ref[span(n), lanes[a]].astype(F32) * down).astype(BF16)
        vs_ref[span(n), lanes[a]] = (v_ref[span(n), lanes[a]].astype(F32) * down).astype(BF16)
        qs_ref[span(n), lanes[a]] = q_up[a, n]
        ks_ref[span(n), lanes[a]] = k_up[a, n]

    def turn(a, n):
        k_turned[a, n] = k_up[a, n].T
        q_turned[a, n] = q_up[a, n].T
        turned_ref[heads[a], :, span(n)] = q_turned[a, n]

    def multiply(a, n):
        scores[a, n] = nn(q_up[a, n], k_turned[a, n])
        turned_weights[a, n] = nn(k_up[a, n], q_turned[a, n])
        if n < blocks - 1:
            updates[a, n] = nn(k_turned[a, n], v_ref[span(n), lanes[a]])

    def mask_out(a, n):
        weights[a, n] = jnp.where(mask, scores[a, n], 0.0).astype(BF16)
        weights_ref[heads[a], n] = jnp.where(turned_mask, turned_weights[a, n], 0.0).astype(BF16)
        lows[a, n] = (mid_scale[a][n : n + 1] * state[a]).astype(BF16)
        low_ref[heads[a], n] = lows[a, n]
        if n < blocks - 1:
            state[a] = end_scale[a][n : n + 1] * state[a] + rest_scale[a][n : n + 1] * updates[a, n]

    def combine(a, n):
        v = v_ref[span(n), lanes[a]]
        if n == 0:
            totals[a, n] = nn(weights[a, n], v)
        else:
            left = jnp.concatenate([weights[a, n], q_up[a, n]], axis=1)
            totals[a, n] = nn(left, jnp.concatenate([v, lows[a, n]], axis=0))

    def store(a, n):
        local_ref[span(n), lanes[a]] = totals[a, n].astype(BF16)

    staggered([scale, turn, multiply, mask_out, combine, store], steps)


def attend_body(first, count, load, *refs):
    k_ref, v_ref, cum_ref = refs[1:4]
    refs = refs[4:]
    copies = []
    if load == "queries":
        q_hbm, outs, (q_ref, sems) = refs[0], refs[1:8], refs[8:]
        for g in range(q_hbm.shape[1] // (GROUP * DH)):
            lanes = slice(g * GROUP * DH, (g + 1) * GROUP * DH)
            copies.append(pltpu.make_async_copy(q_hbm.at[:, lanes], q_ref.at[:, lanes], sems.at[g]))
    elif load == "grad_out":
        q_ref, go_hbm, outs, (go_ref, sems) = refs[0], refs[1], refs[9:16], refs[16:]
        copies.append(pltpu.make_async_copy(go_hbm, go_ref, sems.at[0]))
    else:
        q_ref, outs = refs[0], refs[8:15]
    for copy in copies:
        copy.start()
    both_masks = masks()
    picks = block_picks(k_ref.shape[0] // SPAN)
    held = []
    for at, copy in enumerate(copies):
        if load == "queries" and at * GROUP < first + count:
            copy.wait()
        else:
            held.append(copy)
    attend_heads([first + a for a in range(count)], q_ref, k_ref, v_ref, cum_ref, outs, both_masks, picks)
    for copy in held:
        copy.wait()


def attend(after, first, count, load, keys, values, cum, queries, grad_out, done):
    rows, width = keys.shape
    heads, blocks = width // DH, rows // SPAN
    like = jax.ShapeDtypeStruct((rows, width), BF16)
    squares = jax.ShapeDtypeStruct((heads, blocks, DH, DH), BF16)
    outs = [like, squares, jax.ShapeDtypeStruct((heads, DH, rows), BF16), like, like, like, squares]
    arrays, specs = [after, keys, values, cum, queries], [ANY, VMEM, VMEM, VMEM]
    specs.append(HBM if load == "queries" else VMEM)
    if load == "grad_out":
        arrays.append(grad_out)
        specs.append(HBM)
    aliases = {len(arrays) + i: i for i in range(len(done))}
    if load is not None:
        outs.append(like)
    return pl.pallas_call(
        functools.partial(attend_body, first, count, load),
        in_specs=specs + [VMEM] * len(done),
        out_specs=[VMEM] * len(outs),
        out_shape=outs,
        input_output_aliases=aliases,
        scratch_shapes=[] if load is None else [pltpu.SemaphoreType.DMA((heads // GROUP,))],
        compiler_params=params(6),
        cost_estimate=cost(10 * rows * count * DH * DH, 12 * rows * count * DH),
        name=f"attend_{first}",
    )(*arrays, *done)


def enter_body(of_other, q_ref, local_ref, go_ref, gain_ref, state_ref, cum_ref, before_ref, *refs):
    if of_other:
        attn_ref, low_ref, stats_ref, square_ref, inner_ref = refs[4:]
    else:
        attn_ref, low_ref, square_ref, inner_ref = refs
    core, _, _ = position()
    rows, width = q_ref.shape
    heads, blocks = width // DH, rows // SPAN
    if not of_other:
        square_ref[...] = jnp.zeros_like(square_ref)
        inner_ref[...] = jnp.zeros_like(inner_ref)

    for g in range(heads // 2 // GROUP):
        first = half_heads(core, of_other, g * GROUP, heads)
        lanes = [head_lanes(first + at) for at in range(GROUP)]
        carried, scales, gains = [], [], []
        for at in range(GROUP):
            low = piece_state(state_ref, g * GROUP + at).astype(BF16)
            low_ref[first + at] = low
            carried.append(nn(q_ref[:, lanes[at]], low))
            scales.append(jnp.exp(middle_lane(head_rows(cum_ref, first + at)) + head_rows(before_ref, first + at)))
            gains.append(gain_ref[:, lanes[at]])
        for n in range(blocks):
            square = square_ref[span(n), :]
            inner = inner_ref[span(n), :]
            for at in range(GROUP):
                entered = carried[at][span(n)] * scales[at][n : n + 1]
                attn = (local_ref[span(n), lanes[at]].astype(F32) + entered).astype(BF16)
                attn_ref[span(n), lanes[at]] = attn
                attn = attn.astype(F32)
                square += attn * attn
                inner += go_ref[span(n), lanes[at]].astype(F32) * gains[at] * attn
            square_ref[span(n), :] = square
            inner_ref[span(n), :] = inner

    if of_other:
        ones = jnp.ones((8, DH), F32)
        stats_ref[0:1, :] = dot(ones, square_ref[...], (1, 1), EXACT)[0:1]
        stats_ref[1:2, :] = dot(ones, inner_ref[...], (1, 1), EXACT)[0:1]


def attend_entering(of_other, queries, local, grad_out, gain, state, cum, before, done):
    rows, width = queries.shape
    heads = width // DH
    sums = jax.ShapeDtypeStruct((rows, DH), F32)
    outs = [jax.ShapeDtypeStruct((rows, width), BF16), jax.ShapeDtypeStruct((heads, DH, DH), BF16)]
    if of_other:
        outs, aliases = outs + [jax.ShapeDtypeStruct((2, rows), F32), sums, sums], {7: 0, 8: 1, 9: 3, 10: 4}
    else:
        outs, aliases = outs + [sums, sums], {}
    return pl.pallas_call(
        functools.partial(enter_body, of_other),
        in_specs=[VMEM] * (7 + len(done)),
        out_specs=[VMEM] * len(outs),
        out_shape=outs,
        input_output_aliases=aliases,
        compiler_params=params(4),
        cost_estimate=cost(rows * width * DH, 4 * rows * width),
        name="enter_taken" if of_other else "enter_kept",
    )(queries, local, grad_out, gain, state, cum, before, *done)


def columns(row, ref, blocks):
    for n in range(blocks):
        ref[span(n), :] = jnp.broadcast_to(row[:, span(n)], (SPAN, SPAN)).T


def norm_body(of_other, turned_ref, attn_ref, go_ref, gain_ref, cum_ref, before_ref, total_ref, *refs):
    core, _, _ = position()
    rows, width = attn_ref.shape
    heads, blocks = width // DH, rows // SPAN
    if of_other:
        stats_refs, (ga_ref, out_ref, inverse_ref, factor_ref) = refs[:-4], refs[-4:]
        stats = functools.reduce(jnp.add, [ref[...] for ref in stats_refs]) / (HEAD_TOTAL * DH)
        inverse = lax.rsqrt(stats[0:1] + 1e-06)
        columns(inverse, inverse_ref, blocks)
        columns(inverse * inverse * inverse * stats[1:2], factor_ref, blocks)
    else:
        inverse_ref, factor_ref, _, ga_ref, out_ref = refs

    for g in range(heads // 2 // GROUP):
        places = [g * GROUP + at for at in range(GROUP)]
        heads_now = [half_heads(core, of_other, place, heads) for place in places]
        lanes = [head_lanes(head) for head in heads_now]
        gains = [gain_ref[:, lane] for lane in lanes]
        gain_sums = [jnp.zeros((8, DH), F32) for _ in places]
        grads = [[] for _ in places]
        for n in range(blocks):
            for at in range(GROUP):
                attn = attn_ref[span(n), lanes[at]].astype(F32)
                scaled = go_ref[span(n), lanes[at]].astype(F32) * inverse_ref[span(n), :]
                gain_sums[at] += jnp.sum((scaled * attn).reshape(SPAN // 8, 8, DH), axis=0)
                grad = (scaled * gains[at] - attn * factor_ref[span(n), :]).astype(BF16)
                ga_ref[span(n), lanes[at]] = grad
                grads[at].append(grad)
        updates = [
            [nn(turned_ref[heads_now[at], :, span(n)], grads[at][n]) for n in range(blocks)] for at in range(GROUP)
        ]
        scales = [jnp.exp(middle_lane(head_rows(cum_ref, h)) + head_rows(before_ref, h)) for h in heads_now]
        states = [sum(scales[at][n : n + 1] * updates[at][n] for n in range(blocks)) for at in range(GROUP)]
        for at in range(GROUP):
            decay = jnp.exp(head_rows(total_ref, heads_now[at]))
            piece_store(out_ref, places[at], states[at], extra_rows(decay, jnp.sum(gain_sums[at], axis=0, keepdims=True)))


def norm_backward(of_other, turned, attn, grad_out, gain, cum, before, total, more):
    rows, width = attn.shape
    heads = width // DH
    pieces = jax.ShapeDtypeStruct((heads // 4, PIECE, DH), F32)
    cols = jax.ShapeDtypeStruct((rows, DH), F32)
    outs = [jax.ShapeDtypeStruct((rows, width), BF16), pieces] + ([cols, cols] if of_other else [])
    return pl.pallas_call(
        functools.partial(norm_body, of_other),
        in_specs=[VMEM] * (7 + len(more)),
        out_specs=[VMEM] * len(outs),
        out_shape=outs,
        input_output_aliases={} if of_other else {9: 0},
        compiler_params=params(5),
        cost_estimate=cost(rows * width * DH, 4 * rows * width),
        name="norm_given" if of_other else "norm_kept",
    )(turned, attn, grad_out, gain, cum, before, total, *more)


def grads_heads(heads, places, refs, out_ref, gq_ref, lk_ref, lv_ref, both_masks, picks, send):
    q_ref, k_ref, turned_ref, ks_ref, vs_ref, weights_ref, ga_ref, attn_ref = refs[:8]
    gain_ref, inverse_ref, low_ref, enter_ref, cum_ref, before_ref = refs[8:]
    mask, _ = both_masks
    blocks = k_ref.shape[0] // SPAN
    each = range(len(heads))
    steps = [(a, n) for n in range(blocks) for a in each]
    lanes = [head_lanes(h) for h in heads]
    here = [head_lanes(p) for p in places]
    cums = [head_rows(cum_ref, h) for h in heads]
    mids = [middle_lane(c) for c in cums]
    ends = [last_lane(c) for c in cums]
    query_scale = [jnp.exp(spread(c - m, picks)) for c, m in zip(cums, mids)]
    mid_scale, end_scale = [jnp.exp(m) for m in mids], [jnp.exp(e) for e in ends]
    rest_scale = [jnp.exp(e - m) for e, m in zip(ends, mids)]
    enter_scale = [jnp.exp(m + head_rows(before_ref, h)) for m, h in zip(mids, heads)]
    entering = [enter_ref[h].astype(F32) for h in heads]

    def at(ref, a, n):
        return ref[span(n), lanes[a]]

    ga_up, v_turned, states, scores, updates, weights, lows, lows_turned, grad_q, grad_k, grad_v = ({} for _ in range(11))
    back = {a: jnp.zeros((DH, DH), F32) for a in each}

    def scale(a, n):
        ga_up[a, n] = (at(ga_ref, a, n).astype(F32) * query_scale[a][:, span(n)]).astype(BF16)
        v_turned[a, n] = at(vs_ref, a, n).T
        state = low_ref[heads[a], n].astype(F32) + enter_scale[a][n : n + 1] * entering[a]
        states[a, n] = state.astype(BF16).T

    def multiply(a, n):
        scores[a, n] = nn(ga_up[a, n], v_turned[a, n])
        if n > 0:
            updates[a, n] = nn(turned_ref[heads[a], :, span(n)], at(ga_ref, a, n))

    def mask_out(a, n):
        scores[a, n] = jnp.where(mask, scores[a, n], 0.0).astype(BF16)
        weights[a, n] = scores[a, n].T
        if n < blocks - 1:
            lows[a, n] = (rest_scale[a][n : n + 1] * back[a]).astype(BF16)
            lows_turned[a, n] = lows[a, n].T
        if n > 0:
            back[a] = end_scale[a][n : n + 1] * back[a] + mid_scale[a][n : n + 1] * updates[a, n]

    def combine(a, n):
        left = jnp.concatenate([scores[a, n], ga_up[a, n]], axis=1)
        grad_q[a, n] = nn(left, jnp.concatenate([at(k_ref, a, n), states[a, n]], axis=0))
        left_k, right_k = weights[a, n], at(q_ref, a, n)
        left_v, right_v = weights_ref[heads[a], n], at(ga_ref, a, n)
        if n < blocks - 1:
            left_k = jnp.concatenate([left_k, at(vs_ref, a, n)], axis=1)
            right_k = jnp.concatenate([right_k, lows_turned[a, n]], axis=0)
            left_v = jnp.concatenate([left_v, at(ks_ref, a, n)], axis=1)
            right_v = jnp.concatenate([right_v, lows[a, n]], axis=0)
        grad_k[a, n] = nn(left_k, right_k)
        grad_v[a, n] = nn(left_v, right_v)

    def store(a, n):
        gq_ref[span(n), here[a]] = grad_q[a, n].astype(BF16)
        lv_ref[span(n), lanes[a]] = grad_v[a, n].astype(BF16)
        lk_ref[span(n), lanes[a]] = grad_k[a, n].astype(BF16)
        normed = at(attn_ref, a, n).astype(F32) * inverse_ref[span(n), :]
        out_ref[span(n), here[a]] = (normed * gain_ref[:, lanes[a]]).astype(BF16)
        if a == 0:
            send(n)

    staggered([scale, multiply, mask_out, combine, store], steps[::-1])


def grads_body(first, count, chained, *refs):
    inputs = refs[1:15]
    refs = refs[15 + (4 if chained else 0) :]
    out_hbm, gq_hbm, lk_ref, lv_ref, out_ref, gq_ref, sems = refs
    both_masks = masks()
    picks = block_picks(inputs[0].shape[0] // SPAN)

    copies = []

    def send(n):
        lanes = slice(first * DH, (first + count) * DH)
        for which, (source, target) in enumerate(((out_ref, out_hbm), (gq_ref, gq_hbm))):
            copies.append(pltpu.make_async_copy(source.at[span(n), :], target.at[span(n), lanes], sems.at[which, n]))
            copies[-1].start()

    heads, places = [first + a for a in range(count)], list(range(count))
    grads_heads(heads, places, inputs, out_ref, gq_ref, lk_ref, lv_ref, both_masks, picks, send)
    for copy in copies:
        copy.wait()


def grads_local(after, first, count, inputs, done):
    rows, width = inputs[0].shape
    like = jax.ShapeDtypeStruct((rows, width), BF16)
    kinds = [HBM, HBM, VMEM, VMEM]
    return pl.pallas_call(
        functools.partial(grads_body, first, count, bool(done)),
        in_specs=[ANY] + [VMEM] * 14 + (kinds if done else []),
        out_specs=kinds,
        out_shape=[like] * 4,
        input_output_aliases={15 + i: i for i in range(4)} if done else {},
        scratch_shapes=[
            pltpu.VMEM((rows, count * DH), BF16),
            pltpu.VMEM((rows, count * DH), BF16),
            pltpu.SemaphoreType.DMA((2, rows // SPAN)),
        ],
        compiler_params=params(8),
        cost_estimate=cost(22 * rows * count * DH * DH, 24 * rows * count * DH),
        name=f"grads_{first}",
    )(after, *inputs, *done)


def leave_body(of_other, k_ref, v_ref, lk_ref, lv_ref, state_ref, cum_ref, before_ref, total_ref, *refs):
    core, _, _ = position()
    rows, width = k_ref.shape
    heads, blocks = width // DH, rows // SPAN
    half = heads // 2
    copies = []
    if of_other:
        kept_k_ref, kept_v_ref, kept_gain_ref, gk_hbm, gv_hbm, gg_ref, gk_ref, gv_ref, sems, kept_sems = refs
        there = head_lanes(half_heads(core, False, 0, heads), half)
        for which, (source, target) in enumerate(((kept_k_ref, gk_hbm), (kept_v_ref, gv_hbm))):
            copies.append(pltpu.make_async_copy(source, target.at[:, there], kept_sems.at[which]))
            copies[-1].start()
        gg_ref[...] = kept_gain_ref[...]
    else:
        gk_ref, gv_ref, gg_ref = refs
    for g in range(half // GROUP):

        for at in range(g * GROUP // PAIR, (g + 1) * GROUP // PAIR):
            first = half_heads(core, of_other, at * PAIR, heads)
            lanes = [head_lanes(first + a) for a in range(PAIR)]
            here = [head_lanes(at * PAIR + a) for a in range(PAIR)]
            lows = [piece_state(state_ref, at * PAIR + a).astype(BF16) for a in range(PAIR)]
            from_v = [nt(v_ref[:, lanes[a]], lows[a]) for a in range(PAIR)]
            from_k = [nn(k_ref[:, lanes[a]], lows[a]) for a in range(PAIR)]
            scales = [
                jnp.exp(
                    head_rows(total_ref, first + a)
                    - head_rows(before_ref, first + a)
                    - middle_lane(head_rows(cum_ref, first + a))
                )
                for a in range(PAIR)
            ]
            for n in range(blocks):
                for a in range(PAIR):
                    factor = scales[a][n : n + 1]
                    grad_k = lk_ref[span(n), lanes[a]].astype(F32) + factor * from_v[a][span(n)]
                    grad_v = lv_ref[span(n), lanes[a]].astype(F32) + factor * from_k[a][span(n)]
                    gk_ref[span(n), here[a]] = grad_k.astype(BF16)
                    gv_ref[span(n), here[a]] = grad_v.astype(BF16)
            for a in range(PAIR):
                row = STATES + 4 * (a % 2) + 1
                gg_ref[:, lanes[a]] = state_ref[at * PAIR // 2 + a // 2, row : row + 1, :]

        if of_other:
            here = slice(g * GROUP * DH, (g + 1) * GROUP * DH)
            there = head_lanes(half_heads(core, True, g * GROUP, heads), GROUP)
            for which, (source, target) in enumerate(((gk_ref, gk_hbm), (gv_ref, gv_hbm))):
                copies.append(pltpu.make_async_copy(source.at[:, here], target.at[:, there], sems.at[which, g]))
                copies[-1].start()
    for copy in copies:
        copy.wait()


def grads_leaving(of_other, keys, values, local_k, local_v, state, cum, before, total, done):
    rows, width = keys.shape
    heads = width // DH
    like = jax.ShapeDtypeStruct((rows, width if of_other else width // 2), BF16)
    kept = pltpu.VMEM((rows, width // 2), BF16)
    sems = [pltpu.SemaphoreType.DMA((2, heads // 2 // GROUP)), pltpu.SemaphoreType.DMA((2,))]
    return pl.pallas_call(
        functools.partial(leave_body, of_other),
        in_specs=[VMEM] * (8 + len(done)),
        out_specs=[HBM, HBM, VMEM] if of_other else [VMEM] * 3,
        out_shape=[like, like, jax.ShapeDtypeStruct((1, width), F32)],
        scratch_shapes=[kept, kept] + sems if of_other else [],
        compiler_params=params(6),
        cost_estimate=cost(2 * rows * width * DH, 6 * rows * width),
        name="leave_taken" if of_other else "leave_kept",
    )(keys, values, local_k, local_v, state, cum, before, total, *done)


def per_device(queries, keys, values, log_decay, gain, grad_out):
    gain_row = gain.reshape(1, -1)
    keys, values, queries, grad_out, log_decay = (
        pltpu.with_memory_space_constraint(a, pltpu.HBM) for a in (keys, values, queries, grad_out, log_decay)
    )
    send, keys, values, cum, before, total = local_state(True, keys, values, (log_decay,))
    (own,) = local_state(False, keys, values, (cum, before, total))

    def attend_part(first, count, load):
        def run(after, done):
            held = done[7] if done else queries
            outs = attend(after, first, count, load, keys, values, cum, held, grad_out, done[:7])
            if load == "queries":
                return (*outs[:7], outs[7], outs[0])
            if load == "grad_out":
                return (*outs[:7], held, outs[7], outs[0])
            return (*outs[:7], held, done[8], outs[0])

        return run

    keep, taken, (local, lows, turned, q_up, k_up, v_up, weights, queries, grad_out, _) = scan_over_seq(
        send, own, False, [attend_part(0, 6, "queries"), attend_part(6, 6, "grad_out"), attend_part(12, 4, None)]
    )
    table = (cum, before)
    done = attend_entering(False, q_up, local, grad_out, gain_row, keep, *table, ())
    attn, entering, stats = attend_entering(True, q_up, local, grad_out, gain_row, taken, *table, done)[:3]
    count = lax.axis_size("head")
    stats = [stats] + [
        lax.ppermute(stats, "head", [(i, (i + s) % count) for i in range(count)]) for s in arrival_order(count)[1:]
    ]
    shared = (turned, attn, grad_out, gain_row, cum, before, total)
    grad_attn, send, inverse, factor = norm_backward(True, *shared, stats)
    grad_attn, own = norm_backward(False, *shared, (inverse, factor, grad_attn))
    inputs = (queries, keys, turned, k_up, v_up, weights, grad_attn, attn, gain_row, inverse, lows, entering, cum, before)

    def grads_part(first, count):
        return lambda after, done: grads_local(after, first, count, inputs, done)

    keep, taken, (output, grad_q, local_k, local_v) = scan_over_seq(
        send, own, True, [grads_part(0, 6), grads_part(6, 6), grads_part(12, 4)]
    )
    shared = (k_up, v_up, local_k, local_v)
    done = grads_leaving(False, *shared, keep, cum, before, total, ())
    grad_k, grad_v, grad_gain = grads_leaving(True, *shared, taken, cum, before, total, done)
    return output, grad_q, grad_k, grad_v, grad_gain.reshape(-1)


def solution(mesh):
    tokens, heads = P("seq", "head"), P("head")
    return jax.shard_map(
        per_device,
        mesh=mesh,
        in_specs=(tokens, tokens, tokens, P("head", "seq"), heads, tokens),
        out_specs=(tokens, tokens, tokens, tokens, heads),
        check_vma=False,
    )
```

```python
import functools

import jax
import jax.numpy as jnp
from jax import lax
from jax.experimental import pallas as pl
from jax.experimental.pallas import tpu as pltpu
from jax.sharding import PartitionSpec as P

HEAD_TOTAL = 64
DH = 128
SPAN = 128
ROWS = 8
STATES = 2 * DH
PIECE = STATES + ROWS
GROUP = 4
PAIR = 2
ALONG_X, ALONG_Z = 4, 4
F32 = jnp.float32
BF16 = jnp.bfloat16
EXACT = lax.Precision.HIGHEST
VMEM = pl.BlockSpec(memory_space=pltpu.VMEM)
HBM = pl.BlockSpec(memory_space=pltpu.HBM)
ANY = pl.BlockSpec(memory_space=pl.ANY)


def dot(a, b, contract, precision=None):
    return lax.dot_general(
        a, b, ((contract[:1], contract[1:]), ((), ())), precision=precision, preferred_element_type=F32
    )


def nn(a, b):
    return dot(a, b, (1, 0))


def nt(a, b):
    return dot(a, b, (1, 1))


def params(mib):
    return pltpu.CompilerParams(vmem_limit_bytes=mib * 1024 * 1024)


def cost(flops, nbytes):
    return pl.CostEstimate(flops=int(flops), bytes_accessed=int(nbytes), transcendentals=0)


def head_rows(ref, head):
    return ref[pl.ds(pl.multiple_of(head * ROWS, ROWS), ROWS), :]


def head_lanes(head, count=1):
    return pl.ds(pl.multiple_of(head * DH, DH), count * DH)


def span(n):
    return slice(n * SPAN, (n + 1) * SPAN)


def last_lane(rows):
    return jnp.broadcast_to(rows[:, SPAN - 1 :], rows.shape)


def middle_lane(rows):
    return jnp.broadcast_to(rows[:, SPAN // 2 - 1 : SPAN // 2], rows.shape)


def masks():
    i = lax.broadcasted_iota(jnp.int32, (SPAN, SPAN), 0)
    j = lax.broadcasted_iota(jnp.int32, (SPAN, SPAN), 1)
    return i >= j, i <= j


def join_rows(rows, blocks):
    return jnp.concatenate([rows[n : n + 1] for n in range(blocks)], axis=1)


def piece_store(ref, at, state, extra):
    pair, which = divmod(at, 2)
    ref[pair, which * DH : (which + 1) * DH, :] = state
    ref[pair, STATES + 4 * which : STATES + 4 * which + 4, :] = extra[:4]


def piece_state(ref, at):
    pair, which = divmod(at, 2)
    return ref[pair, which * DH : (which + 1) * DH, :]


def each_state(piece):
    return [(slice(w * DH, (w + 1) * DH), slice(STATES + 4 * w, STATES + 4 * w + 1)) for w in range(2)]


def extra_rows(decay, gain_row=None):
    place = lax.broadcasted_iota(jnp.int32, (ROWS, DH), 0)
    rest = 0.0 if gain_row is None else jnp.where(place == 1, gain_row, 0.0)
    return jnp.where(place == 0, decay, rest)


def position():
    place = lax.axis_index("seq")
    return lax.rem(place, 2), lax.rem(place // 2, ALONG_Z), place // (2 * ALONG_Z)


def half_heads(core, of_other, at, heads):
    half = heads // 2
    start = (1 - core) if of_other else core
    return start * half + at


def decay_tables(log_ref, cum_ref, before_ref, total_ref):
    heads, rows = log_ref.shape
    _, triangle = masks()
    triangle = triangle.astype(F32)
    cum_ref[...] = jnp.zeros_like(cum_ref)
    before_ref[...] = jnp.zeros_like(before_ref)
    before = jnp.zeros((heads, SPAN), F32)
    for n in range(rows // SPAN):
        cum = dot(log_ref[:, span(n)], triangle, (1, 0), EXACT)
        for h in range(heads):
            cum_ref[h * ROWS + n : h * ROWS + n + 1, :] = cum[h : h + 1]
            before_ref[h * ROWS + n : h * ROWS + n + 1, :] = before[h : h + 1]
        before = before + last_lane(cum)
    for h in range(heads):
        total_ref[h * ROWS : (h + 1) * ROWS, :] = jnp.broadcast_to(before[h : h + 1], (ROWS, SPAN))


def state_body(of_other, *refs):
    core, _, _ = position()
    if of_other:
        k_hbm, v_hbm, log_hbm, out_ref, k_ref, v_ref, cum_ref, before_ref, total_ref, sems, log_ref, log_sem = refs
    else:
        k_ref, v_ref, cum_ref, before_ref, total_ref, out_ref = refs
    rows, width = k_ref.shape
    heads, blocks = width // DH, rows // SPAN
    copies = []
    if of_other:
        log_copy = pltpu.make_async_copy(log_hbm, log_ref, log_sem)
        log_copy.start()
        for g in range(heads // GROUP):
            lanes = head_lanes(lax.rem(half_heads(core, True, g * GROUP, heads), heads), GROUP)
            for which, (source, target) in enumerate(((k_hbm, k_ref), (v_hbm, v_ref))):
                copies.append(pltpu.make_async_copy(source.at[:, lanes], target.at[:, lanes], sems.at[which, g]))
                copies[-1].start()
        log_copy.wait()
        decay_tables(log_ref, cum_ref, before_ref, total_ref)

    for g in range(heads // 2 // GROUP):
        first = half_heads(core, of_other, g * GROUP, heads)
        if of_other:
            copies[2 * g].wait()
            copies[2 * g + 1].wait()
        totals = [head_rows(total_ref, first + at) for at in range(GROUP)]
        scales = [
            jnp.exp(totals[at] - head_rows(before_ref, first + at) - head_rows(cum_ref, first + at)) for at in range(GROUP)
        ]
        decayed = [
            (k_ref[:, head_lanes(first + at)].T.astype(F32) * join_rows(scales[at], blocks)).astype(BF16)
            for at in range(GROUP)
        ]
        states = [nn(decayed[at], v_ref[:, head_lanes(first + at)]) for at in range(GROUP)]
        for at in range(GROUP):
            piece_store(out_ref, g * GROUP + at, states[at], extra_rows(jnp.exp(totals[at])))
    for copy in copies[heads // GROUP :]:
        copy.wait()


def local_state(of_other, keys, values, more):
    rows, width = keys.shape
    heads = width // DH
    pieces = jax.ShapeDtypeStruct((heads // 4, PIECE, DH), F32)
    table = jax.ShapeDtypeStruct((heads * ROWS, SPAN), F32)
    like = jax.ShapeDtypeStruct(keys.shape, BF16)
    if of_other:
        specs, outs = [HBM] * 3, [pieces, like, like, table, table, table]
        scratch = [
            pltpu.SemaphoreType.DMA((2, heads // GROUP)),
            pltpu.VMEM(more[0].shape, F32),
            pltpu.SemaphoreType.DMA,
        ]
    else:
        specs, outs, scratch = [VMEM] * 5, [pieces], []
    return pl.pallas_call(
        functools.partial(state_body, of_other),
        in_specs=specs,
        out_specs=[VMEM] * len(outs),
        out_shape=outs,
        scratch_shapes=scratch,
        compiler_params=params(4),
        cost_estimate=cost(heads * rows * DH * DH, 2 * rows * heads * DH),
        name="state_given" if of_other else "state_kept",
    )(keys, values, *more)


def arrival_order(count):
    return [0] + sorted(range(1, count), key=lambda s: -min(s, count - s))


def join_extra(a, b):
    decays = lax.broadcasted_iota(jnp.int32, (ROWS, DH), 0) % 4 == 0
    return jnp.where(decays, a * b, a + b)


def cores_body(reverse, own_ref, got_ref, *out_refs):
    core, z, _ = position()
    near_here = (core == 0) != reverse
    for shift, out_ref in enumerate(out_refs):
        pair = lax.rem(z + shift, ALONG_Z)
        own, got = own_ref[pair], got_ref[pair]
        near, far = jnp.where(near_here, own, got), jnp.where(near_here, got, own)
        for rows, decay in each_state(near):
            out_ref[rows, :] = far[decay] * near[rows] + far[rows]
        out_ref[STATES:, :] = join_extra(near[STATES:], far[STATES:])


def along_z_body(reverse, *refs):
    in_refs, (_, total_ref, prefix_ref, slots) = refs[:ALONG_Z], refs[ALONG_Z:]
    _, z, _ = position()
    for shift, ref in zip(arrival_order(len(in_refs)), in_refs):
        slots[lax.rem(z - shift + ALONG_Z, ALONG_Z)] = ref[...]
    laps = [ALONG_Z - 1 - lap if reverse else lap for lap in range(ALONG_Z)]
    for rows, decay in each_state(total_ref):
        state = jnp.zeros((DH, DH), F32)
        for at in laps:
            prefix_ref[at, rows, :] = state
            state = slots[at, decay, :] * state + slots[at, rows, :]
        total_ref[rows, :] = state
    extra = jnp.where(lax.broadcasted_iota(jnp.int32, (ROWS, DH), 0) % 4 == 0, 1.0, 0.0)
    for at in laps:
        prefix_ref[at, STATES:, :] = extra
        extra = join_extra(extra, slots[at, STATES:, :])
    total_ref[STATES:, :] = extra


def along_x_body(reverse, *refs):
    in_refs, prefix_ref, out_refs, slots = refs[:ALONG_X], refs[ALONG_X], refs[ALONG_X + 2 : -1], refs[-1]
    _, z, x = position()
    for shift, ref in zip(arrival_order(len(in_refs)), in_refs):
        slots[lax.rem(x - shift + ALONG_X, ALONG_X)] = ref[...]
    for rows, decay in each_state(prefix_ref):
        state = jnp.zeros((DH, DH), F32)
        for lap in range(ALONG_X):
            at = ALONG_X - 1 - lap if reverse else lap
            taken = (at > x) if reverse else (at < x)
            state = jnp.where(taken, slots[at, decay, :] * state + slots[at, rows, :], state)
        for shift, out_ref in enumerate(out_refs):
            at = lax.rem(z + shift, ALONG_Z)
            out_ref[rows, :] = prefix_ref[at, rows, :] + prefix_ref[at, decay, :] * state
    if reverse:
        extra = sum(slots[at, STATES:, :] for at in range(ALONG_X))
        for out_ref in out_refs:
            out_ref[STATES:, :] = extra


def entering_body(reverse, *refs):
    in_refs, (own_ref, got_ref, _, keep_ref, give_ref) = refs[:ALONG_Z], refs[ALONG_Z:]
    core, z, _ = position()
    near_here = (core == 0) != reverse
    for shift, ref in zip(arrival_order(len(in_refs)), in_refs):
        pair = lax.rem(z - shift + ALONG_Z, ALONG_Z)
        near = jnp.where(near_here, own_ref[pair], got_ref[pair])
        for rows, decay in each_state(near):
            entering = ref[rows, :]
            passed = near[decay] * entering + near[rows]
            keep_ref[pair, rows, :] = jnp.where(near_here, entering, passed)
            give_ref[pair, rows, :] = jnp.where(near_here, passed, entering)
        if reverse:
            keep_ref[pair, STATES:, :] = ref[STATES:, :]
            give_ref[pair, STATES:, :] = ref[STATES:, :]


def scan_step(body, name, reverse, arrays, after, out_counts, scratch):
    shapes = [jax.ShapeDtypeStruct(shape, F32) for shape in out_counts]
    afters = [] if after is None else [after]
    return pl.pallas_call(
        functools.partial(body, reverse),
        in_specs=[VMEM] * len(arrays) + [ANY] * len(afters),
        out_specs=[VMEM] * len(shapes),
        out_shape=shapes,
        scratch_shapes=scratch,
        compiler_params=params(3),
        cost_estimate=cost(10**6, 10**6),
        name=name,
    )(*arrays, *afters)


def scan_over_seq(send, own, reverse, works):
    count = lax.axis_size("seq")

    def index(x, z, c):
        return (x % ALONG_X * ALONG_Z + z % ALONG_Z) * 2 + c

    every = [(x, z, c) for x in range(ALONG_X) for z in range(ALONG_Z) for c in range(2)]
    across = [(i, i ^ 1) for i in range(count)]
    by_z = [[(index(x, z, c), index(x, z + s, c)) for x, z, c in every] for s in range(ALONG_Z)]
    by_x = [[(index(x, z, c), index(x + s, z, c)) for x, z, c in every] for s in range(ALONG_X)]
    piece = (PIECE, DH)
    back = (PIECE if reverse else STATES, DH)

    def shifted(arrays, moves):
        return [lax.ppermute(arrays[s], "seq", moves[s]) if s else arrays[0] for s in arrival_order(len(moves))]

    got = lax.ppermute(send, "seq", across)
    parts = scan_step(cores_body, "join_cores", reverse, [own, got], None, [piece] * ALONG_Z, [])
    arrived = shifted(parts, by_z)
    done = works[0](parts[0], ())
    total, prefix = scan_step(
        along_z_body, "join_z", reverse, arrived, done[-1],
        [piece, (ALONG_Z,) + piece], [pltpu.VMEM((ALONG_Z,) + piece, F32)],
    )
    totals = shifted([total] * ALONG_X, by_x)
    done = works[1](total, done)
    parts = scan_step(
        along_x_body, "join_x", reverse, totals + [prefix], done[-1],
        [back] * ALONG_Z, [pltpu.VMEM((ALONG_X,) + piece, F32)],
    )
    arrived = shifted(parts, by_z)
    done = works[2](parts[0], done)
    keep, give = scan_step(
        entering_body, "entering", reverse, arrived + [own, got], done[-1], [own.shape[:1] + back] * 2, []
    )
    return keep, lax.ppermute(give, "seq", across), done


def block_picks(blocks):
    part = lax.broadcasted_iota(jnp.int32, (4 * ROWS, blocks * SPAN), 0)
    place = lax.broadcasted_iota(jnp.int32, (4 * ROWS, blocks * SPAN), 1)
    return (lax.rem(part, ROWS) == place // SPAN).astype(BF16)


def spread(rows, picks):
    high = rows.astype(BF16).astype(F32)
    middle = (rows - high).astype(BF16).astype(F32)
    parts = jnp.concatenate([high, middle, rows - high - middle, jnp.zeros_like(rows)], axis=0)
    return nn(parts.T.astype(BF16), picks)


def staggered(stages, steps):
    for at in range(len(steps) + len(stages) - 1):
        for back, stage in enumerate(stages):
            if 0 <= at - back < len(steps):
                stage(*steps[at - back])


def attend_heads(heads, q_ref, k_ref, v_ref, cum_ref, outs, both_masks, picks):
    local_ref, low_ref, turned_ref, qs_ref, ks_ref, vs_ref, weights_ref = outs
    mask, turned_mask = both_masks
    blocks = k_ref.shape[0] // SPAN
    each = range(len(heads))
    steps = [(a, n) for n in range(blocks) for a in each]
    lanes = [head_lanes(h) for h in heads]
    cums = [head_rows(cum_ref, h) for h in heads]
    mids = [middle_lane(c) for c in cums]
    ends = [last_lane(c) for c in cums]
    shifts = [spread(c - m, picks) for c, m in zip(cums, mids)]
    mid_scale, end_scale = [jnp.exp(m) for m in mids], [jnp.exp(e) for e in ends]
    rest_scale = [jnp.exp(e - m) for e, m in zip(ends, mids)]
    q_up, k_up, q_turned, k_turned, scores, turned_weights, updates, weights, lows, totals = ({} for _ in range(10))
    state = {a: jnp.zeros((DH, DH), F32) for a in each}

    def scale(a, n):
        shift = shifts[a][:, span(n)]
        up, down = jnp.exp(shift), jnp.exp(-shift)
        q_up[a, n] = (q_ref[span(n), lanes[a]].astype(F32) * up).astype(BF16)
        k_up[a, n] = (k_ref[span(n), lanes[a]].astype(F32) * down).astype(BF16)
        vs_ref[span(n), lanes[a]] = (v_ref[span(n), lanes[a]].astype(F32) * down).astype(BF16)
        qs_ref[span(n), lanes[a]] = q_up[a, n]
        ks_ref[span(n), lanes[a]] = k_up[a, n]

    def turn(a, n):
        k_turned[a, n] = k_up[a, n].T
        q_turned[a, n] = q_up[a, n].T
        turned_ref[heads[a], :, span(n)] = q_turned[a, n]

    def multiply(a, n):
        scores[a, n] = nn(q_up[a, n], k_turned[a, n])
        turned_weights[a, n] = nn(k_up[a, n], q_turned[a, n])
        if n < blocks - 1:
            updates[a, n] = nn(k_turned[a, n], v_ref[span(n), lanes[a]])

    def mask_out(a, n):
        weights[a, n] = jnp.where(mask, scores[a, n], 0.0).astype(BF16)
        weights_ref[heads[a], n] = jnp.where(turned_mask, turned_weights[a, n], 0.0).astype(BF16)
        lows[a, n] = (mid_scale[a][n : n + 1] * state[a]).astype(BF16)
        low_ref[heads[a], n] = lows[a, n]
        if n < blocks - 1:
            state[a] = end_scale[a][n : n + 1] * state[a] + rest_scale[a][n : n + 1] * updates[a, n]

    def combine(a, n):
        v = v_ref[span(n), lanes[a]]
        if n == 0:
            totals[a, n] = nn(weights[a, n], v)
        else:
            left = jnp.concatenate([weights[a, n], q_up[a, n]], axis=1)
            totals[a, n] = nn(left, jnp.concatenate([v, lows[a, n]], axis=0))

    def store(a, n):
        local_ref[span(n), lanes[a]] = totals[a, n].astype(BF16)

    staggered([scale, turn, multiply, mask_out, combine, store], steps)


def attend_body(first, count, load, *refs):
    k_ref, v_ref, cum_ref = refs[1:4]
    refs = refs[4:]
    copies = []
    if load == "queries":
        q_hbm, outs, (q_ref, sems) = refs[0], refs[1:8], refs[8:]
        for g in range(q_hbm.shape[1] // (GROUP * DH)):
            lanes = slice(g * GROUP * DH, (g + 1) * GROUP * DH)
            copies.append(pltpu.make_async_copy(q_hbm.at[:, lanes], q_ref.at[:, lanes], sems.at[g]))
    elif load == "grad_out":
        q_ref, go_hbm, outs, (go_ref, sems) = refs[0], refs[1], refs[9:16], refs[16:]
        copies.append(pltpu.make_async_copy(go_hbm, go_ref, sems.at[0]))
    else:
        q_ref, outs = refs[0], refs[8:15]
    for copy in copies:
        copy.start()
    both_masks = masks()
    picks = block_picks(k_ref.shape[0] // SPAN)
    held = []
    for at, copy in enumerate(copies):
        if load == "queries" and at * GROUP < first + count:
            copy.wait()
        else:
            held.append(copy)

    @pl.loop(0, count // PAIR)
    def _(at):
        heads = [first + at * PAIR + a for a in range(PAIR)]
        attend_heads(heads, q_ref, k_ref, v_ref, cum_ref, outs, both_masks, picks)

    for copy in held:
        copy.wait()


def attend(after, first, count, load, keys, values, cum, queries, grad_out, done):
    rows, width = keys.shape
    heads, blocks = width // DH, rows // SPAN
    like = jax.ShapeDtypeStruct((rows, width), BF16)
    squares = jax.ShapeDtypeStruct((heads, blocks, DH, DH), BF16)
    outs = [like, squares, jax.ShapeDtypeStruct((heads, DH, rows), BF16), like, like, like, squares]
    arrays, specs = [after, keys, values, cum, queries], [ANY, VMEM, VMEM, VMEM]
    specs.append(HBM if load == "queries" else VMEM)
    if load == "grad_out":
        arrays.append(grad_out)
        specs.append(HBM)
    aliases = {len(arrays) + i: i for i in range(len(done))}
    if load is not None:
        outs.append(like)
    return pl.pallas_call(
        functools.partial(attend_body, first, count, load),
        in_specs=specs + [VMEM] * len(done),
        out_specs=[VMEM] * len(outs),
        out_shape=outs,
        input_output_aliases=aliases,
        scratch_shapes=[] if load is None else [pltpu.SemaphoreType.DMA((heads // GROUP,))],
        compiler_params=params(6),
        cost_estimate=cost(10 * rows * count * DH * DH, 12 * rows * count * DH),
        name=f"attend_{first}",
    )(*arrays, *done)


def enter_body(of_other, q_ref, local_ref, go_ref, gain_ref, state_ref, cum_ref, before_ref, *refs):
    if of_other:
        attn_ref, low_ref, stats_ref, square_ref, inner_ref = refs[4:]
    else:
        attn_ref, low_ref, square_ref, inner_ref = refs
    core, _, _ = position()
    rows, width = q_ref.shape
    heads, blocks = width // DH, rows // SPAN
    if not of_other:
        square_ref[...] = jnp.zeros_like(square_ref)
        inner_ref[...] = jnp.zeros_like(inner_ref)

    for g in range(heads // 2 // GROUP):
        first = half_heads(core, of_other, g * GROUP, heads)
        lanes = [head_lanes(first + at) for at in range(GROUP)]
        carried, scales, gains = [], [], []
        for at in range(GROUP):
            low = piece_state(state_ref, g * GROUP + at).astype(BF16)
            low_ref[first + at] = low
            carried.append(nn(q_ref[:, lanes[at]], low))
            scales.append(jnp.exp(middle_lane(head_rows(cum_ref, first + at)) + head_rows(before_ref, first + at)))
            gains.append(gain_ref[:, lanes[at]])
        for n in range(blocks):
            square = square_ref[span(n), :]
            inner = inner_ref[span(n), :]
            for at in range(GROUP):
                entered = carried[at][span(n)] * scales[at][n : n + 1]
                attn = (local_ref[span(n), lanes[at]].astype(F32) + entered).astype(BF16)
                attn_ref[span(n), lanes[at]] = attn
                attn = attn.astype(F32)
                square += attn * attn
                inner += go_ref[span(n), lanes[at]].astype(F32) * gains[at] * attn
            square_ref[span(n), :] = square
            inner_ref[span(n), :] = inner

    if of_other:
        ones = jnp.ones((8, DH), F32)
        stats_ref[0:1, :] = dot(ones, square_ref[...], (1, 1), EXACT)[0:1]
        stats_ref[1:2, :] = dot(ones, inner_ref[...], (1, 1), EXACT)[0:1]


def attend_entering(of_other, queries, local, grad_out, gain, state, cum, before, done):
    rows, width = queries.shape
    heads = width // DH
    sums = jax.ShapeDtypeStruct((rows, DH), F32)
    outs = [jax.ShapeDtypeStruct((rows, width), BF16), jax.ShapeDtypeStruct((heads, DH, DH), BF16)]
    if of_other:
        outs, aliases = outs + [jax.ShapeDtypeStruct((2, rows), F32), sums, sums], {7: 0, 8: 1, 9: 3, 10: 4}
    else:
        outs, aliases = outs + [sums, sums], {}
    return pl.pallas_call(
        functools.partial(enter_body, of_other),
        in_specs=[VMEM] * (7 + len(done)),
        out_specs=[VMEM] * len(outs),
        out_shape=outs,
        input_output_aliases=aliases,
        compiler_params=params(4),
        cost_estimate=cost(rows * width * DH, 4 * rows * width),
        name="enter_taken" if of_other else "enter_kept",
    )(queries, local, grad_out, gain, state, cum, before, *done)


def columns(row, ref, blocks):
    for n in range(blocks):
        ref[span(n), :] = jnp.broadcast_to(row[:, span(n)], (SPAN, SPAN)).T


def norm_body(of_other, turned_ref, attn_ref, go_ref, gain_ref, cum_ref, before_ref, total_ref, *refs):
    core, _, _ = position()
    rows, width = attn_ref.shape
    heads, blocks = width // DH, rows // SPAN
    if of_other:
        stats_refs, (ga_ref, out_ref, inverse_ref, factor_ref) = refs[:-4], refs[-4:]
        stats = functools.reduce(jnp.add, [ref[...] for ref in stats_refs]) / (HEAD_TOTAL * DH)
        inverse = lax.rsqrt(stats[0:1] + 1e-06)
        columns(inverse, inverse_ref, blocks)
        columns(inverse * inverse * inverse * stats[1:2], factor_ref, blocks)
    else:
        inverse_ref, factor_ref, _, ga_ref, out_ref = refs

    for g in range(heads // 2 // GROUP):
        places = [g * GROUP + at for at in range(GROUP)]
        heads_now = [half_heads(core, of_other, place, heads) for place in places]
        lanes = [head_lanes(head) for head in heads_now]
        gains = [gain_ref[:, lane] for lane in lanes]
        gain_sums = [jnp.zeros((8, DH), F32) for _ in places]
        grads = [[] for _ in places]
        for n in range(blocks):
            for at in range(GROUP):
                attn = attn_ref[span(n), lanes[at]].astype(F32)
                scaled = go_ref[span(n), lanes[at]].astype(F32) * inverse_ref[span(n), :]
                gain_sums[at] += jnp.sum((scaled * attn).reshape(SPAN // 8, 8, DH), axis=0)
                grad = (scaled * gains[at] - attn * factor_ref[span(n), :]).astype(BF16)
                ga_ref[span(n), lanes[at]] = grad
                grads[at].append(grad)
        updates = [
            [nn(turned_ref[heads_now[at], :, span(n)], grads[at][n]) for n in range(blocks)] for at in range(GROUP)
        ]
        scales = [jnp.exp(middle_lane(head_rows(cum_ref, h)) + head_rows(before_ref, h)) for h in heads_now]
        states = [sum(scales[at][n : n + 1] * updates[at][n] for n in range(blocks)) for at in range(GROUP)]
        for at in range(GROUP):
            decay = jnp.exp(head_rows(total_ref, heads_now[at]))
            piece_store(out_ref, places[at], states[at], extra_rows(decay, jnp.sum(gain_sums[at], axis=0, keepdims=True)))


def norm_backward(of_other, turned, attn, grad_out, gain, cum, before, total, more):
    rows, width = attn.shape
    heads = width // DH
    pieces = jax.ShapeDtypeStruct((heads // 4, PIECE, DH), F32)
    cols = jax.ShapeDtypeStruct((rows, DH), F32)
    outs = [jax.ShapeDtypeStruct((rows, width), BF16), pieces] + ([cols, cols] if of_other else [])
    return pl.pallas_call(
        functools.partial(norm_body, of_other),
        in_specs=[VMEM] * (7 + len(more)),
        out_specs=[VMEM] * len(outs),
        out_shape=outs,
        input_output_aliases={} if of_other else {9: 0},
        compiler_params=params(5),
        cost_estimate=cost(rows * width * DH, 4 * rows * width),
        name="norm_given" if of_other else "norm_kept",
    )(turned, attn, grad_out, gain, cum, before, total, *more)


def grads_heads(heads, places, refs, out_ref, gq_ref, lk_ref, lv_ref, both_masks, picks):
    q_ref, k_ref, turned_ref, ks_ref, vs_ref, weights_ref, ga_ref, attn_ref = refs[:8]
    gain_ref, inverse_ref, low_ref, enter_ref, cum_ref, before_ref = refs[8:]
    mask, _ = both_masks
    blocks = k_ref.shape[0] // SPAN
    each = range(len(heads))
    steps = [(a, n) for n in range(blocks) for a in each]
    lanes = [head_lanes(h) for h in heads]
    here = [head_lanes(p) for p in places]
    cums = [head_rows(cum_ref, h) for h in heads]
    mids = [middle_lane(c) for c in cums]
    ends = [last_lane(c) for c in cums]
    query_scale = [jnp.exp(spread(c - m, picks)) for c, m in zip(cums, mids)]
    mid_scale, end_scale = [jnp.exp(m) for m in mids], [jnp.exp(e) for e in ends]
    rest_scale = [jnp.exp(e - m) for e, m in zip(ends, mids)]
    enter_scale = [jnp.exp(m + head_rows(before_ref, h)) for m, h in zip(mids, heads)]
    entering = [enter_ref[h].astype(F32) for h in heads]

    def at(ref, a, n):
        return ref[span(n), lanes[a]]

    ga_up, v_turned, states, scores, updates, weights, lows, lows_turned, grad_q, grad_k, grad_v = ({} for _ in range(11))
    back = {a: jnp.zeros((DH, DH), F32) for a in each}

    def scale(a, n):
        ga_up[a, n] = (at(ga_ref, a, n).astype(F32) * query_scale[a][:, span(n)]).astype(BF16)
        v_turned[a, n] = at(vs_ref, a, n).T
        state = low_ref[heads[a], n].astype(F32) + enter_scale[a][n : n + 1] * entering[a]
        states[a, n] = state.astype(BF16).T

    def multiply(a, n):
        scores[a, n] = nn(ga_up[a, n], v_turned[a, n])
        if n > 0:
            updates[a, n] = nn(turned_ref[heads[a], :, span(n)], at(ga_ref, a, n))

    def mask_out(a, n):
        scores[a, n] = jnp.where(mask, scores[a, n], 0.0).astype(BF16)
        weights[a, n] = scores[a, n].T
        if n < blocks - 1:
            lows[a, n] = (rest_scale[a][n : n + 1] * back[a]).astype(BF16)
            lows_turned[a, n] = lows[a, n].T
        if n > 0:
            back[a] = end_scale[a][n : n + 1] * back[a] + mid_scale[a][n : n + 1] * updates[a, n]

    def combine(a, n):
        left = jnp.concatenate([scores[a, n], ga_up[a, n]], axis=1)
        grad_q[a, n] = nn(left, jnp.concatenate([at(k_ref, a, n), states[a, n]], axis=0))
        left_k, right_k = weights[a, n], at(q_ref, a, n)
        left_v, right_v = weights_ref[heads[a], n], at(ga_ref, a, n)
        if n < blocks - 1:
            left_k = jnp.concatenate([left_k, at(vs_ref, a, n)], axis=1)
            right_k = jnp.concatenate([right_k, lows_turned[a, n]], axis=0)
            left_v = jnp.concatenate([left_v, at(ks_ref, a, n)], axis=1)
            right_v = jnp.concatenate([right_v, lows[a, n]], axis=0)
        grad_k[a, n] = nn(left_k, right_k)
        grad_v[a, n] = nn(left_v, right_v)

    def store(a, n):
        gq_ref[span(n), here[a]] = grad_q[a, n].astype(BF16)
        lv_ref[span(n), lanes[a]] = grad_v[a, n].astype(BF16)
        lk_ref[span(n), lanes[a]] = grad_k[a, n].astype(BF16)
        normed = at(attn_ref, a, n).astype(F32) * inverse_ref[span(n), :]
        out_ref[span(n), here[a]] = (normed * gain_ref[:, lanes[a]]).astype(BF16)

    staggered([scale, multiply, mask_out, combine, store], steps[::-1])


def grads_body(first, count, chained, *refs):
    inputs = refs[1:15]
    refs = refs[15 + (4 if chained else 0) :]
    out_hbm, gq_hbm, lk_ref, lv_ref, out_ref, gq_ref, sems = refs
    both_masks = masks()
    picks = block_picks(inputs[0].shape[0] // SPAN)

    def copies(at):
        here, there = head_lanes(at * PAIR, PAIR), head_lanes(first + at * PAIR, PAIR)
        return [
            pltpu.make_async_copy(out_ref.at[:, here], out_hbm.at[:, there], sems.at[0, at]),
            pltpu.make_async_copy(gq_ref.at[:, here], gq_hbm.at[:, there], sems.at[1, at]),
        ]

    @pl.loop(0, count // PAIR)
    def _(at):
        places = [at * PAIR + a for a in range(PAIR)]
        heads = [first + p for p in places]
        grads_heads(heads, places, inputs, out_ref, gq_ref, lk_ref, lv_ref, both_masks, picks)
        for copy in copies(at):
            copy.start()

    @pl.loop(0, count // PAIR)
    def _(at):
        for copy in copies(at):
            copy.wait()


def grads_local(after, first, count, inputs, done):
    rows, width = inputs[0].shape
    like = jax.ShapeDtypeStruct((rows, width), BF16)
    kinds = [HBM, HBM, VMEM, VMEM]
    return pl.pallas_call(
        functools.partial(grads_body, first, count, bool(done)),
        in_specs=[ANY] + [VMEM] * 14 + (kinds if done else []),
        out_specs=kinds,
        out_shape=[like] * 4,
        input_output_aliases={15 + i: i for i in range(4)} if done else {},
        scratch_shapes=[
            pltpu.VMEM((rows, count * DH), BF16),
            pltpu.VMEM((rows, count * DH), BF16),
            pltpu.SemaphoreType.DMA((2, count // PAIR)),
        ],
        compiler_params=params(8),
        cost_estimate=cost(22 * rows * count * DH * DH, 24 * rows * count * DH),
        name=f"grads_{first}",
    )(after, *inputs, *done)


def leave_body(of_other, k_ref, v_ref, lk_ref, lv_ref, state_ref, cum_ref, before_ref, total_ref, *refs):
    core, _, _ = position()
    rows, width = k_ref.shape
    heads, blocks = width // DH, rows // SPAN
    half = heads // 2
    copies = []
    if of_other:
        kept_k_ref, kept_v_ref, kept_gain_ref, gk_hbm, gv_hbm, gg_ref, gk_ref, gv_ref, sems, kept_sems = refs
        there = head_lanes(half_heads(core, False, 0, heads), half)
        for which, (source, target) in enumerate(((kept_k_ref, gk_hbm), (kept_v_ref, gv_hbm))):
            copies.append(pltpu.make_async_copy(source, target.at[:, there], kept_sems.at[which]))
            copies[-1].start()
        gg_ref[...] = kept_gain_ref[...]
    else:
        gk_ref, gv_ref, gg_ref = refs
    for g in range(half // GROUP):

        for at in range(g * GROUP // PAIR, (g + 1) * GROUP // PAIR):
            first = half_heads(core, of_other, at * PAIR, heads)
            lanes = [head_lanes(first + a) for a in range(PAIR)]
            here = [head_lanes(at * PAIR + a) for a in range(PAIR)]
            lows = [piece_state(state_ref, at * PAIR + a).astype(BF16) for a in range(PAIR)]
            from_v = [nt(v_ref[:, lanes[a]], lows[a]) for a in range(PAIR)]
            from_k = [nn(k_ref[:, lanes[a]], lows[a]) for a in range(PAIR)]
            scales = [
                jnp.exp(
                    head_rows(total_ref, first + a)
                    - head_rows(before_ref, first + a)
                    - middle_lane(head_rows(cum_ref, first + a))
                )
                for a in range(PAIR)
            ]
            for n in range(blocks):
                for a in range(PAIR):
                    factor = scales[a][n : n + 1]
                    grad_k = lk_ref[span(n), lanes[a]].astype(F32) + factor * from_v[a][span(n)]
                    grad_v = lv_ref[span(n), lanes[a]].astype(F32) + factor * from_k[a][span(n)]
                    gk_ref[span(n), here[a]] = grad_k.astype(BF16)
                    gv_ref[span(n), here[a]] = grad_v.astype(BF16)
            for a in range(PAIR):
                row = STATES + 4 * (a % 2) + 1
                gg_ref[:, lanes[a]] = state_ref[at * PAIR // 2 + a // 2, row : row + 1, :]

        if of_other:
            here = slice(g * GROUP * DH, (g + 1) * GROUP * DH)
            there = head_lanes(half_heads(core, True, g * GROUP, heads), GROUP)
            for which, (source, target) in enumerate(((gk_ref, gk_hbm), (gv_ref, gv_hbm))):
                copies.append(pltpu.make_async_copy(source.at[:, here], target.at[:, there], sems.at[which, g]))
                copies[-1].start()
    for copy in copies:
        copy.wait()


def grads_leaving(of_other, keys, values, local_k, local_v, state, cum, before, total, done):
    rows, width = keys.shape
    heads = width // DH
    like = jax.ShapeDtypeStruct((rows, width if of_other else width // 2), BF16)
    kept = pltpu.VMEM((rows, width // 2), BF16)
    sems = [pltpu.SemaphoreType.DMA((2, heads // 2 // GROUP)), pltpu.SemaphoreType.DMA((2,))]
    return pl.pallas_call(
        functools.partial(leave_body, of_other),
        in_specs=[VMEM] * (8 + len(done)),
        out_specs=[HBM, HBM, VMEM] if of_other else [VMEM] * 3,
        out_shape=[like, like, jax.ShapeDtypeStruct((1, width), F32)],
        scratch_shapes=[kept, kept] + sems if of_other else [],
        compiler_params=params(6),
        cost_estimate=cost(2 * rows * width * DH, 6 * rows * width),
        name="leave_taken" if of_other else "leave_kept",
    )(keys, values, local_k, local_v, state, cum, before, total, *done)


def per_device(queries, keys, values, log_decay, gain, grad_out):
    gain_row = gain.reshape(1, -1)
    keys, values, queries, grad_out, log_decay = (
        pltpu.with_memory_space_constraint(a, pltpu.HBM) for a in (keys, values, queries, grad_out, log_decay)
    )
    send, keys, values, cum, before, total = local_state(True, keys, values, (log_decay,))
    (own,) = local_state(False, keys, values, (cum, before, total))

    def attend_part(first, count, load):
        def run(after, done):
            held = done[7] if done else queries
            outs = attend(after, first, count, load, keys, values, cum, held, grad_out, done[:7])
            if load == "queries":
                return (*outs[:7], outs[7], outs[0])
            if load == "grad_out":
                return (*outs[:7], held, outs[7], outs[0])
            return (*outs[:7], held, done[8], outs[0])

        return run

    keep, taken, (local, lows, turned, q_up, k_up, v_up, weights, queries, grad_out, _) = scan_over_seq(
        send, own, False, [attend_part(0, 6, "queries"), attend_part(6, 6, "grad_out"), attend_part(12, 4, None)]
    )
    table = (cum, before)
    done = attend_entering(False, q_up, local, grad_out, gain_row, keep, *table, ())
    attn, entering, stats = attend_entering(True, q_up, local, grad_out, gain_row, taken, *table, done)[:3]
    count = lax.axis_size("head")
    stats = [stats] + [
        lax.ppermute(stats, "head", [(i, (i + s) % count) for i in range(count)]) for s in arrival_order(count)[1:]
    ]
    shared = (turned, attn, grad_out, gain_row, cum, before, total)
    grad_attn, send, inverse, factor = norm_backward(True, *shared, stats)
    grad_attn, own = norm_backward(False, *shared, (inverse, factor, grad_attn))
    inputs = (queries, keys, turned, k_up, v_up, weights, grad_attn, attn, gain_row, inverse, lows, entering, cum, before)

    def grads_part(first, count):
        return lambda after, done: grads_local(after, first, count, inputs, done)

    keep, taken, (output, grad_q, local_k, local_v) = scan_over_seq(
        send, own, True, [grads_part(0, 6), grads_part(6, 6), grads_part(12, 4)]
    )
    shared = (k_up, v_up, local_k, local_v)
    done = grads_leaving(False, *shared, keep, cum, before, total, ())
    grad_k, grad_v, grad_gain = grads_leaving(True, *shared, taken, cum, before, total, done)
    return output, grad_q, grad_k, grad_v, grad_gain.reshape(-1)


def solution(mesh):
    tokens, heads = P("seq", "head"), P("head")
    return jax.shard_map(
        per_device,
        mesh=mesh,
        in_specs=(tokens, tokens, tokens, P("head", "seq"), heads, tokens),
        out_specs=(tokens, tokens, tokens, tokens, heads),
        check_vma=False,
    )
```

```python
import functools

import jax
import jax.numpy as jnp
from jax import lax
from jax.experimental import pallas as pl
from jax.experimental.pallas import tpu as pltpu
from jax.sharding import PartitionSpec as P

HEAD_TOTAL = 64
DH = 128
SPAN = 128
ROWS = 8
STATES = 2 * DH
PIECE = STATES + ROWS
GROUP = 4
PAIR = 2
ALONG_X, ALONG_Z = 4, 4
F32 = jnp.float32
BF16 = jnp.bfloat16
EXACT = lax.Precision.HIGHEST
VMEM = pl.BlockSpec(memory_space=pltpu.VMEM)
HBM = pl.BlockSpec(memory_space=pltpu.HBM)
ANY = pl.BlockSpec(memory_space=pl.ANY)


def dot(a, b, contract, precision=None):
    return lax.dot_general(
        a, b, ((contract[:1], contract[1:]), ((), ())), precision=precision, preferred_element_type=F32
    )


def nn(a, b):
    return dot(a, b, (1, 0))


def nt(a, b):
    return dot(a, b, (1, 1))


def params(mib):
    return pltpu.CompilerParams(vmem_limit_bytes=mib * 1024 * 1024)


def cost(flops, nbytes):
    return pl.CostEstimate(flops=int(flops), bytes_accessed=int(nbytes), transcendentals=0)


def side_by_side(count):
    return 3 if count % 3 == 0 else PAIR


def head_rows(ref, head):
    return ref[pl.ds(pl.multiple_of(head * ROWS, ROWS), ROWS), :]


def head_lanes(head, count=1):
    return pl.ds(pl.multiple_of(head * DH, DH), count * DH)


def span(n):
    return slice(n * SPAN, (n + 1) * SPAN)


def last_lane(rows):
    return jnp.broadcast_to(rows[:, SPAN - 1 :], rows.shape)


def middle_lane(rows):
    return jnp.broadcast_to(rows[:, SPAN // 2 - 1 : SPAN // 2], rows.shape)


def masks():
    i = lax.broadcasted_iota(jnp.int32, (SPAN, SPAN), 0)
    j = lax.broadcasted_iota(jnp.int32, (SPAN, SPAN), 1)
    return i >= j, i <= j


def join_rows(rows, blocks):
    return jnp.concatenate([rows[n : n + 1] for n in range(blocks)], axis=1)


def piece_store(ref, at, state, extra):
    pair, which = divmod(at, 2)
    ref[pair, which * DH : (which + 1) * DH, :] = state
    ref[pair, STATES + 4 * which : STATES + 4 * which + 4, :] = extra[:4]


def piece_state(ref, at):
    pair, which = divmod(at, 2)
    return ref[pair, which * DH : (which + 1) * DH, :]


def each_state(piece):
    return [(slice(w * DH, (w + 1) * DH), slice(STATES + 4 * w, STATES + 4 * w + 1)) for w in range(2)]


def extra_rows(decay, gain_row=None):
    place = lax.broadcasted_iota(jnp.int32, (ROWS, DH), 0)
    rest = 0.0 if gain_row is None else jnp.where(place == 1, gain_row, 0.0)
    return jnp.where(place == 0, decay, rest)


def position():
    place = lax.axis_index("seq")
    return lax.rem(place, 2), lax.rem(place // 2, ALONG_Z), place // (2 * ALONG_Z)


def half_heads(core, of_other, at, heads):
    half = heads // 2
    start = (1 - core) if of_other else core
    return start * half + at


def decay_tables(log_ref, cum_ref, before_ref, total_ref):
    heads, rows = log_ref.shape
    _, triangle = masks()
    triangle = triangle.astype(F32)
    cum_ref[...] = jnp.zeros_like(cum_ref)
    before_ref[...] = jnp.zeros_like(before_ref)
    before = jnp.zeros((heads, SPAN), F32)
    for n in range(rows // SPAN):
        cum = dot(log_ref[:, span(n)], triangle, (1, 0), EXACT)
        for h in range(heads):
            cum_ref[h * ROWS + n : h * ROWS + n + 1, :] = cum[h : h + 1]
            before_ref[h * ROWS + n : h * ROWS + n + 1, :] = before[h : h + 1]
        before = before + last_lane(cum)
    for h in range(heads):
        total_ref[h * ROWS : (h + 1) * ROWS, :] = jnp.broadcast_to(before[h : h + 1], (ROWS, SPAN))


def state_body(of_other, *refs):
    core, _, _ = position()
    if of_other:
        k_hbm, v_hbm, log_hbm, out_ref, k_ref, v_ref, cum_ref, before_ref, total_ref, sems, log_ref, log_sem = refs
    else:
        k_ref, v_ref, cum_ref, before_ref, total_ref, out_ref = refs
    rows, width = k_ref.shape
    heads, blocks = width // DH, rows // SPAN
    copies = []
    if of_other:
        log_copy = pltpu.make_async_copy(log_hbm, log_ref, log_sem)
        log_copy.start()
        for g in range(heads // GROUP):
            lanes = head_lanes(lax.rem(half_heads(core, True, g * GROUP, heads), heads), GROUP)
            for which, (source, target) in enumerate(((k_hbm, k_ref), (v_hbm, v_ref))):
                copies.append(pltpu.make_async_copy(source.at[:, lanes], target.at[:, lanes], sems.at[which, g]))
                copies[-1].start()
        log_copy.wait()
        decay_tables(log_ref, cum_ref, before_ref, total_ref)

    for g in range(heads // 2 // GROUP):
        first = half_heads(core, of_other, g * GROUP, heads)
        if of_other:
            copies[2 * g].wait()
            copies[2 * g + 1].wait()
        totals = [head_rows(total_ref, first + at) for at in range(GROUP)]
        scales = [
            jnp.exp(totals[at] - head_rows(before_ref, first + at) - head_rows(cum_ref, first + at)) for at in range(GROUP)
        ]
        decayed = [
            (k_ref[:, head_lanes(first + at)].T.astype(F32) * join_rows(scales[at], blocks)).astype(BF16)
            for at in range(GROUP)
        ]
        states = [nn(decayed[at], v_ref[:, head_lanes(first + at)]) for at in range(GROUP)]
        for at in range(GROUP):
            piece_store(out_ref, g * GROUP + at, states[at], extra_rows(jnp.exp(totals[at])))
    for copy in copies[heads // GROUP :]:
        copy.wait()


def local_state(of_other, keys, values, more):
    rows, width = keys.shape
    heads = width // DH
    pieces = jax.ShapeDtypeStruct((heads // 4, PIECE, DH), F32)
    table = jax.ShapeDtypeStruct((heads * ROWS, SPAN), F32)
    like = jax.ShapeDtypeStruct(keys.shape, BF16)
    if of_other:
        specs, outs = [HBM] * 3, [pieces, like, like, table, table, table]
        scratch = [
            pltpu.SemaphoreType.DMA((2, heads // GROUP)),
            pltpu.VMEM(more[0].shape, F32),
            pltpu.SemaphoreType.DMA,
        ]
    else:
        specs, outs, scratch = [VMEM] * 5, [pieces], []
    return pl.pallas_call(
        functools.partial(state_body, of_other),
        in_specs=specs,
        out_specs=[VMEM] * len(outs),
        out_shape=outs,
        scratch_shapes=scratch,
        compiler_params=params(4),
        cost_estimate=cost(heads * rows * DH * DH, 2 * rows * heads * DH),
        name="state_given" if of_other else "state_kept",
    )(keys, values, *more)


def arrival_order(count):
    return [0] + sorted(range(1, count), key=lambda s: -min(s, count - s))


def join_extra(a, b):
    decays = lax.broadcasted_iota(jnp.int32, (ROWS, DH), 0) % 4 == 0
    return jnp.where(decays, a * b, a + b)


def cores_body(reverse, own_ref, got_ref, *out_refs):
    core, z, _ = position()
    near_here = (core == 0) != reverse
    for shift, out_ref in enumerate(out_refs):
        pair = lax.rem(z + shift, ALONG_Z)
        own, got = own_ref[pair], got_ref[pair]
        near, far = jnp.where(near_here, own, got), jnp.where(near_here, got, own)
        for rows, decay in each_state(near):
            out_ref[rows, :] = far[decay] * near[rows] + far[rows]
        out_ref[STATES:, :] = join_extra(near[STATES:], far[STATES:])


def along_z_body(reverse, *refs):
    in_refs, (_, total_ref, prefix_ref, slots) = refs[:ALONG_Z], refs[ALONG_Z:]
    _, z, _ = position()
    for shift, ref in zip(arrival_order(len(in_refs)), in_refs):
        slots[lax.rem(z - shift + ALONG_Z, ALONG_Z)] = ref[...]
    laps = [ALONG_Z - 1 - lap if reverse else lap for lap in range(ALONG_Z)]
    for rows, decay in each_state(total_ref):
        state = jnp.zeros((DH, DH), F32)
        for at in laps:
            prefix_ref[at, rows, :] = state
            state = slots[at, decay, :] * state + slots[at, rows, :]
        total_ref[rows, :] = state
    extra = jnp.where(lax.broadcasted_iota(jnp.int32, (ROWS, DH), 0) % 4 == 0, 1.0, 0.0)
    for at in laps:
        prefix_ref[at, STATES:, :] = extra
        extra = join_extra(extra, slots[at, STATES:, :])
    total_ref[STATES:, :] = extra


def along_x_body(reverse, *refs):
    in_refs, prefix_ref, out_refs, slots = refs[:ALONG_X], refs[ALONG_X], refs[ALONG_X + 2 : -1], refs[-1]
    _, z, x = position()
    for shift, ref in zip(arrival_order(len(in_refs)), in_refs):
        slots[lax.rem(x - shift + ALONG_X, ALONG_X)] = ref[...]
    for rows, decay in each_state(prefix_ref):
        state = jnp.zeros((DH, DH), F32)
        for lap in range(ALONG_X):
            at = ALONG_X - 1 - lap if reverse else lap
            taken = (at > x) if reverse else (at < x)
            state = jnp.where(taken, slots[at, decay, :] * state + slots[at, rows, :], state)
        for shift, out_ref in enumerate(out_refs):
            at = lax.rem(z + shift, ALONG_Z)
            out_ref[rows, :] = prefix_ref[at, rows, :] + prefix_ref[at, decay, :] * state
    if reverse:
        extra = sum(slots[at, STATES:, :] for at in range(ALONG_X))
        for out_ref in out_refs:
            out_ref[STATES:, :] = extra


def entering_body(reverse, *refs):
    in_refs, (own_ref, got_ref, _, keep_ref, give_ref) = refs[:ALONG_Z], refs[ALONG_Z:]
    core, z, _ = position()
    near_here = (core == 0) != reverse
    for shift, ref in zip(arrival_order(len(in_refs)), in_refs):
        pair = lax.rem(z - shift + ALONG_Z, ALONG_Z)
        near = jnp.where(near_here, own_ref[pair], got_ref[pair])
        for rows, decay in each_state(near):
            entering = ref[rows, :]
            passed = near[decay] * entering + near[rows]
            keep_ref[pair, rows, :] = jnp.where(near_here, entering, passed)
            give_ref[pair, rows, :] = jnp.where(near_here, passed, entering)
        if reverse:
            keep_ref[pair, STATES:, :] = ref[STATES:, :]
            give_ref[pair, STATES:, :] = ref[STATES:, :]


def scan_step(body, name, reverse, arrays, after, out_counts, scratch):
    shapes = [jax.ShapeDtypeStruct(shape, F32) for shape in out_counts]
    afters = [] if after is None else [after]
    return pl.pallas_call(
        functools.partial(body, reverse),
        in_specs=[VMEM] * len(arrays) + [ANY] * len(afters),
        out_specs=[VMEM] * len(shapes),
        out_shape=shapes,
        scratch_shapes=scratch,
        compiler_params=params(3),
        cost_estimate=cost(10**6, 10**6),
        name=name,
    )(*arrays, *afters)


def scan_over_seq(send, own, reverse, works):
    count = lax.axis_size("seq")

    def index(x, z, c):
        return (x % ALONG_X * ALONG_Z + z % ALONG_Z) * 2 + c

    every = [(x, z, c) for x in range(ALONG_X) for z in range(ALONG_Z) for c in range(2)]
    across = [(i, i ^ 1) for i in range(count)]
    by_z = [[(index(x, z, c), index(x, z + s, c)) for x, z, c in every] for s in range(ALONG_Z)]
    by_x = [[(index(x, z, c), index(x + s, z, c)) for x, z, c in every] for s in range(ALONG_X)]
    piece = (PIECE, DH)
    back = (PIECE if reverse else STATES, DH)

    def shifted(arrays, moves):
        return [lax.ppermute(arrays[s], "seq", moves[s]) if s else arrays[0] for s in arrival_order(len(moves))]

    got = lax.ppermute(send, "seq", across)
    parts = scan_step(cores_body, "join_cores", reverse, [own, got], None, [piece] * ALONG_Z, [])
    arrived = shifted(parts, by_z)
    done = works[0](parts[0], ())
    total, prefix = scan_step(
        along_z_body, "join_z", reverse, arrived, done[-1],
        [piece, (ALONG_Z,) + piece], [pltpu.VMEM((ALONG_Z,) + piece, F32)],
    )
    totals = shifted([total] * ALONG_X, by_x)
    done = works[1](total, done)
    parts = scan_step(
        along_x_body, "join_x", reverse, totals + [prefix], done[-1],
        [back] * ALONG_Z, [pltpu.VMEM((ALONG_X,) + piece, F32)],
    )
    arrived = shifted(parts, by_z)
    done = works[2](parts[0], done)
    keep, give = scan_step(
        entering_body, "entering", reverse, arrived + [own, got], done[-1], [own.shape[:1] + back] * 2, []
    )
    return keep, lax.ppermute(give, "seq", across), done


def block_picks(blocks):
    part = lax.broadcasted_iota(jnp.int32, (4 * ROWS, blocks * SPAN), 0)
    place = lax.broadcasted_iota(jnp.int32, (4 * ROWS, blocks * SPAN), 1)
    return (lax.rem(part, ROWS) == place // SPAN).astype(BF16)


def spread(rows, picks):
    high = rows.astype(BF16).astype(F32)
    middle = (rows - high).astype(BF16).astype(F32)
    parts = jnp.concatenate([high, middle, rows - high - middle, jnp.zeros_like(rows)], axis=0)
    return nn(parts.T.astype(BF16), picks)


def staggered(stages, steps):
    for at in range(len(steps) + len(stages) - 1):
        for back, stage in enumerate(stages):
            if 0 <= at - back < len(steps):
                stage(*steps[at - back])


def attend_heads(heads, q_ref, k_ref, v_ref, cum_ref, outs, both_masks, picks):
    local_ref, low_ref, turned_ref, qs_ref, ks_ref, vs_ref, weights_ref = outs
    mask, turned_mask = both_masks
    blocks = k_ref.shape[0] // SPAN
    each = range(len(heads))
    steps = [(a, n) for n in range(blocks) for a in each]
    lanes = [head_lanes(h) for h in heads]
    cums = [head_rows(cum_ref, h) for h in heads]
    mids = [middle_lane(c) for c in cums]
    ends = [last_lane(c) for c in cums]
    shifts = [spread(c - m, picks) for c, m in zip(cums, mids)]
    mid_scale, end_scale = [jnp.exp(m) for m in mids], [jnp.exp(e) for e in ends]
    rest_scale = [jnp.exp(e - m) for e, m in zip(ends, mids)]
    q_up, k_up, q_turned, k_turned, scores, turned_weights, updates, weights, lows, totals = ({} for _ in range(10))
    state = {a: jnp.zeros((DH, DH), F32) for a in each}

    def scale(a, n):
        shift = shifts[a][:, span(n)]
        up, down = jnp.exp(shift), jnp.exp(-shift)
        q_up[a, n] = (q_ref[span(n), lanes[a]].astype(F32) * up).astype(BF16)
        k_up[a, n] = (k_ref[span(n), lanes[a]].astype(F32) * down).astype(BF16)
        vs_ref[span(n), lanes[a]] = (v_ref[span(n), lanes[a]].astype(F32) * down).astype(BF16)
        qs_ref[span(n), lanes[a]] = q_up[a, n]
        ks_ref[span(n), lanes[a]] = k_up[a, n]

    def turn(a, n):
        k_turned[a, n] = k_up[a, n].T
        q_turned[a, n] = q_up[a, n].T
        turned_ref[heads[a], :, span(n)] = q_turned[a, n]

    def multiply(a, n):
        scores[a, n] = nn(q_up[a, n], k_turned[a, n])
        turned_weights[a, n] = nn(k_up[a, n], q_turned[a, n])
        if n < blocks - 1:
            updates[a, n] = nn(k_turned[a, n], v_ref[span(n), lanes[a]])

    def mask_out(a, n):
        weights[a, n] = jnp.where(mask, scores[a, n], 0.0).astype(BF16)
        weights_ref[heads[a], n] = jnp.where(turned_mask, turned_weights[a, n], 0.0).astype(BF16)
        lows[a, n] = (mid_scale[a][n : n + 1] * state[a]).astype(BF16)
        low_ref[heads[a], n] = lows[a, n]
        if n < blocks - 1:
            state[a] = end_scale[a][n : n + 1] * state[a] + rest_scale[a][n : n + 1] * updates[a, n]

    def combine(a, n):
        v = v_ref[span(n), lanes[a]]
        if n == 0:
            totals[a, n] = nn(weights[a, n], v)
        else:
            left = jnp.concatenate([weights[a, n], q_up[a, n]], axis=1)
            totals[a, n] = nn(left, jnp.concatenate([v, lows[a, n]], axis=0))

    def store(a, n):
        local_ref[span(n), lanes[a]] = totals[a, n].astype(BF16)

    staggered([scale, turn, multiply, mask_out, combine, store], steps)


def attend_body(first, count, load, *refs):
    k_ref, v_ref, cum_ref = refs[1:4]
    refs = refs[4:]
    copies = []
    if load == "queries":
        q_hbm, outs, (q_ref, sems) = refs[0], refs[1:8], refs[8:]
        for g in range(q_hbm.shape[1] // (GROUP * DH)):
            lanes = slice(g * GROUP * DH, (g + 1) * GROUP * DH)
            copies.append(pltpu.make_async_copy(q_hbm.at[:, lanes], q_ref.at[:, lanes], sems.at[g]))
    elif load == "grad_out":
        q_ref, go_hbm, outs, (go_ref, sems) = refs[0], refs[1], refs[9:16], refs[16:]
        copies.append(pltpu.make_async_copy(go_hbm, go_ref, sems.at[0]))
    else:
        q_ref, outs = refs[0], refs[8:15]
    for copy in copies:
        copy.start()
    both_masks = masks()
    picks = block_picks(k_ref.shape[0] // SPAN)
    held = []
    for at, copy in enumerate(copies):
        if load == "queries" and at * GROUP < first + count:
            copy.wait()
        else:
            held.append(copy)

    size = side_by_side(count)

    @pl.loop(0, count // size)
    def _(at):
        heads = [first + at * size + a for a in range(size)]
        attend_heads(heads, q_ref, k_ref, v_ref, cum_ref, outs, both_masks, picks)

    for copy in held:
        copy.wait()


def attend(after, first, count, load, keys, values, cum, queries, grad_out, done):
    rows, width = keys.shape
    heads, blocks = width // DH, rows // SPAN
    like = jax.ShapeDtypeStruct((rows, width), BF16)
    squares = jax.ShapeDtypeStruct((heads, blocks, DH, DH), BF16)
    outs = [like, squares, jax.ShapeDtypeStruct((heads, DH, rows), BF16), like, like, like, squares]
    arrays, specs = [after, keys, values, cum, queries], [ANY, VMEM, VMEM, VMEM]
    specs.append(HBM if load == "queries" else VMEM)
    if load == "grad_out":
        arrays.append(grad_out)
        specs.append(HBM)
    aliases = {len(arrays) + i: i for i in range(len(done))}
    if load is not None:
        outs.append(like)
    return pl.pallas_call(
        functools.partial(attend_body, first, count, load),
        in_specs=specs + [VMEM] * len(done),
        out_specs=[VMEM] * len(outs),
        out_shape=outs,
        input_output_aliases=aliases,
        scratch_shapes=[] if load is None else [pltpu.SemaphoreType.DMA((heads // GROUP,))],
        compiler_params=params(6),
        cost_estimate=cost(10 * rows * count * DH * DH, 12 * rows * count * DH),
        name=f"attend_{first}",
    )(*arrays, *done)


def enter_body(of_other, q_ref, local_ref, go_ref, gain_ref, state_ref, cum_ref, before_ref, *refs):
    if of_other:
        attn_ref, low_ref, stats_ref, square_ref, inner_ref = refs[4:]
    else:
        attn_ref, low_ref, square_ref, inner_ref = refs
    core, _, _ = position()
    rows, width = q_ref.shape
    heads, blocks = width // DH, rows // SPAN
    if not of_other:
        square_ref[...] = jnp.zeros_like(square_ref)
        inner_ref[...] = jnp.zeros_like(inner_ref)

    for g in range(heads // 2 // GROUP):
        first = half_heads(core, of_other, g * GROUP, heads)
        lanes = [head_lanes(first + at) for at in range(GROUP)]
        carried, scales, gains = [], [], []
        for at in range(GROUP):
            low = piece_state(state_ref, g * GROUP + at).astype(BF16)
            low_ref[first + at] = low
            carried.append(nn(q_ref[:, lanes[at]], low))
            scales.append(jnp.exp(middle_lane(head_rows(cum_ref, first + at)) + head_rows(before_ref, first + at)))
            gains.append(gain_ref[:, lanes[at]])
        for n in range(blocks):
            square = square_ref[span(n), :]
            inner = inner_ref[span(n), :]
            for at in range(GROUP):
                entered = carried[at][span(n)] * scales[at][n : n + 1]
                attn = (local_ref[span(n), lanes[at]].astype(F32) + entered).astype(BF16)
                attn_ref[span(n), lanes[at]] = attn
                attn = attn.astype(F32)
                square += attn * attn
                inner += go_ref[span(n), lanes[at]].astype(F32) * gains[at] * attn
            square_ref[span(n), :] = square
            inner_ref[span(n), :] = inner

    if of_other:
        ones = jnp.ones((8, DH), F32)
        stats_ref[0:1, :] = dot(ones, square_ref[...], (1, 1), EXACT)[0:1]
        stats_ref[1:2, :] = dot(ones, inner_ref[...], (1, 1), EXACT)[0:1]


def attend_entering(of_other, queries, local, grad_out, gain, state, cum, before, done):
    rows, width = queries.shape
    heads = width // DH
    sums = jax.ShapeDtypeStruct((rows, DH), F32)
    outs = [jax.ShapeDtypeStruct((rows, width), BF16), jax.ShapeDtypeStruct((heads, DH, DH), BF16)]
    if of_other:
        outs, aliases = outs + [jax.ShapeDtypeStruct((2, rows), F32), sums, sums], {7: 0, 8: 1, 9: 3, 10: 4}
    else:
        outs, aliases = outs + [sums, sums], {}
    return pl.pallas_call(
        functools.partial(enter_body, of_other),
        in_specs=[VMEM] * (7 + len(done)),
        out_specs=[VMEM] * len(outs),
        out_shape=outs,
        input_output_aliases=aliases,
        compiler_params=params(4),
        cost_estimate=cost(rows * width * DH, 4 * rows * width),
        name="enter_taken" if of_other else "enter_kept",
    )(queries, local, grad_out, gain, state, cum, before, *done)


def columns(row, ref, blocks):
    for n in range(blocks):
        ref[span(n), :] = jnp.broadcast_to(row[:, span(n)], (SPAN, SPAN)).T


def norm_body(of_other, turned_ref, attn_ref, go_ref, gain_ref, cum_ref, before_ref, total_ref, *refs):
    core, _, _ = position()
    rows, width = attn_ref.shape
    heads, blocks = width // DH, rows // SPAN
    if of_other:
        stats_refs, (ga_ref, out_ref, inverse_ref, factor_ref) = refs[:-4], refs[-4:]
        stats = functools.reduce(jnp.add, [ref[...] for ref in stats_refs]) / (HEAD_TOTAL * DH)
        inverse = lax.rsqrt(stats[0:1] + 1e-06)
        columns(inverse, inverse_ref, blocks)
        columns(inverse * inverse * inverse * stats[1:2], factor_ref, blocks)
    else:
        inverse_ref, factor_ref, _, ga_ref, out_ref = refs

    for g in range(heads // 2 // GROUP):
        places = [g * GROUP + at for at in range(GROUP)]
        heads_now = [half_heads(core, of_other, place, heads) for place in places]
        lanes = [head_lanes(head) for head in heads_now]
        gains = [gain_ref[:, lane] for lane in lanes]
        gain_sums = [jnp.zeros((8, DH), F32) for _ in places]
        grads = [[] for _ in places]
        for n in range(blocks):
            for at in range(GROUP):
                attn = attn_ref[span(n), lanes[at]].astype(F32)
                scaled = go_ref[span(n), lanes[at]].astype(F32) * inverse_ref[span(n), :]
                gain_sums[at] += jnp.sum((scaled * attn).reshape(SPAN // 8, 8, DH), axis=0)
                grad = (scaled * gains[at] - attn * factor_ref[span(n), :]).astype(BF16)
                ga_ref[span(n), lanes[at]] = grad
                grads[at].append(grad)
        updates = [
            [nn(turned_ref[heads_now[at], :, span(n)], grads[at][n]) for n in range(blocks)] for at in range(GROUP)
        ]
        scales = [jnp.exp(middle_lane(head_rows(cum_ref, h)) + head_rows(before_ref, h)) for h in heads_now]
        states = [sum(scales[at][n : n + 1] * updates[at][n] for n in range(blocks)) for at in range(GROUP)]
        for at in range(GROUP):
            decay = jnp.exp(head_rows(total_ref, heads_now[at]))
            piece_store(out_ref, places[at], states[at], extra_rows(decay, jnp.sum(gain_sums[at], axis=0, keepdims=True)))


def norm_backward(of_other, turned, attn, grad_out, gain, cum, before, total, more):
    rows, width = attn.shape
    heads = width // DH
    pieces = jax.ShapeDtypeStruct((heads // 4, PIECE, DH), F32)
    cols = jax.ShapeDtypeStruct((rows, DH), F32)
    outs = [jax.ShapeDtypeStruct((rows, width), BF16), pieces] + ([cols, cols] if of_other else [])
    return pl.pallas_call(
        functools.partial(norm_body, of_other),
        in_specs=[VMEM] * (7 + len(more)),
        out_specs=[VMEM] * len(outs),
        out_shape=outs,
        input_output_aliases={} if of_other else {9: 0},
        compiler_params=params(5),
        cost_estimate=cost(rows * width * DH, 4 * rows * width),
        name="norm_given" if of_other else "norm_kept",
    )(turned, attn, grad_out, gain, cum, before, total, *more)


def grads_heads(heads, places, refs, out_ref, gq_ref, lk_ref, lv_ref, both_masks, picks):
    q_ref, k_ref, turned_ref, ks_ref, vs_ref, weights_ref, ga_ref, attn_ref = refs[:8]
    gain_ref, inverse_ref, low_ref, enter_ref, cum_ref, before_ref = refs[8:]
    mask, _ = both_masks
    blocks = k_ref.shape[0] // SPAN
    each = range(len(heads))
    steps = [(a, n) for n in range(blocks) for a in each]
    lanes = [head_lanes(h) for h in heads]
    here = [head_lanes(p) for p in places]
    cums = [head_rows(cum_ref, h) for h in heads]
    mids = [middle_lane(c) for c in cums]
    ends = [last_lane(c) for c in cums]
    query_scale = [jnp.exp(spread(c - m, picks)) for c, m in zip(cums, mids)]
    mid_scale, end_scale = [jnp.exp(m) for m in mids], [jnp.exp(e) for e in ends]
    rest_scale = [jnp.exp(e - m) for e, m in zip(ends, mids)]
    enter_scale = [jnp.exp(m + head_rows(before_ref, h)) for m, h in zip(mids, heads)]
    entering = [enter_ref[h].astype(F32) for h in heads]

    def at(ref, a, n):
        return ref[span(n), lanes[a]]

    ga_up, v_turned, states, scores, updates, weights, lows, lows_turned, grad_q, grad_k, grad_v = ({} for _ in range(11))
    back = {a: jnp.zeros((DH, DH), F32) for a in each}

    def scale(a, n):
        ga_up[a, n] = (at(ga_ref, a, n).astype(F32) * query_scale[a][:, span(n)]).astype(BF16)
        v_turned[a, n] = at(vs_ref, a, n).T
        state = low_ref[heads[a], n].astype(F32) + enter_scale[a][n : n + 1] * entering[a]
        states[a, n] = state.astype(BF16).T

    def multiply(a, n):
        scores[a, n] = nn(ga_up[a, n], v_turned[a, n])
        if n > 0:
            updates[a, n] = nn(turned_ref[heads[a], :, span(n)], at(ga_ref, a, n))

    def mask_out(a, n):
        scores[a, n] = jnp.where(mask, scores[a, n], 0.0).astype(BF16)
        weights[a, n] = scores[a, n].T
        if n < blocks - 1:
            lows[a, n] = (rest_scale[a][n : n + 1] * back[a]).astype(BF16)
            lows_turned[a, n] = lows[a, n].T
        if n > 0:
            back[a] = end_scale[a][n : n + 1] * back[a] + mid_scale[a][n : n + 1] * updates[a, n]

    def combine(a, n):
        left = jnp.concatenate([scores[a, n], ga_up[a, n]], axis=1)
        grad_q[a, n] = nn(left, jnp.concatenate([at(k_ref, a, n), states[a, n]], axis=0))
        left_k, right_k = weights[a, n], at(q_ref, a, n)
        left_v, right_v = weights_ref[heads[a], n], at(ga_ref, a, n)
        if n < blocks - 1:
            left_k = jnp.concatenate([left_k, at(vs_ref, a, n)], axis=1)
            right_k = jnp.concatenate([right_k, lows_turned[a, n]], axis=0)
            left_v = jnp.concatenate([left_v, at(ks_ref, a, n)], axis=1)
            right_v = jnp.concatenate([right_v, lows[a, n]], axis=0)
        grad_k[a, n] = nn(left_k, right_k)
        grad_v[a, n] = nn(left_v, right_v)

    def store(a, n):
        gq_ref[span(n), here[a]] = grad_q[a, n].astype(BF16)
        lv_ref[span(n), lanes[a]] = grad_v[a, n].astype(BF16)
        lk_ref[span(n), lanes[a]] = grad_k[a, n].astype(BF16)
        normed = at(attn_ref, a, n).astype(F32) * inverse_ref[span(n), :]
        out_ref[span(n), here[a]] = (normed * gain_ref[:, lanes[a]]).astype(BF16)

    staggered([scale, multiply, mask_out, combine, store], steps[::-1])


def grads_body(first, count, chained, *refs):
    inputs = refs[1:15]
    refs = refs[15 + (4 if chained else 0) :]
    out_hbm, gq_hbm, lk_ref, lv_ref, out_ref, gq_ref, sems = refs
    both_masks = masks()
    picks = block_picks(inputs[0].shape[0] // SPAN)

    size = side_by_side(count)

    def copies(at):
        here, there = head_lanes(at * size, size), head_lanes(first + at * size, size)
        return [
            pltpu.make_async_copy(out_ref.at[:, here], out_hbm.at[:, there], sems.at[0, at]),
            pltpu.make_async_copy(gq_ref.at[:, here], gq_hbm.at[:, there], sems.at[1, at]),
        ]

    @pl.loop(0, count // size)
    def _(at):
        places = [at * size + a for a in range(size)]
        heads = [first + p for p in places]
        grads_heads(heads, places, inputs, out_ref, gq_ref, lk_ref, lv_ref, both_masks, picks)
        for copy in copies(at):
            copy.start()

    @pl.loop(0, count // size)
    def _(at):
        for copy in copies(at):
            copy.wait()


def grads_local(after, first, count, inputs, done):
    rows, width = inputs[0].shape
    like = jax.ShapeDtypeStruct((rows, width), BF16)
    kinds = [HBM, HBM, VMEM, VMEM]
    return pl.pallas_call(
        functools.partial(grads_body, first, count, bool(done)),
        in_specs=[ANY] + [VMEM] * 14 + (kinds if done else []),
        out_specs=kinds,
        out_shape=[like] * 4,
        input_output_aliases={15 + i: i for i in range(4)} if done else {},
        scratch_shapes=[
            pltpu.VMEM((rows, count * DH), BF16),
            pltpu.VMEM((rows, count * DH), BF16),
            pltpu.SemaphoreType.DMA((2, count // side_by_side(count))),
        ],
        compiler_params=params(8),
        cost_estimate=cost(22 * rows * count * DH * DH, 24 * rows * count * DH),
        name=f"grads_{first}",
    )(after, *inputs, *done)


def leave_body(of_other, k_ref, v_ref, lk_ref, lv_ref, state_ref, cum_ref, before_ref, total_ref, *refs):
    core, _, _ = position()
    rows, width = k_ref.shape
    heads, blocks = width // DH, rows // SPAN
    half = heads // 2
    copies = []
    if of_other:
        kept_k_ref, kept_v_ref, kept_gain_ref, gk_hbm, gv_hbm, gg_ref, gk_ref, gv_ref, sems, kept_sems = refs
        there = head_lanes(half_heads(core, False, 0, heads), half)
        for which, (source, target) in enumerate(((kept_k_ref, gk_hbm), (kept_v_ref, gv_hbm))):
            copies.append(pltpu.make_async_copy(source, target.at[:, there], kept_sems.at[which]))
            copies[-1].start()
        gg_ref[...] = kept_gain_ref[...]
    else:
        gk_ref, gv_ref, gg_ref = refs
    for g in range(half // GROUP):

        for at in range(g * GROUP // PAIR, (g + 1) * GROUP // PAIR):
            first = half_heads(core, of_other, at * PAIR, heads)
            lanes = [head_lanes(first + a) for a in range(PAIR)]
            here = [head_lanes(at * PAIR + a) for a in range(PAIR)]
            lows = [piece_state(state_ref, at * PAIR + a).astype(BF16) for a in range(PAIR)]
            from_v = [nt(v_ref[:, lanes[a]], lows[a]) for a in range(PAIR)]
            from_k = [nn(k_ref[:, lanes[a]], lows[a]) for a in range(PAIR)]
            scales = [
                jnp.exp(
                    head_rows(total_ref, first + a)
                    - head_rows(before_ref, first + a)
                    - middle_lane(head_rows(cum_ref, first + a))
                )
                for a in range(PAIR)
            ]
            for n in range(blocks):
                for a in range(PAIR):
                    factor = scales[a][n : n + 1]
                    grad_k = lk_ref[span(n), lanes[a]].astype(F32) + factor * from_v[a][span(n)]
                    grad_v = lv_ref[span(n), lanes[a]].astype(F32) + factor * from_k[a][span(n)]
                    gk_ref[span(n), here[a]] = grad_k.astype(BF16)
                    gv_ref[span(n), here[a]] = grad_v.astype(BF16)
            for a in range(PAIR):
                row = STATES + 4 * (a % 2) + 1
                gg_ref[:, lanes[a]] = state_ref[at * PAIR // 2 + a // 2, row : row + 1, :]

        if of_other:
            here = slice(g * GROUP * DH, (g + 1) * GROUP * DH)
            there = head_lanes(half_heads(core, True, g * GROUP, heads), GROUP)
            for which, (source, target) in enumerate(((gk_ref, gk_hbm), (gv_ref, gv_hbm))):
                copies.append(pltpu.make_async_copy(source.at[:, here], target.at[:, there], sems.at[which, g]))
                copies[-1].start()
    for copy in copies:
        copy.wait()


def grads_leaving(of_other, keys, values, local_k, local_v, state, cum, before, total, done):
    rows, width = keys.shape
    heads = width // DH
    like = jax.ShapeDtypeStruct((rows, width if of_other else width // 2), BF16)
    kept = pltpu.VMEM((rows, width // 2), BF16)
    sems = [pltpu.SemaphoreType.DMA((2, heads // 2 // GROUP)), pltpu.SemaphoreType.DMA((2,))]
    return pl.pallas_call(
        functools.partial(leave_body, of_other),
        in_specs=[VMEM] * (8 + len(done)),
        out_specs=[HBM, HBM, VMEM] if of_other else [VMEM] * 3,
        out_shape=[like, like, jax.ShapeDtypeStruct((1, width), F32)],
        scratch_shapes=[kept, kept] + sems if of_other else [],
        compiler_params=params(6),
        cost_estimate=cost(2 * rows * width * DH, 6 * rows * width),
        name="leave_taken" if of_other else "leave_kept",
    )(keys, values, local_k, local_v, state, cum, before, total, *done)


def per_device(queries, keys, values, log_decay, gain, grad_out):
    gain_row = gain.reshape(1, -1)
    keys, values, queries, grad_out, log_decay = (
        pltpu.with_memory_space_constraint(a, pltpu.HBM) for a in (keys, values, queries, grad_out, log_decay)
    )
    send, keys, values, cum, before, total = local_state(True, keys, values, (log_decay,))
    (own,) = local_state(False, keys, values, (cum, before, total))

    def attend_part(first, count, load):
        def run(after, done):
            held = done[7] if done else queries
            outs = attend(after, first, count, load, keys, values, cum, held, grad_out, done[:7])
            if load == "queries":
                return (*outs[:7], outs[7], outs[0])
            if load == "grad_out":
                return (*outs[:7], held, outs[7], outs[0])
            return (*outs[:7], held, done[8], outs[0])

        return run

    keep, taken, (local, lows, turned, q_up, k_up, v_up, weights, queries, grad_out, _) = scan_over_seq(
        send, own, False, [attend_part(0, 6, "queries"), attend_part(6, 6, "grad_out"), attend_part(12, 4, None)]
    )
    table = (cum, before)
    done = attend_entering(False, q_up, local, grad_out, gain_row, keep, *table, ())
    attn, entering, stats = attend_entering(True, q_up, local, grad_out, gain_row, taken, *table, done)[:3]
    count = lax.axis_size("head")
    stats = [stats] + [
        lax.ppermute(stats, "head", [(i, (i + s) % count) for i in range(count)]) for s in arrival_order(count)[1:]
    ]
    shared = (turned, attn, grad_out, gain_row, cum, before, total)
    grad_attn, send, inverse, factor = norm_backward(True, *shared, stats)
    grad_attn, own = norm_backward(False, *shared, (inverse, factor, grad_attn))
    inputs = (queries, keys, turned, k_up, v_up, weights, grad_attn, attn, gain_row, inverse, lows, entering, cum, before)

    def grads_part(first, count):
        return lambda after, done: grads_local(after, first, count, inputs, done)

    keep, taken, (output, grad_q, local_k, local_v) = scan_over_seq(
        send, own, True, [grads_part(0, 6), grads_part(6, 6), grads_part(12, 4)]
    )
    shared = (k_up, v_up, local_k, local_v)
    done = grads_leaving(False, *shared, keep, cum, before, total, ())
    grad_k, grad_v, grad_gain = grads_leaving(True, *shared, taken, cum, before, total, done)
    return output, grad_q, grad_k, grad_v, grad_gain.reshape(-1)


def solution(mesh):
    tokens, heads = P("seq", "head"), P("head")
    return jax.shard_map(
        per_device,
        mesh=mesh,
        in_specs=(tokens, tokens, tokens, P("head", "seq"), heads, tokens),
        out_specs=(tokens, tokens, tokens, tokens, heads),
        check_vma=False,
    )
```
